32 devices in a mesh: space: 8 (over y, x, core), chan: 4 (over z).
Axes of the slice: x: 2, y: 2, z: 4, core: 2. Of those that a mesh axis runs over, the one named last changes fastest.
Arguments:
- volume: bfloat16 [128, 32, 16, 128], P('chan', 'space'), may hold values from -6 to 6
- kernel: bfloat16 [128, 3, 3, 3, 128], P('chan'), may hold values from -0.109375 to 0.109375
- upstream: bfloat16 [128, 8, 4, 32], P('chan', 'space'), may hold values from -24 to 24
Outputs:
- pooled: bfloat16 [128, 8, 4, 32], P('chan', 'space')
- volume_grad: bfloat16 [128, 32, 16, 128], P('chan', 'space')
- kernel_grad: float32 [128, 3, 3, 3, 128], P('chan')
The draws below stay inside these ranges and needn't reach their ends.
All inputs are finite; a program needn't handle non-finite values.
Results may differ from the reference program's by a relative error of at most 0.013.
Values may be sent and summed in bfloat16 or wider, within the bound.
No kernel may reach another device: no remote copies, remote signals or barrier semaphores. Data moves between devices by JAX's collectives and lax.ppermute only.
A program may use at most 64 MiB of HBM per device.

```python
import jax
import jax.numpy as jnp
from jax import lax

CIN = 128
COUT = 128
HGT = 16
WID = 128
DEPTH = 32


def block_levels(stream_key, shape, cuts, smallest, top_value):
    level, own = 1.0, jax.random.fold_in(stream_key, 6)
    for dim, blocks in cuts:
        heights = jnp.exp(jax.random.uniform(jax.random.fold_in(own, dim), (blocks,), jnp.float32, smallest / len(cuts), top_value / len(cuts)))
        level = level * jnp.repeat(heights, shape[dim] // blocks).reshape([-1 if axis == dim else 1 for axis in range(len(shape))])
    return level


def scatter_about(rng, extent, scale, limit, pieces=(), dtype=jnp.bfloat16):
    result = jax.random.normal(rng, extent, jnp.float32) * scale
    if len(pieces) > 0:
        result = block_levels(rng, extent, pieces, -0.22, 0.18) * result
    return jnp.clip(result, min=-limit, max=limit).astype(dtype)


def setup_inputs(seed: int = 0) -> dict:
    key_of = jax.random.split(jax.random.key(seed), 4)
    return {
        "volume": scatter_about(key_of[0], (CIN, DEPTH, HGT, WID), 1.0, 6.0, ((0, 4), (1, 8))),
        "kernel": scatter_about(key_of[1], (CIN, 3, 3, 3, COUT), (CIN * 27) ** -0.5, 0.109375, ((0, 4),)),
        "upstream": scatter_about(key_of[2], (COUT, DEPTH // 4, HGT // 4, WID // 4), 4.0, 24.0, ((0, 4), (1, 8))),
    }


slope_neg = 0.3


def reference(volume, kernel, upstream):
    vol_f = volume.astype(jnp.float32)
    ker_f = kernel.astype(jnp.float32)
    pre = lax.conv_general_dilated(vol_f[None], ker_f, (2, 2, 2), ((1, 1), (1, 1), (1, 1)), dimension_numbers=("NCDHW", "IDHWO", "NCDHW"), precision=lax.Precision.HIGHEST)[0]
    activated = jnp.where(pre > 0, pre, slope_neg * pre)
    chans, depth_out, rows_out, cols_out = pre.shape
    blocks = activated.reshape(chans, depth_out // 2, 2, rows_out // 2, 2, cols_out // 2, 2)
    pooled = jnp.mean(blocks, axis=(2, 4, 6)).astype(jnp.bfloat16)
    spread = upstream.astype(jnp.float32) * 0.125
    spread = jnp.broadcast_to(spread[:, :, None, :, None, :, None], blocks.shape).reshape(pre.shape)
    pre_grad = (spread * jnp.where(pre > 0, 1.0, slope_neg)).astype(jnp.bfloat16)
    grad_f = pre_grad.astype(jnp.float32)
    flipped = ker_f[:, ::-1, ::-1, ::-1, :]
    volume_grad = lax.conv_general_dilated(grad_f[None], flipped, (1, 1, 1), ((1, 2), (1, 2), (1, 2)), lhs_dilation=(2, 2, 2), dimension_numbers=("NCDHW", "ODHWI", "NCDHW"), precision=lax.Precision.HIGHEST)[0].astype(jnp.bfloat16)
    kernel_grad = lax.conv_general_dilated(vol_f[None], grad_f[None], (1, 1, 1), ((1, 0), (1, 0), (1, 0)), rhs_dilation=(2, 2, 2), dimension_numbers=("CNDHW", "IODHW", "NDHWC"), precision=lax.Precision.HIGHEST)
    return pooled, volume_grad, kernel_grad
```

```python
import functools

import jax
import jax.numpy as jnp
from jax import lax
from jax.experimental import pallas as pl
from jax.experimental.pallas import tpu as pltpu
from jax.sharding import PartitionSpec as P

SLOPE = 0.3
VMEM = 56 * 1024 * 1024
FEW = 4


def params():
    return pltpu.CompilerParams(vmem_limit_bytes=VMEM)


def pair_matrix(transposed, wid, half):
    shape = (3 * wid, 2 * wid) if transposed else (2 * wid, 3 * wid)
    long, short = (0, 1) if transposed else (1, 0)
    src = lax.broadcasted_iota(jnp.int32, shape, short)
    dst = lax.broadcasted_iota(jnp.int32, shape, long)
    e = (dst >= wid).astype(jnp.int32) + (dst >= 2 * wid).astype(jnp.int32)
    rest = dst - e * wid
    h = (rest >= half).astype(jnp.int32)
    x = 2 * (rest - h * half) + e - 1
    hit = (x >= 0) & (x < wid) & (src == h * wid + x)
    return jnp.where(hit, 1.0, 0.0).astype(jnp.bfloat16)


def fwd_kernel(n, ob, vol_ref, rim_ref, w_ref, cols_ref, *rest):
    part_refs = rest[:-2] if n > 1 else rest[:-1]
    wide_ref = rest[-2] if n > 1 else rest[-1]
    cb, planes, hgt, wid = vol_ref.shape
    half = wid // 2
    groups = hgt // 4
    lanes = groups * wid
    sel = pair_matrix(False, wid, half)
    zero = jnp.zeros((cb, wid), jnp.float32)
    for p in range(-1, planes):
        plane = rim_ref[:, 0] if p < 0 else vol_ref[:, p]
        wide_ref[...] = plane.astype(jnp.float32).reshape(cb * hgt, wid)
        row = [wide_ref[pl.ds(y, cb, stride=hgt), :] for y in range(hgt)]
        cls = [[row[4 * j + r] for j in range(groups)] for r in range(4)]

        def stack(blocks):
            return jnp.concatenate(blocks, axis=0).astype(jnp.bfloat16)

        back = stack([zero] + cls[3][:-1])
        cls = [stack(c) for c in cls]
        for b, (left, right) in enumerate(((back, cls[1]), (cls[0], cls[2]), (cls[1], cls[3]))):
            taps = jnp.dot(
                jnp.concatenate([left, right], axis=1), sel, preferred_element_type=jnp.float32
            )
            for e in range(3):
                block = taps[:, e * wid : (e + 1) * wid].astype(jnp.bfloat16)
                block = jnp.concatenate(
                    [block[j * cb : (j + 1) * cb] for j in range(groups)], axis=1
                )
                for z in range(planes // 2):
                    a = p + 1 - 2 * z
                    if 0 <= a <= 2:
                        tap = (a * 3 + b) * 3 + e
                        cols_ref[tap * cb : (tap + 1) * cb, z * lanes : (z + 1) * lanes] = block
    part = lax.dot_general(
        w_ref[...],
        cols_ref[...],
        (((0,), (0,)), ((), ())),
        preferred_element_type=jnp.float32,
    )
    if n == 1:
        part_refs[0][...] = part
        return
    all_ref = rest[-1]
    all_ref[...] = part
    me = lax.axis_index("chan")
    for k, ref in enumerate(part_refs):
        start = pl.multiple_of(lax.rem(me + k, n) * ob, ob)
        ref[...] = all_ref[pl.ds(start, ob), :]


def act_kernel(up_ref, *rest):
    *part_refs, pooled_ref, grad_ref = rest
    pre = part_refs[0][...]
    for ref in part_refs[1:]:
        pre = pre + ref[...]
    groups, ob, small = up_ref.shape
    wid = 4 * small
    lanes = groups * wid
    grow_r = lax.broadcasted_iota(jnp.int32, (small, wid), 0)
    grow_c = lax.broadcasted_iota(jnp.int32, (small, wid), 1)
    grow_c = grow_c - jnp.where(grow_c >= 2 * small, 2 * small, 0)
    grow = jnp.where((grow_c >= 2 * grow_r) & (grow_c <= 2 * grow_r + 1), 1.0, 0.0)
    pool_r = lax.broadcasted_iota(jnp.int32, (wid, small), 0)
    pool_c = lax.broadcasted_iota(jnp.int32, (wid, small), 1)
    pool_r = pool_r - jnp.where(pool_r >= 2 * small, 2 * small, 0)
    pool = jnp.where((pool_r >= 2 * pool_c) & (pool_r <= 2 * pool_c + 1), 0.125, 0.0)
    grow = grow.astype(jnp.bfloat16)
    scale = jnp.where(pre > 0, 1.0, SLOPE)
    act = jnp.where(pre > 0, pre, SLOPE * pre)
    act = act[:, :lanes] + act[:, lanes:]
    for j in range(groups):
        spread = jnp.dot(up_ref[j], grow, preferred_element_type=jnp.float32) * 0.125
        for z in range(2):
            at = slice(z * lanes + j * wid, z * lanes + (j + 1) * wid)
            grad_ref[:, at] = (spread * scale[:, at]).astype(jnp.bfloat16)
        pooled_ref[j] = jnp.dot(
            act[:, j * wid : (j + 1) * wid],
            pool,
            precision=lax.Precision.HIGHEST,
            preferred_element_type=jnp.float32,
        ).astype(jnp.bfloat16)


def weight_kernel(n, cols_ref, *rest):
    *block_refs, wgrad_ref, grad_ref = rest
    if n == 1:
        grad_ref[...] = block_refs[0][...]
    else:
        me = lax.axis_index("chan")
        ob = block_refs[0].shape[0]
        for k, ref in enumerate(block_refs):
            start = pl.multiple_of(lax.rem(me + n - k, n) * ob, ob)
            grad_ref[pl.ds(start, ob), :] = ref[...]
    wgrad_ref[...] = lax.dot_general(
        cols_ref[...],
        grad_ref[...],
        (((1,), (1,)), ((), ())),
        preferred_element_type=jnp.float32,
    )


def input_kernel(w_ref, grad_ref, rim_ref, out_ref, wide_ref):
    cb, planes, hgt, wid = out_ref.shape
    half = wid // 2
    groups = hgt // 4
    lanes = groups * wid
    taps = 9 * cb
    spread = pair_matrix(True, wid, half)
    spread = jnp.concatenate([spread, spread], axis=0)
    keep = lax.broadcasted_iota(jnp.int32, (3 * cb, lanes), 1) < lanes - half
    w = [w_ref[a * taps : (a + 1) * taps, :] for a in range(3)]
    behind = jnp.concatenate([w[2], w[0]], axis=1)
    g = [grad_ref[:, z * lanes : (z + 1) * lanes] for z in range(planes // 2)]
    g.append(rim_ref[...])
    for i in range(planes):
        z = i // 2
        if i % 2 == 0:
            e_all = jnp.dot(w[1], g[z], preferred_element_type=jnp.float32)
        else:
            e_all = jnp.dot(
                behind,
                jnp.concatenate([g[z], g[z + 1]], axis=0),
                preferred_element_type=jnp.float32,
            )
        by_b = [e_all[b * 3 * cb : (b + 1) * 3 * cb] for b in range(3)]
        shifted = pltpu.roll(by_b[0], lanes - half, 1)
        rows = (by_b[1], by_b[2] + jnp.where(keep, shifted, 0.0))
        left = []
        for f in rows:
            for j in range(groups):
                t = f[:, j * wid : (j + 1) * wid]
                left.append(
                    jnp.concatenate([t[e * cb : (e + 1) * cb] for e in range(3)], axis=1)
                )
        left = jnp.concatenate(left, axis=0)
        high = left.astype(jnp.bfloat16)
        low = (left - high.astype(jnp.float32)).astype(jnp.bfloat16)
        full = jnp.dot(
            jnp.concatenate([high, low], axis=1), spread, preferred_element_type=jnp.float32
        )
        for par in range(2):
            for j in range(groups):
                for h in range(2):
                    y = 2 * (2 * j + h) + par
                    at = (par * groups + j) * cb
                    wide_ref[pl.ds(i * hgt + y, cb, stride=planes * hgt), :] = full[
                        at : at + cb, h * wid : (h + 1) * wid
                    ]
    out_ref[...] = wide_ref[...].reshape(cb, planes, hgt, wid).astype(jnp.bfloat16)


def shifted_by(block, axis, k):
    n = lax.axis_size(axis)
    return lax.ppermute(block, axis, [(i, (i + k) % n) for i in range(n)])


def swapped(block, axis, bit):
    n = lax.axis_size(axis)
    return lax.ppermute(block, axis, [(i, i ^ bit) for i in range(n)])


def sum_over(term, axis):
    n = lax.axis_size(axis)
    if n & (n - 1):
        return lax.psum(term, axis)
    if n > 1:
        term = term + swapped(term, axis, 1)
    bits = [1 << b for b in range(1, n.bit_length() - 1)]
    halves = jnp.split(term, 2, axis=0)
    for first, second in zip(bits, bits[::-1]):
        sent = [h.astype(jnp.bfloat16) for h in halves]
        got = [swapped(s, axis, bit) for s, bit in zip(sent, (first, second))]
        halves = [s.astype(jnp.float32) + r.astype(jnp.float32) for s, r in zip(sent, got)]
    return jnp.concatenate(halves, axis=0)


def on_device(volume, kernel, upstream):
    cb, planes, hgt, wid = volume.shape
    ob = upstream.shape[0]
    out_ch = kernel.shape[4]
    n_chan, n_space = lax.axis_size("chan"), lax.axis_size("space")
    direct = n_chan <= FEW
    n = n_chan if direct else 1
    taps = 27 * cb
    lanes = hgt // 4 * wid
    cells = planes // 2 * lanes
    rim = lax.ppermute(volume[:, -1:], "space", [(i, i + 1) for i in range(n_space - 1)])
    weights = kernel.transpose(1, 2, 3, 0, 4).reshape(taps, out_ch)
    up = upstream[:, 0].transpose(1, 0, 2)

    part_shape = jax.ShapeDtypeStruct((ob if direct else out_ch, cells), jnp.float32)
    scratch = [pltpu.VMEM((cb * hgt, wid), jnp.float32)]
    if n > 1:
        scratch.append(pltpu.VMEM((out_ch, cells), jnp.float32))
    cols, *parts = pl.pallas_call(
        functools.partial(fwd_kernel, n, ob),
        out_shape=[jax.ShapeDtypeStruct((taps, cells), jnp.bfloat16)] + [part_shape] * n,
        scratch_shapes=scratch,
        compiler_params=params(),
    )(volume, rim, weights)
    if direct:
        parts = parts[:1] + [shifted_by(parts[k], "chan", k) for k in range(1, n)]
    else:
        parts = [lax.psum_scatter(parts[0], "chan", scatter_dimension=0, tiled=True)]

    pooled, own = pl.pallas_call(
        act_kernel,
        out_shape=[
            jax.ShapeDtypeStruct(up.shape, jnp.bfloat16),
            jax.ShapeDtypeStruct((ob, cells), jnp.bfloat16),
        ],
        compiler_params=params(),
    )(up, *parts)
    pooled = pooled.transpose(1, 0, 2)[:, None]
    if direct:
        blocks = [own] + [shifted_by(own, "chan", k) for k in range(1, n)]
    else:
        blocks = [lax.all_gather(own, "chan", axis=0, tiled=True)]

    weight_grad, grad = pl.pallas_call(
        functools.partial(weight_kernel, n),
        out_shape=[
            jax.ShapeDtypeStruct((taps, out_ch), jnp.float32),
            jax.ShapeDtypeStruct((out_ch, cells), jnp.bfloat16),
        ],
        compiler_params=params(),
    )(cols, *blocks)
    weight_grad = sum_over(weight_grad, "space")
    weight_grad = weight_grad.reshape(3, 3, 3, cb, out_ch).transpose(3, 0, 1, 2, 4)

    after = lax.ppermute(grad[:, :lanes], "space", [(i + 1, i) for i in range(n_space - 1)])
    input_grad = pl.pallas_call(
        input_kernel,
        out_shape=jax.ShapeDtypeStruct(volume.shape, jnp.bfloat16),
        scratch_shapes=[pltpu.VMEM((cb * planes * hgt, wid), jnp.float32)],
        compiler_params=params(),
    )(weights, grad, after)
    return pooled, input_grad, weight_grad


def solution(mesh):
    return jax.shard_map(
        on_device,
        mesh=mesh,
        in_specs=(
            P("chan", "space", None, None),
            P("chan", None, None, None, None),
            P("chan", "space", None, None),
        ),
        out_specs=(
            P("chan", "space", None, None),
            P("chan", "space", None, None),
            P("chan", None, None, None, None),
        ),
        check_vma=False,
    )
```

```python
import functools

import jax
import jax.numpy as jnp
from jax import lax
from jax.experimental import pallas as pl
from jax.experimental.pallas import tpu as pltpu
from jax.sharding import PartitionSpec as P

SLOPE = 0.3
VMEM = 56 * 1024 * 1024
FEW = 4


def params():
    return pltpu.CompilerParams(vmem_limit_bytes=VMEM)


def pair_matrix(transposed, wid, half):
    shape = (3 * wid, 2 * wid) if transposed else (2 * wid, 3 * wid)
    long, short = (0, 1) if transposed else (1, 0)
    src = lax.broadcasted_iota(jnp.int32, shape, short)
    dst = lax.broadcasted_iota(jnp.int32, shape, long)
    e = (dst >= wid).astype(jnp.int32) + (dst >= 2 * wid).astype(jnp.int32)
    rest = dst - e * wid
    h = (rest >= half).astype(jnp.int32)
    x = 2 * (rest - h * half) + e - 1
    hit = (x >= 0) & (x < wid) & (src == h * wid + x)
    return jnp.where(hit, 1.0, 0.0).astype(jnp.bfloat16)


def fwd_kernel(n, ob, behind_ref, even_ref, odd_ref, w_ref, cols_ref, *rest):
    part_refs = rest[:-2] if n > 1 else rest[:-1]
    wide_ref = rest[-2] if n > 1 else rest[-1]
    cb, _, hgt, wid = even_ref.shape
    groups = hgt // 4
    sel = pair_matrix(False, wid, wid // 2)
    zero = jnp.zeros((cb, wid), jnp.float32)
    for a, plane_ref in enumerate((behind_ref, even_ref, odd_ref)):
        wide_ref[...] = plane_ref[:, 0].astype(jnp.float32).reshape(cb * hgt, wid)
        row = [wide_ref[pl.ds(y, cb, stride=hgt), :] for y in range(hgt)]
        cls = [[row[4 * j + r] for j in range(groups)] for r in range(4)]

        def stack(blocks):
            return jnp.concatenate(blocks, axis=0).astype(jnp.bfloat16)

        back = stack([zero] + cls[3][:-1])
        cls = [stack(c) for c in cls]
        for b, (left, right) in enumerate(((back, cls[1]), (cls[0], cls[2]), (cls[1], cls[3]))):
            taps = jnp.dot(
                jnp.concatenate([left, right], axis=1), sel, preferred_element_type=jnp.float32
            )
            for e in range(3):
                block = taps[:, e * wid : (e + 1) * wid].astype(jnp.bfloat16)
                tap = (a * 3 + b) * 3 + e
                cols_ref[tap * cb : (tap + 1) * cb, :] = jnp.concatenate(
                    [block[j * cb : (j + 1) * cb] for j in range(groups)], axis=1
                )
    part = lax.dot_general(
        w_ref[...],
        cols_ref[...],
        (((0,), (0,)), ((), ())),
        preferred_element_type=jnp.float32,
    )
    if n == 1:
        part_refs[0][...] = part
        return
    all_ref = rest[-1]
    all_ref[...] = part
    me = lax.axis_index("chan")
    for k, ref in enumerate(part_refs):
        start = pl.multiple_of(lax.rem(me + k, n) * ob, ob)
        ref[...] = all_ref[pl.ds(start, ob), :]


def spread_kernel(up_ref, out_ref):
    groups, ob, small = up_ref.shape
    wid = 4 * small
    r = lax.broadcasted_iota(jnp.int32, (small, wid), 0)
    c = lax.broadcasted_iota(jnp.int32, (small, wid), 1)
    c = c - jnp.where(c >= 2 * small, 2 * small, 0)
    grow = jnp.where((c >= 2 * r) & (c <= 2 * r + 1), 1.0, 0.0).astype(jnp.bfloat16)
    for j in range(groups):
        spread = jnp.dot(up_ref[j], grow, preferred_element_type=jnp.float32)
        out_ref[:, j * wid : (j + 1) * wid] = spread * 0.125


def act_kernel(spread_ref, *rest):
    *part_refs, grad_ref, act_ref = rest
    pre = part_refs[0][...]
    for ref in part_refs[1:]:
        pre = pre + ref[...]
    grad = spread_ref[...] * jnp.where(pre > 0, 1.0, SLOPE)
    grad_ref[...] = grad.astype(jnp.bfloat16)
    act_ref[...] = jnp.where(pre > 0, pre, SLOPE * pre)


def pool_kernel(one_ref, two_ref, out_ref):
    groups, ob, small = out_ref.shape
    wid = 4 * small
    r = lax.broadcasted_iota(jnp.int32, (wid, small), 0)
    c = lax.broadcasted_iota(jnp.int32, (wid, small), 1)
    r = r - jnp.where(r >= 2 * small, 2 * small, 0)
    pool = jnp.where((r >= 2 * c) & (r <= 2 * c + 1), 0.125, 0.0)
    act = one_ref[...] + two_ref[...]
    for j in range(groups):
        out_ref[j] = jnp.dot(
            act[:, j * wid : (j + 1) * wid],
            pool,
            precision=lax.Precision.HIGHEST,
            preferred_element_type=jnp.float32,
        ).astype(jnp.bfloat16)


def weight_kernel(n, first, *refs):
    if first:
        cols_ref, *block_refs, wgrad_ref, grad_ref = refs
    else:
        sum_ref, cols_ref, *block_refs, wgrad_ref, grad_ref = refs
    if n == 1:
        grad_ref[...] = block_refs[0][...]
    else:
        me = lax.axis_index("chan")
        ob = block_refs[0].shape[0]
        for k, ref in enumerate(block_refs):
            start = pl.multiple_of(lax.rem(me + n - k, n) * ob, ob)
            grad_ref[pl.ds(start, ob), :] = ref[...]
    term = lax.dot_general(
        cols_ref[...],
        grad_ref[...],
        (((1,), (1,)), ((), ())),
        preferred_element_type=jnp.float32,
    )
    wgrad_ref[...] = term if first else sum_ref[...] + term


def input_kernel(w_ref, *rest):
    *grad_refs, out_ref, wide_ref = rest
    cb, planes, hgt, wid = out_ref.shape
    half = wid // 2
    groups = hgt // 4
    lanes = groups * wid
    taps = 9 * cb
    spread = pair_matrix(True, wid, half)
    spread = jnp.concatenate([spread, spread], axis=0)
    keep = lax.broadcasted_iota(jnp.int32, (3 * cb, lanes), 1) < lanes - half
    w = [w_ref[a * taps : (a + 1) * taps, :] for a in range(3)]
    behind = jnp.concatenate([w[2], w[0]], axis=1)
    g = [ref[...] for ref in grad_refs]
    for i in range(planes):
        z = i // 2
        if i % 2 == 0:
            e_all = jnp.dot(w[1], g[z], preferred_element_type=jnp.float32)
        else:
            e_all = jnp.dot(
                behind,
                jnp.concatenate([g[z], g[z + 1]], axis=0),
                preferred_element_type=jnp.float32,
            )
        by_b = [e_all[b * 3 * cb : (b + 1) * 3 * cb] for b in range(3)]
        shifted = pltpu.roll(by_b[0], lanes - half, 1)
        rows = (by_b[1], by_b[2] + jnp.where(keep, shifted, 0.0))
        left = []
        for f in rows:
            for j in range(groups):
                t = f[:, j * wid : (j + 1) * wid]
                left.append(
                    jnp.concatenate([t[e * cb : (e + 1) * cb] for e in range(3)], axis=1)
                )
        left = jnp.concatenate(left, axis=0)
        high = left.astype(jnp.bfloat16)
        low = (left - high.astype(jnp.float32)).astype(jnp.bfloat16)
        full = jnp.dot(
            jnp.concatenate([high, low], axis=1), spread, preferred_element_type=jnp.float32
        )
        for par in range(2):
            for j in range(groups):
                for h in range(2):
                    y = 2 * (2 * j + h) + par
                    at = (par * groups + j) * cb
                    wide_ref[pl.ds(i * hgt + y, cb, stride=planes * hgt), :] = full[
                        at : at + cb, h * wid : (h + 1) * wid
                    ]
    out_ref[...] = wide_ref[...].reshape(cb, planes, hgt, wid).astype(jnp.bfloat16)


def shifted_by(block, axis, k):
    n = lax.axis_size(axis)
    return lax.ppermute(block, axis, [(i, (i + k) % n) for i in range(n)])


def swapped(block, axis, bit):
    n = lax.axis_size(axis)
    return lax.ppermute(block, axis, [(i, i ^ bit) for i in range(n)])


def sum_over(term, axis):
    n = lax.axis_size(axis)
    if n & (n - 1):
        return lax.psum(term, axis)
    if n > 1:
        term = term + swapped(term, axis, 1)
    bits = [1 << b for b in range(1, n.bit_length() - 1)]
    halves = jnp.split(term, 2, axis=0)
    for first, second in zip(bits, bits[::-1]):
        sent = [h.astype(jnp.bfloat16) for h in halves]
        got = [swapped(s, axis, bit) for s, bit in zip(sent, (first, second))]
        halves = [s.astype(jnp.float32) + r.astype(jnp.float32) for s, r in zip(sent, got)]
    return jnp.concatenate(halves, axis=0)


def on_device(volume, kernel, upstream):
    cb, planes, hgt, wid = volume.shape
    ob = upstream.shape[0]
    out_ch = kernel.shape[4]
    n_chan, n_space = lax.axis_size("chan"), lax.axis_size("space")
    direct = n_chan <= FEW
    n = n_chan if direct else 1
    taps = 27 * cb
    cells = hgt // 4 * wid
    f32, bf16 = jnp.float32, jnp.bfloat16
    rim = lax.ppermute(volume[:, -1:], "space", [(i, i + 1) for i in range(n_space - 1)])
    weights = kernel.transpose(1, 2, 3, 0, 4).reshape(taps, out_ch)
    up = upstream[:, 0].transpose(1, 0, 2)
    spread = pl.pallas_call(
        spread_kernel,
        out_shape=jax.ShapeDtypeStruct((ob, cells), f32),
        compiler_params=params(),
    )(up)

    scratch = [pltpu.VMEM((cb * hgt, wid), f32)]
    if n > 1:
        scratch.append(pltpu.VMEM((out_ch, cells), f32))
    part_shape = jax.ShapeDtypeStruct((ob if direct else out_ch, cells), f32)
    whole = pl.BlockSpec(memory_space=pltpu.VMEM)

    def plane(p):
        return pl.BlockSpec((cb, 1, hgt, wid), lambda i: (0, max(p, 0), 0, 0))

    out_planes = range(planes // 2)
    cols, grads, acts = {}, {}, {}
    for z in reversed(out_planes):
        cols[z], *parts = pl.pallas_call(
            functools.partial(fwd_kernel, n, ob),
            grid=(1,),
            in_specs=[plane(2 * z - 1), plane(2 * z), plane(2 * z + 1), whole],
            out_specs=[whole] * (n + 1),
            out_shape=[jax.ShapeDtypeStruct((taps, cells), bf16)] + [part_shape] * n,
            scratch_shapes=scratch,
            compiler_params=params(),
        )(volume if z else rim, volume, volume, weights)
        if direct:
            parts = parts[:1] + [shifted_by(parts[k], "chan", k) for k in range(1, n)]
        else:
            parts = [lax.psum_scatter(parts[0], "chan", scatter_dimension=0, tiled=True)]
        own, acts[z] = pl.pallas_call(
            act_kernel,
            out_shape=[
                jax.ShapeDtypeStruct((ob, cells), bf16),
                jax.ShapeDtypeStruct((ob, cells), f32),
            ],
            compiler_params=params(),
        )(spread, *parts)
        if direct:
            grads[z] = [own] + [shifted_by(own, "chan", k) for k in range(1, n)]
        else:
            grads[z] = [lax.all_gather(own, "chan", axis=0, tiled=True)]

    pooled = pl.pallas_call(
        pool_kernel,
        out_shape=jax.ShapeDtypeStruct(up.shape, bf16),
        compiler_params=params(),
    )(acts[0], acts[1])
    pooled = pooled.transpose(1, 0, 2)[:, None]

    weight_grad = []
    for z in reversed(out_planes):
        wgrad, grads[z] = pl.pallas_call(
            functools.partial(weight_kernel, n, not weight_grad),
            out_shape=[
                jax.ShapeDtypeStruct((taps, out_ch), f32),
                jax.ShapeDtypeStruct((out_ch, cells), bf16),
            ],
            compiler_params=params(),
        )(*weight_grad, cols[z], *grads[z])
        weight_grad = [wgrad]
    after = lax.ppermute(grads[0], "space", [(i + 1, i) for i in range(n_space - 1)])
    weight_grad = sum_over(weight_grad[0], "space")
    weight_grad = weight_grad.reshape(3, 3, 3, cb, out_ch).transpose(3, 0, 1, 2, 4)

    input_grad = pl.pallas_call(
        input_kernel,
        out_shape=jax.ShapeDtypeStruct(volume.shape, bf16),
        scratch_shapes=[pltpu.VMEM((cb * planes * hgt, wid), f32)],
        compiler_params=params(),
    )(weights, *[grads[z] for z in out_planes], after)
    return pooled, input_grad, weight_grad


def solution(mesh):
    return jax.shard_map(
        on_device,
        mesh=mesh,
        in_specs=(
            P("chan", "space", None, None),
            P("chan", None, None, None, None),
            P("chan", "space", None, None),
        ),
        out_specs=(
            P("chan", "space", None, None),
            P("chan", "space", None, None),
            P("chan", None, None, None, None),
        ),
        check_vma=False,
    )
```

```python
import functools

import jax
import jax.numpy as jnp
from jax import lax
from jax.experimental import pallas as pl
from jax.experimental.pallas import tpu as pltpu
from jax.sharding import PartitionSpec as P

SLOPE = 0.3
VMEM = 24 * 1024 * 1024
FEW = 4


def params():
    return pltpu.CompilerParams(vmem_limit_bytes=VMEM)


def pair_matrix(transposed, wid, half):
    shape = (3 * wid, 2 * wid) if transposed else (2 * wid, 3 * wid)
    long, short = (0, 1) if transposed else (1, 0)
    src = lax.broadcasted_iota(jnp.int32, shape, short)
    dst = lax.broadcasted_iota(jnp.int32, shape, long)
    e = (dst >= wid).astype(jnp.int32) + (dst >= 2 * wid).astype(jnp.int32)
    rest = dst - e * wid
    h = (rest >= half).astype(jnp.int32)
    x = 2 * (rest - h * half) + e - 1
    hit = (x >= 0) & (x < wid) & (src == h * wid + x)
    return jnp.where(hit, 1.0, 0.0).astype(jnp.bfloat16)


def fwd_kernel(n, ob, behind_ref, even_ref, odd_ref, w_ref, cols_ref, *rest):
    part_refs = rest[:-2] if n > 1 else rest[:-1]
    wide_ref = rest[-2] if n > 1 else rest[-1]
    cb, _, hgt, wid = even_ref.shape
    groups = hgt // 4
    sel = pair_matrix(False, wid, wid // 2)
    zero = jnp.zeros((cb, wid), jnp.float32)
    for a, plane_ref in enumerate((behind_ref, even_ref, odd_ref)):
        wide_ref[...] = plane_ref[:, 0].astype(jnp.float32).reshape(cb * hgt, wid)
        row = [wide_ref[pl.ds(y, cb, stride=hgt), :] for y in range(hgt)]
        cls = [[row[4 * j + r] for j in range(groups)] for r in range(4)]

        def stack(blocks):
            return jnp.concatenate(blocks, axis=0).astype(jnp.bfloat16)

        back = stack([zero] + cls[3][:-1])
        cls = [stack(c) for c in cls]
        for b, (left, right) in enumerate(((back, cls[1]), (cls[0], cls[2]), (cls[1], cls[3]))):
            taps = jnp.dot(
                jnp.concatenate([left, right], axis=1), sel, preferred_element_type=jnp.float32
            )
            for e in range(3):
                block = taps[:, e * wid : (e + 1) * wid].astype(jnp.bfloat16)
                tap = (a * 3 + b) * 3 + e
                cols_ref[tap * cb : (tap + 1) * cb, :] = jnp.concatenate(
                    [block[j * cb : (j + 1) * cb] for j in range(groups)], axis=1
                )
    part = lax.dot_general(
        w_ref[...],
        cols_ref[...],
        (((0,), (0,)), ((), ())),
        preferred_element_type=jnp.float32,
    )
    if n == 1:
        part_refs[0][...] = part
        return
    all_ref = rest[-1]
    all_ref[...] = part
    me = lax.axis_index("chan")
    for k, ref in enumerate(part_refs):
        start = pl.multiple_of(lax.rem(me + k, n) * ob, ob)
        ref[...] = all_ref[pl.ds(start, ob), :]


def spread_kernel(up_ref, out_ref):
    groups, ob, small = up_ref.shape
    wid = 4 * small
    r = lax.broadcasted_iota(jnp.int32, (small, wid), 0)
    c = lax.broadcasted_iota(jnp.int32, (small, wid), 1)
    c = c - jnp.where(c >= 2 * small, 2 * small, 0)
    grow = jnp.where((c >= 2 * r) & (c <= 2 * r + 1), 1.0, 0.0).astype(jnp.bfloat16)
    for j in range(groups):
        spread = jnp.dot(up_ref[j], grow, preferred_element_type=jnp.float32)
        out_ref[:, j * wid : (j + 1) * wid] = spread * 0.125


def act_kernel(spread_ref, *rest):
    *part_refs, grad_ref, act_ref = rest
    pre = part_refs[0][...]
    for ref in part_refs[1:]:
        pre = pre + ref[...]
    grad = spread_ref[...] * jnp.where(pre > 0, 1.0, SLOPE)
    grad_ref[...] = grad.astype(jnp.bfloat16)
    act_ref[...] = jnp.where(pre > 0, pre, SLOPE * pre)


def pool_kernel(one_ref, two_ref, out_ref):
    groups, ob, small = out_ref.shape
    wid = 4 * small
    r = lax.broadcasted_iota(jnp.int32, (wid, small), 0)
    c = lax.broadcasted_iota(jnp.int32, (wid, small), 1)
    r = r - jnp.where(r >= 2 * small, 2 * small, 0)
    pool = jnp.where((r >= 2 * c) & (r <= 2 * c + 1), 0.125, 0.0)
    act = one_ref[...] + two_ref[...]
    for j in range(groups):
        out_ref[j] = jnp.dot(
            act[:, j * wid : (j + 1) * wid],
            pool,
            precision=lax.Precision.HIGHEST,
            preferred_element_type=jnp.float32,
        ).astype(jnp.bfloat16)


def weight_kernel(n, first, *refs):
    if first:
        cols_ref, *block_refs, wgrad_ref, grad_ref = refs
    else:
        sum_ref, cols_ref, *block_refs, wgrad_ref, grad_ref = refs
    if n == 1:
        grad_ref[...] = block_refs[0][...]
    else:
        me = lax.axis_index("chan")
        ob = block_refs[0].shape[0]
        for k, ref in enumerate(block_refs):
            start = pl.multiple_of(lax.rem(me + n - k, n) * ob, ob)
            grad_ref[pl.ds(start, ob), :] = ref[...]
    term = lax.dot_general(
        cols_ref[...],
        grad_ref[...],
        (((1,), (1,)), ((), ())),
        preferred_element_type=jnp.float32,
    )
    wgrad_ref[...] = term if first else sum_ref[...] + term


def input_kernel(w_ref, *rest):
    *grad_refs, out_ref, wide_ref = rest
    cb, planes, hgt, wid = out_ref.shape
    half = wid // 2
    groups = hgt // 4
    lanes = groups * wid
    taps = 9 * cb
    spread = pair_matrix(True, wid, half)
    spread = jnp.concatenate([spread, spread], axis=0)
    keep = lax.broadcasted_iota(jnp.int32, (3 * cb, lanes), 1) < lanes - half
    w = [w_ref[a * taps : (a + 1) * taps, :] for a in range(3)]
    behind = jnp.concatenate([w[2], w[0]], axis=1)
    g = [ref[...] for ref in grad_refs]
    for i in range(planes):
        z = i // 2
        if i % 2 == 0:
            e_all = jnp.dot(w[1], g[z], preferred_element_type=jnp.float32)
        else:
            e_all = jnp.dot(
                behind,
                jnp.concatenate([g[z], g[z + 1]], axis=0),
                preferred_element_type=jnp.float32,
            )
        by_b = [e_all[b * 3 * cb : (b + 1) * 3 * cb] for b in range(3)]
        shifted = pltpu.roll(by_b[0], lanes - half, 1)
        rows = (by_b[1], by_b[2] + jnp.where(keep, shifted, 0.0))
        left = []
        for f in rows:
            for j in range(groups):
                t = f[:, j * wid : (j + 1) * wid]
                left.append(
                    jnp.concatenate([t[e * cb : (e + 1) * cb] for e in range(3)], axis=1)
                )
        left = jnp.concatenate(left, axis=0)
        high = left.astype(jnp.bfloat16)
        low = (left - high.astype(jnp.float32)).astype(jnp.bfloat16)
        full = jnp.dot(
            jnp.concatenate([high, low], axis=1), spread, preferred_element_type=jnp.float32
        )
        for par in range(2):
            for j in range(groups):
                for h in range(2):
                    y = 2 * (2 * j + h) + par
                    at = (par * groups + j) * cb
                    wide_ref[pl.ds(i * hgt + y, cb, stride=planes * hgt), :] = full[
                        at : at + cb, h * wid : (h + 1) * wid
                    ]
    out_ref[...] = wide_ref[...].reshape(cb, planes, hgt, wid).astype(jnp.bfloat16)


def shifted_by(block, axis, k):
    n = lax.axis_size(axis)
    return lax.ppermute(block, axis, [(i, (i + k) % n) for i in range(n)])


def swapped(block, axis, bit):
    n = lax.axis_size(axis)
    return lax.ppermute(block, axis, [(i, i ^ bit) for i in range(n)])


def sum_over(term, axis):
    n = lax.axis_size(axis)
    if n & (n - 1):
        return lax.psum(term, axis)
    if n > 1:
        term = term + swapped(term, axis, 1)
    bits = [1 << b for b in range(1, n.bit_length() - 1)]
    halves = jnp.split(term, 2, axis=0)
    for first, second in zip(bits, bits[::-1]):
        sent = [h.astype(jnp.bfloat16) for h in halves]
        got = [swapped(s, axis, bit) for s, bit in zip(sent, (first, second))]
        halves = [s.astype(jnp.float32) + r.astype(jnp.float32) for s, r in zip(sent, got)]
    return jnp.concatenate(halves, axis=0)


def on_device(volume, kernel, upstream):
    cb, planes, hgt, wid = volume.shape
    ob = upstream.shape[0]
    out_ch = kernel.shape[4]
    n_chan, n_space = lax.axis_size("chan"), lax.axis_size("space")
    direct = n_chan <= FEW
    n = n_chan if direct else 1
    taps = 27 * cb
    cells = hgt // 4 * wid
    f32, bf16 = jnp.float32, jnp.bfloat16
    rim = lax.ppermute(volume[:, -1:], "space", [(i, i + 1) for i in range(n_space - 1)])
    weights = kernel.transpose(1, 2, 3, 0, 4).reshape(taps, out_ch)
    up = upstream[:, 0].transpose(1, 0, 2)
    spread = pl.pallas_call(
        spread_kernel,
        out_shape=jax.ShapeDtypeStruct((ob, cells), f32),
        compiler_params=params(),
    )(up)

    scratch = [pltpu.VMEM((cb * hgt, wid), f32)]
    if n > 1:
        scratch.append(pltpu.VMEM((out_ch, cells), f32))
    part_shape = jax.ShapeDtypeStruct((ob if direct else out_ch, cells), f32)
    whole = pl.BlockSpec(memory_space=pltpu.VMEM)

    def plane(p):
        return pl.BlockSpec((cb, 1, hgt, wid), lambda i: (0, max(p, 0), 0, 0))

    out_planes = range(planes // 2)
    cols, grads, acts = {}, {}, {}
    for z in reversed(out_planes):
        cols[z], *parts = pl.pallas_call(
            functools.partial(fwd_kernel, n, ob),
            grid=(1,),
            in_specs=[plane(2 * z - 1), plane(2 * z), plane(2 * z + 1), whole],
            out_specs=[whole] * (n + 1),
            out_shape=[jax.ShapeDtypeStruct((taps, cells), bf16)] + [part_shape] * n,
            scratch_shapes=scratch,
            compiler_params=params(),
        )(volume if z else rim, volume, volume, weights)
        if direct:
            parts = parts[:1] + [shifted_by(parts[k], "chan", k) for k in range(1, n)]
        else:
            parts = [lax.psum_scatter(parts[0], "chan", scatter_dimension=0, tiled=True)]
        own, acts[z] = pl.pallas_call(
            act_kernel,
            out_shape=[
                jax.ShapeDtypeStruct((ob, cells), bf16),
                jax.ShapeDtypeStruct((ob, cells), f32),
            ],
            compiler_params=params(),
        )(spread, *parts)
        if direct:
            grads[z] = [own] + [shifted_by(own, "chan", k) for k in range(1, n)]
        else:
            grads[z] = [lax.all_gather(own, "chan", axis=0, tiled=True)]

    pooled = pl.pallas_call(
        pool_kernel,
        out_shape=jax.ShapeDtypeStruct(up.shape, bf16),
        compiler_params=params(),
    )(acts[0], acts[1])
    pooled = pooled.transpose(1, 0, 2)[:, None]

    weight_grad = []
    for z in reversed(out_planes):
        wgrad, grads[z] = pl.pallas_call(
            functools.partial(weight_kernel, n, not weight_grad),
            out_shape=[
                jax.ShapeDtypeStruct((taps, out_ch), f32),
                jax.ShapeDtypeStruct((out_ch, cells), bf16),
            ],
            compiler_params=params(),
        )(*weight_grad, cols[z], *grads[z])
        weight_grad = [wgrad]
    after = lax.ppermute(grads[0], "space", [(i + 1, i) for i in range(n_space - 1)])
    weight_grad = sum_over(weight_grad[0], "space")
    weight_grad = weight_grad.reshape(3, 3, 3, cb, out_ch).transpose(3, 0, 1, 2, 4)

    input_grad = pl.pallas_call(
        input_kernel,
        out_shape=jax.ShapeDtypeStruct(volume.shape, bf16),
        scratch_shapes=[pltpu.VMEM((cb * planes * hgt, wid), f32)],
        compiler_params=params(),
    )(weights, *[grads[z] for z in out_planes], after)
    return pooled, input_grad, weight_grad


def solution(mesh):
    return jax.shard_map(
        on_device,
        mesh=mesh,
        in_specs=(
            P("chan", "space", None, None),
            P("chan", None, None, None, None),
            P("chan", "space", None, None),
        ),
        out_specs=(
            P("chan", "space", None, None),
            P("chan", "space", None, None),
            P("chan", None, None, None, None),
        ),
        check_vma=False,
    )
```

```python
import functools

import jax
import jax.numpy as jnp
from jax import lax
from jax.experimental import pallas as pl
from jax.experimental.pallas import tpu as pltpu
from jax.sharding import PartitionSpec as P

SLOPE = 0.3
VMEM = 24 * 1024 * 1024
XOR = True
RS = (1, 2, 3)
AG = (1, 2, 3)
FEW = 4


def params():
    return pltpu.CompilerParams(vmem_limit_bytes=VMEM)


def pair_matrix(transposed, wid, half):
    shape = (3 * wid, 2 * wid) if transposed else (2 * wid, 3 * wid)
    long, short = (0, 1) if transposed else (1, 0)
    src = lax.broadcasted_iota(jnp.int32, shape, short)
    dst = lax.broadcasted_iota(jnp.int32, shape, long)
    e = (dst >= wid).astype(jnp.int32) + (dst >= 2 * wid).astype(jnp.int32)
    rest = dst - e * wid
    h = (rest >= half).astype(jnp.int32)
    x = 2 * (rest - h * half) + e - 1
    hit = (x >= 0) & (x < wid) & (src == h * wid + x)
    return jnp.where(hit, 1.0, 0.0).astype(jnp.bfloat16)


def fwd_kernel(n, ob, z, *refs):
    if z:
        vol_hbm, w_hbm, vol_ref, w_ref, edge_ref, cols_ref, *rest, sems = refs
        planes = vol_ref.shape[1]
        copies = [
            pltpu.make_async_copy(vol_hbm.at[:, p], vol_ref.at[:, p], sems.at[p])
            for p in range(planes)
        ]
        w_copy = pltpu.make_async_copy(w_hbm, w_ref, sems.at[planes])
        order = list(range(2 * z - 1, planes)) + list(range(2 * z - 1))
        for i, p in enumerate(order):
            copies[p].start()
            if i == 2:
                w_copy.start()
    else:
        rim_ref, vol_ref, w_ref, cols_ref, *rest = refs
    part_refs = rest[:-2] if n > 1 else rest[:-1]
    wide_ref = rest[-2] if n > 1 else rest[-1]
    cb, _, hgt, wid = vol_ref.shape
    groups = hgt // 4
    sel = pair_matrix(False, wid, wid // 2)
    zero = jnp.zeros((cb, wid), jnp.float32)
    for a in range(3):
        if z:
            copies[2 * z + a - 1].wait()
            if a == 2:
                edge_ref[...] = vol_ref[:, -1:]
        plane = vol_ref[:, 2 * z + a - 1] if z or a else rim_ref[:, 0]
        wide_ref[...] = plane.astype(jnp.float32).reshape(cb * hgt, wid)
        row = [wide_ref[pl.ds(y, cb, stride=hgt), :] for y in range(hgt)]
        cls = [[row[4 * j + r] for j in range(groups)] for r in range(4)]

        def stack(blocks):
            return jnp.concatenate(blocks, axis=0).astype(jnp.bfloat16)

        back = stack([zero] + cls[3][:-1])
        cls = [stack(c) for c in cls]
        for b, (left, right) in enumerate(((back, cls[1]), (cls[0], cls[2]), (cls[1], cls[3]))):
            taps = jnp.dot(
                jnp.concatenate([left, right], axis=1), sel, preferred_element_type=jnp.float32
            )
            for e in range(3):
                block = taps[:, e * wid : (e + 1) * wid].astype(jnp.bfloat16)
                tap = (a * 3 + b) * 3 + e
                cols_ref[tap * cb : (tap + 1) * cb, :] = jnp.concatenate(
                    [block[j * cb : (j + 1) * cb] for j in range(groups)], axis=1
                )
    if z:
        w_copy.wait()
        for p in range(2 * z - 1):
            copies[p].wait()
    part = lax.dot_general(
        w_ref[...],
        cols_ref[...],
        (((0,), (0,)), ((), ())),
        preferred_element_type=jnp.float32,
    )
    if n == 1:
        part_refs[0][...] = part
        return
    all_ref = rest[-1]
    all_ref[...] = part
    me = lax.axis_index("chan")
    for k, ref in zip((0,) + RS, part_refs):
        start = pl.multiple_of((me ^ k if XOR else lax.rem(me + k, n)) * ob, ob)
        ref[...] = all_ref[pl.ds(start, ob), :]


def spread_kernel(up_ref, out_ref):
    groups, ob, small = up_ref.shape
    wid = 4 * small
    r = lax.broadcasted_iota(jnp.int32, (small, wid), 0)
    c = lax.broadcasted_iota(jnp.int32, (small, wid), 1)
    c = c - jnp.where(c >= 2 * small, 2 * small, 0)
    grow = jnp.where((c >= 2 * r) & (c <= 2 * r + 1), 1.0, 0.0).astype(jnp.bfloat16)
    for j in range(groups):
        spread = jnp.dot(up_ref[j], grow, preferred_element_type=jnp.float32)
        out_ref[:, j * wid : (j + 1) * wid] = spread * 0.125


def act_kernel(spread_ref, *rest):
    *part_refs, grad_ref, act_ref = rest
    pre = part_refs[0][...]
    for ref in part_refs[1:]:
        pre = pre + ref[...]
    grad = spread_ref[...] * jnp.where(pre > 0, 1.0, SLOPE)
    grad_ref[...] = grad.astype(jnp.bfloat16)
    act_ref[...] = jnp.where(pre > 0, pre, SLOPE * pre)


def pool_kernel(one_ref, two_ref, out_ref):
    groups, ob, small = out_ref.shape
    wid = 4 * small
    r = lax.broadcasted_iota(jnp.int32, (wid, small), 0)
    c = lax.broadcasted_iota(jnp.int32, (wid, small), 1)
    r = r - jnp.where(r >= 2 * small, 2 * small, 0)
    pool = jnp.where((r >= 2 * c) & (r <= 2 * c + 1), 0.125, 0.0)
    act = one_ref[...] + two_ref[...]
    for j in range(groups):
        out_ref[j] = jnp.dot(
            act[:, j * wid : (j + 1) * wid],
            pool,
            precision=lax.Precision.HIGHEST,
            preferred_element_type=jnp.float32,
        ).astype(jnp.bfloat16)


def in_order(n, block_refs, grad_ref):
    if n == 1:
        grad_ref[...] = block_refs[0][...]
        return
    me = lax.axis_index("chan")
    ob = block_refs[0].shape[0]
    for k, ref in zip((0,) + AG, block_refs):
        start = pl.multiple_of((me ^ k if XOR else lax.rem(me + n - k, n)) * ob, ob)
        grad_ref[pl.ds(start, ob), :] = ref[...]


def weight_term(cols_ref, grad_ref):
    return lax.dot_general(
        cols_ref[...],
        grad_ref[...],
        (((1,), (1,)), ((), ())),
        preferred_element_type=jnp.float32,
    )


def weight_kernel(n, cols_ref, *refs):
    *block_refs, wgrad_ref, grad_ref = refs
    in_order(n, block_refs, grad_ref)
    wgrad_ref[...] = weight_term(cols_ref, grad_ref)


def last_weight_kernel(n, sum_ref, cols_ref, *refs):
    *block_refs, keep_ref, send_ref, grad_ref, rows_ref = refs
    in_order(n, block_refs, grad_ref)
    taps, half = cols_ref.shape[0], keep_ref.shape[0]
    rows_ref[0:taps, :] = sum_ref[...] + weight_term(cols_ref, grad_ref)
    if 2 * half > taps:
        rows_ref[taps:, :] = jnp.zeros((2 * half - taps, rows_ref.shape[1]), jnp.float32)
    core = lax.rem(lax.axis_index("space"), 2)
    keep_ref[...] = rows_ref[pl.ds(pl.multiple_of(core * half, 8), half), :]
    send_ref[...] = rows_ref[pl.ds(pl.multiple_of((1 - core) * half, 8), half), :]


def join_kernel(own_ref, other_ref, out_ref, sems):
    half = own_ref.shape[0]
    for core in range(2):

        @pl.when(lax.rem(lax.axis_index("space"), 2) == core)
        def _():
            copies = []
            for ref, start in ((own_ref, core * half), (other_ref, (1 - core) * half)):
                size = min(half, out_ref.shape[0] - start)
                copies.append(
                    pltpu.make_async_copy(
                        ref.at[pl.ds(0, size)], out_ref.at[pl.ds(start, size)], sems.at[start // half]
                    )
                )
            for copy in copies:
                copy.start()
            for copy in copies:
                copy.wait()


def input_kernel(w_ref, *rest):
    *grad_refs, out_ref, wide_ref = rest
    cb, planes, hgt, wid = out_ref.shape
    half = wid // 2
    groups = hgt // 4
    lanes = groups * wid
    taps = 9 * cb
    spread = pair_matrix(True, wid, half)
    spread = jnp.concatenate([spread, spread], axis=0)
    keep = lax.broadcasted_iota(jnp.int32, (3 * cb, lanes), 1) < lanes - half
    w = [w_ref[a * taps : (a + 1) * taps, :] for a in range(3)]
    behind = jnp.concatenate([w[2], w[0]], axis=1)
    g = [ref[...] for ref in grad_refs]
    for i in range(planes):
        z = i // 2
        if i % 2 == 0:
            e_all = jnp.dot(w[1], g[z], preferred_element_type=jnp.float32)
        else:
            e_all = jnp.dot(
                behind,
                jnp.concatenate([g[z], g[z + 1]], axis=0),
                preferred_element_type=jnp.float32,
            )
        by_b = [e_all[b * 3 * cb : (b + 1) * 3 * cb] for b in range(3)]
        shifted = pltpu.roll(by_b[0], lanes - half, 1)
        rows = (by_b[1], by_b[2] + jnp.where(keep, shifted, 0.0))
        left = []
        for f in rows:
            for j in range(groups):
                t = f[:, j * wid : (j + 1) * wid]
                left.append(
                    jnp.concatenate([t[e * cb : (e + 1) * cb] for e in range(3)], axis=1)
                )
        left = jnp.concatenate(left, axis=0)
        high = left.astype(jnp.bfloat16)
        low = (left - high.astype(jnp.float32)).astype(jnp.bfloat16)
        full = jnp.dot(
            jnp.concatenate([high, low], axis=1), spread, preferred_element_type=jnp.float32
        )
        for par in range(2):
            for j in range(groups):
                for h in range(2):
                    y = 2 * (2 * j + h) + par
                    at = (par * groups + j) * cb
                    wide_ref[pl.ds(i * hgt + y, cb, stride=planes * hgt), :] = full[
                        at : at + cb, h * wid : (h + 1) * wid
                    ]
    out_ref[...] = wide_ref[...].reshape(cb, planes, hgt, wid).astype(jnp.bfloat16)


def moved(block, axis, k):
    n = lax.axis_size(axis)
    return lax.ppermute(block, axis, [(i, i ^ k if XOR else (i + k) % n) for i in range(n)])


def on_device(volume, kernel, upstream):
    cb, planes, hgt, wid = volume.shape
    ob = upstream.shape[0]
    out_ch = kernel.shape[4]
    n_chan, n_space = lax.axis_size("chan"), lax.axis_size("space")
    direct = n_chan <= FEW and n_chan & (n_chan - 1) == 0
    n = n_chan if direct else 1
    taps = 27 * cb
    cells = hgt // 4 * wid
    f32, bf16 = jnp.float32, jnp.bfloat16
    shape = jax.ShapeDtypeStruct
    weights = kernel.transpose(1, 2, 3, 0, 4).reshape(taps, out_ch)
    up = upstream[:, 0].transpose(1, 0, 2)
    spread = pl.pallas_call(
        spread_kernel, out_shape=shape((ob, cells), f32), compiler_params=params()
    )(up)

    scratch = [pltpu.VMEM((cb * hgt, wid), f32)]
    if n > 1:
        scratch.append(pltpu.VMEM((out_ch, cells), f32))
    part_shapes = [shape((ob if direct else out_ch, cells), f32)] * n
    cols_shape = [shape((taps, cells), bf16)]
    out_planes = range(planes // 2)
    cols, grads, acts = {}, {}, {}
    rim = ()
    for z in reversed(out_planes):
        call = functools.partial(fwd_kernel, n, ob, z)
        if z:
            vol, w, edge, cols[z], *parts = pl.pallas_call(
                call,
                in_specs=[pl.BlockSpec(memory_space=pltpu.HBM)] * 2,
                out_shape=[
                    shape(volume.shape, bf16),
                    shape(weights.shape, bf16),
                    shape((cb, 1, hgt, wid), bf16),
                ]
                + cols_shape
                + part_shapes,
                scratch_shapes=scratch + [pltpu.SemaphoreType.DMA((planes + 1,))],
                compiler_params=params(),
            )(*[pltpu.with_memory_space_constraint(x, pltpu.HBM) for x in (volume, weights)])
            rim = lax.ppermute(edge, "space", [(i, i + 1) for i in range(n_space - 1)])
        else:
            cols[z], *parts = pl.pallas_call(
                call,
                out_shape=cols_shape + part_shapes,
                scratch_shapes=scratch,
                compiler_params=params(),
            )(rim, vol, w)
        if direct:
            parts = parts[:1] + [moved(p, "chan", k) for k, p in zip(RS, parts[1:])]
        else:
            parts = [lax.psum_scatter(parts[0], "chan", scatter_dimension=0, tiled=True)]
        own, acts[z] = pl.pallas_call(
            act_kernel,
            out_shape=[shape((ob, cells), bf16), shape((ob, cells), f32)],
            compiler_params=params(),
        )(spread, *parts)
        if direct:
            grads[z] = [own] + [moved(own, "chan", k) for k in AG]
        else:
            grads[z] = [lax.all_gather(own, "chan", axis=0, tiled=True)]

    pooled = pl.pallas_call(
        pool_kernel, out_shape=shape(up.shape, bf16), compiler_params=params()
    )(acts[0], acts[1])
    pooled = pooled.transpose(1, 0, 2)[:, None]
    half = -(-taps // 32) * 16
    grad_shape = shape((out_ch, cells), bf16)
    term, grads[1] = pl.pallas_call(
        functools.partial(weight_kernel, n),
        out_shape=[shape((taps, out_ch), f32), grad_shape],
        compiler_params=params(),
    )(cols[1], *grads[1])
    keep, send, grads[0] = pl.pallas_call(
        functools.partial(last_weight_kernel, n),
        out_shape=[shape((half, out_ch), f32)] * 2 + [grad_shape],
        scratch_shapes=[pltpu.VMEM((2 * half, out_ch), f32)],
        compiler_params=params(),
    )(term, cols[0], *grads[0])

    rows = keep + lax.ppermute(send, "space", [(i, i ^ 1) for i in range(n_space)])
    bits = [1 << b for b in range(1, n_space.bit_length() - 1)]
    after = input_grad = None
    for r, bit in enumerate(bits):
        sent = rows.astype(bf16)
        if r == 0:
            sent, grads[0] = lax.optimization_barrier((sent, grads[0]))
            after = lax.ppermute(grads[0], "space", [(i + 1, i) for i in range(n_space - 1)])
        if r == len(bits) - 1:
            sent, grads[1] = lax.optimization_barrier((sent, grads[1]))
            input_grad = pl.pallas_call(
                input_kernel,
                out_shape=shape(volume.shape, bf16),
                scratch_shapes=[pltpu.VMEM((cb * planes * hgt, wid), f32)],
                compiler_params=params(),
            )(w, grads[0], grads[1], after)
        pairs = [(i, i ^ (bits[-1 - r] if i & 1 else bit)) for i in range(n_space)]
        got = lax.ppermute(sent, "space", pairs)
        rows = sent.astype(f32) + got.astype(f32)
    rows, input_grad = lax.optimization_barrier((rows, input_grad))
    other = lax.ppermute(rows, "space", [(i, i ^ 1) for i in range(n_space)])
    weight_grad = pl.pallas_call(
        join_kernel,
        out_specs=pl.BlockSpec(memory_space=pltpu.HBM),
        out_shape=shape((taps, out_ch), f32),
        scratch_shapes=[pltpu.SemaphoreType.DMA((2,))],
        compiler_params=params(),
    )(rows, other)
    weight_grad = weight_grad.reshape(3, 3, 3, cb, out_ch).transpose(3, 0, 1, 2, 4)
    return pooled, input_grad, weight_grad


def solution(mesh):
    return jax.shard_map(
        on_device,
        mesh=mesh,
        in_specs=(
            P("chan", "space", None, None),
            P("chan", None, None, None, None),
            P("chan", "space", None, None),
        ),
        out_specs=(
            P("chan", "space", None, None),
            P("chan", "space", None, None),
            P("chan", None, None, None, None),
        ),
        check_vma=False,
    )
```

```python
import functools

import jax
import jax.numpy as jnp
from jax import lax
from jax.experimental import pallas as pl
from jax.experimental.pallas import tpu as pltpu
from jax.sharding import PartitionSpec as P

SLOPE = 0.3
VMEM = 24 * 1024 * 1024
XOR = True
RS = (1, 2, 3)
AG = (1, 2, 3)
FEW = 4


def params():
    return pltpu.CompilerParams(vmem_limit_bytes=VMEM)


def pair_matrix(transposed, wid, half):
    shape = (3 * wid, 2 * wid) if transposed else (2 * wid, 3 * wid)
    long, short = (0, 1) if transposed else (1, 0)
    src = lax.broadcasted_iota(jnp.int32, shape, short)
    dst = lax.broadcasted_iota(jnp.int32, shape, long)
    e = (dst >= wid).astype(jnp.int32) + (dst >= 2 * wid).astype(jnp.int32)
    rest = dst - e * wid
    h = (rest >= half).astype(jnp.int32)
    x = 2 * (rest - h * half) + e - 1
    hit = (x >= 0) & (x < wid) & (src == h * wid + x)
    return jnp.where(hit, 1.0, 0.0).astype(jnp.bfloat16)


def load_kernel(vol_hbm, w_hbm, vol_ref, w_ref, edge_ref, sems):
    planes = vol_ref.shape[1]
    copies = [pltpu.make_async_copy(vol_hbm.at[:, planes - 1 :], edge_ref, sems.at[planes + 1])]
    for p in reversed(range(planes)):
        copies.append(pltpu.make_async_copy(vol_hbm.at[:, p], vol_ref.at[:, p], sems.at[p]))
    copies.append(pltpu.make_async_copy(w_hbm, w_ref, sems.at[planes]))
    for copy in copies:
        copy.start()
    for copy in copies:
        copy.wait()


def fwd_kernel(n, ob, z, *refs):
    if z:
        vol_ref, w_ref, cols_ref, *rest = refs
    else:
        rim_ref, vol_ref, w_ref, cols_ref, *rest = refs
    part_refs = rest[:-2] if n > 1 else rest[:-1]
    wide_ref = rest[-2] if n > 1 else rest[-1]
    cb, _, hgt, wid = vol_ref.shape
    groups = hgt // 4
    sel = pair_matrix(False, wid, wid // 2)
    zero = jnp.zeros((cb, wid), jnp.float32)
    for a in range(3):
        plane = vol_ref[:, 2 * z + a - 1] if z or a else rim_ref[:, 0]
        wide_ref[...] = plane.astype(jnp.float32).reshape(cb * hgt, wid)
        row = [wide_ref[pl.ds(y, cb, stride=hgt), :] for y in range(hgt)]
        cls = [[row[4 * j + r] for j in range(groups)] for r in range(4)]

        def stack(blocks):
            return jnp.concatenate(blocks, axis=0).astype(jnp.bfloat16)

        back = stack([zero] + cls[3][:-1])
        cls = [stack(c) for c in cls]
        for b, (left, right) in enumerate(((back, cls[1]), (cls[0], cls[2]), (cls[1], cls[3]))):
            taps = jnp.dot(
                jnp.concatenate([left, right], axis=1), sel, preferred_element_type=jnp.float32
            )
            for e in range(3):
                block = taps[:, e * wid : (e + 1) * wid].astype(jnp.bfloat16)
                tap = (a * 3 + b) * 3 + e
                cols_ref[tap * cb : (tap + 1) * cb, :] = jnp.concatenate(
                    [block[j * cb : (j + 1) * cb] for j in range(groups)], axis=1
                )
    part = lax.dot_general(
        w_ref[...],
        cols_ref[...],
        (((0,), (0,)), ((), ())),
        preferred_element_type=jnp.float32,
    )
    if n == 1:
        part_refs[0][...] = part
        return
    all_ref = rest[-1]
    all_ref[...] = part
    me = lax.axis_index("chan")
    for k, ref in zip((0,) + RS, part_refs):
        start = pl.multiple_of((me ^ k if XOR else lax.rem(me + k, n)) * ob, ob)
        ref[...] = all_ref[pl.ds(start, ob), :]


def spread_kernel(up_ref, out_ref):
    groups, ob, small = up_ref.shape
    wid = 4 * small
    r = lax.broadcasted_iota(jnp.int32, (small, wid), 0)
    c = lax.broadcasted_iota(jnp.int32, (small, wid), 1)
    c = c - jnp.where(c >= 2 * small, 2 * small, 0)
    grow = jnp.where((c >= 2 * r) & (c <= 2 * r + 1), 1.0, 0.0).astype(jnp.bfloat16)
    for j in range(groups):
        spread = jnp.dot(up_ref[j], grow, preferred_element_type=jnp.float32)
        out_ref[:, j * wid : (j + 1) * wid] = spread * 0.125


def act_kernel(spread_ref, *rest):
    *part_refs, grad_ref, act_ref = rest
    pre = part_refs[0][...]
    for ref in part_refs[1:]:
        pre = pre + ref[...]
    grad = spread_ref[...] * jnp.where(pre > 0, 1.0, SLOPE)
    grad_ref[...] = grad.astype(jnp.bfloat16)
    act_ref[...] = jnp.where(pre > 0, pre, SLOPE * pre)


def pool_kernel(one_ref, two_ref, out_ref):
    ob, _, groups, small = out_ref.shape
    wid = 4 * small
    r = lax.broadcasted_iota(jnp.int32, (wid, small), 0)
    c = lax.broadcasted_iota(jnp.int32, (wid, small), 1)
    r = r - jnp.where(r >= 2 * small, 2 * small, 0)
    pool = jnp.where((r >= 2 * c) & (r <= 2 * c + 1), 0.125, 0.0)
    act = one_ref[...] + two_ref[...]
    means = [
        jnp.dot(
            act[:, j * wid : (j + 1) * wid],
            pool,
            precision=lax.Precision.HIGHEST,
            preferred_element_type=jnp.float32,
        )
        for j in range(groups)
    ]
    out_ref[:, 0] = jnp.stack(means, axis=1).astype(jnp.bfloat16)


def in_order(n, block_refs, grad_ref):
    if n == 1:
        grad_ref[...] = block_refs[0][...]
        return
    me = lax.axis_index("chan")
    ob = block_refs[0].shape[0]
    for k, ref in zip((0,) + AG, block_refs):
        start = pl.multiple_of((me ^ k if XOR else lax.rem(me + n - k, n)) * ob, ob)
        grad_ref[pl.ds(start, ob), :] = ref[...]


def weight_term(cols_ref, grad_ref):
    return lax.dot_general(
        cols_ref[...],
        grad_ref[...],
        (((1,), (1,)), ((), ())),
        preferred_element_type=jnp.float32,
    )


def weight_kernel(n, cols_ref, *refs):
    *block_refs, wgrad_ref, grad_ref = refs
    in_order(n, block_refs, grad_ref)
    wgrad_ref[...] = weight_term(cols_ref, grad_ref)


def last_weight_kernel(n, sum_ref, cols_ref, *refs):
    *block_refs, keep_ref, send_ref, grad_ref, rows_ref = refs
    in_order(n, block_refs, grad_ref)
    taps, half = cols_ref.shape[0], keep_ref.shape[0]
    rows_ref[0:taps, :] = sum_ref[...] + weight_term(cols_ref, grad_ref)
    if 2 * half > taps:
        rows_ref[taps:, :] = jnp.zeros((2 * half - taps, rows_ref.shape[1]), jnp.float32)
    core = lax.rem(lax.axis_index("space"), 2)
    keep_ref[...] = rows_ref[pl.ds(pl.multiple_of(core * half, 8), half), :]
    send_ref[...] = rows_ref[pl.ds(pl.multiple_of((1 - core) * half, 8), half), :]


def join_kernel(own_ref, other_ref, out_ref, sems):
    half = own_ref.shape[0]
    for core in range(2):

        @pl.when(lax.rem(lax.axis_index("space"), 2) == core)
        def _():
            copies = []
            for ref, start in ((own_ref, core * half), (other_ref, (1 - core) * half)):
                size = min(half, out_ref.shape[0] - start)
                copies.append(
                    pltpu.make_async_copy(
                        ref.at[pl.ds(0, size)], out_ref.at[pl.ds(start, size)], sems.at[start // half]
                    )
                )
            for copy in copies:
                copy.start()
            for copy in copies:
                copy.wait()


def input_kernel(own, w_ref, *refs):
    *grad_refs, out_ref, wide_ref, done_ref, sems = refs
    if not own:
        *grad_refs, _ = grad_refs
    cb, planes, hgt, wid = out_ref.shape
    half = wid // 2
    groups = hgt // 4
    lanes = groups * wid
    taps = 9 * cb
    spread = pair_matrix(True, wid, half)
    spread = jnp.concatenate([spread, spread], axis=0)
    keep = lax.broadcasted_iota(jnp.int32, (3 * cb, lanes), 1) < lanes - half
    w = [w_ref[a * taps : (a + 1) * taps, :] for a in range(3)]
    behind = jnp.concatenate([w[2], w[0]], axis=1)
    g = [ref[...] for ref in grad_refs]
    copies = []
    for i in range(planes - 1) if own else (planes - 1,):
        z = i // 2 if own else 0
        if i % 2 == 0:
            e_all = jnp.dot(w[1], g[z], preferred_element_type=jnp.float32)
        else:
            e_all = jnp.dot(
                behind,
                jnp.concatenate([g[z], g[z + 1]], axis=0),
                preferred_element_type=jnp.float32,
            )
        by_b = [e_all[b * 3 * cb : (b + 1) * 3 * cb] for b in range(3)]
        shifted = pltpu.roll(by_b[0], lanes - half, 1)
        rows = (by_b[1], by_b[2] + jnp.where(keep, shifted, 0.0))
        left = []
        for f in rows:
            for j in range(groups):
                t = f[:, j * wid : (j + 1) * wid]
                left.append(
                    jnp.concatenate([t[e * cb : (e + 1) * cb] for e in range(3)], axis=1)
                )
        left = jnp.concatenate(left, axis=0)
        high = left.astype(jnp.bfloat16)
        low = (left - high.astype(jnp.float32)).astype(jnp.bfloat16)
        full = jnp.dot(
            jnp.concatenate([high, low], axis=1), spread, preferred_element_type=jnp.float32
        )
        for par in range(2):
            for j in range(groups):
                for h in range(2):
                    y = 2 * (2 * j + h) + par
                    at = (par * groups + j) * cb
                    wide_ref[pl.ds(y, cb, stride=hgt), :] = full[
                        at : at + cb, h * wid : (h + 1) * wid
                    ]
        slot = i if own else 0
        done_ref[slot] = wide_ref[...].reshape(cb, hgt, wid).astype(jnp.bfloat16)
        copies.append(pltpu.make_async_copy(done_ref.at[slot], out_ref.at[:, i], sems.at[slot]))
        copies[-1].start()
    for copy in copies:
        copy.wait()


def moved(block, axis, k):
    n = lax.axis_size(axis)
    return lax.ppermute(block, axis, [(i, i ^ k if XOR else (i + k) % n) for i in range(n)])


def on_device(volume, kernel, upstream):
    cb, planes, hgt, wid = volume.shape
    ob = upstream.shape[0]
    out_ch = kernel.shape[4]
    n_chan, n_space = lax.axis_size("chan"), lax.axis_size("space")
    direct = n_chan <= FEW and n_chan & (n_chan - 1) == 0
    n = n_chan if direct else 1
    taps = 27 * cb
    cells = hgt // 4 * wid
    f32, bf16 = jnp.float32, jnp.bfloat16
    shape = jax.ShapeDtypeStruct
    weights = kernel.transpose(1, 2, 3, 0, 4).reshape(taps, out_ch)
    up = upstream[:, 0].transpose(1, 0, 2)
    spread = pl.pallas_call(
        spread_kernel, out_shape=shape((ob, cells), f32), compiler_params=params()
    )(up)

    scratch = [pltpu.VMEM((cb * hgt, wid), f32)]
    if n > 1:
        scratch.append(pltpu.VMEM((out_ch, cells), f32))
    part_shapes = [shape((ob if direct else out_ch, cells), f32)] * n
    out_planes = range(planes // 2)
    cols, grads, acts = {}, {}, {}
    vol, w, edge = pl.pallas_call(
        load_kernel,
        in_specs=[pl.BlockSpec(memory_space=pltpu.HBM)] * 2,
        out_shape=[
            shape(volume.shape, bf16),
            shape(weights.shape, bf16),
            shape((cb, 1, hgt, wid), bf16),
        ],
        scratch_shapes=[pltpu.SemaphoreType.DMA((planes + 2,))],
        compiler_params=params(),
    )(*[pltpu.with_memory_space_constraint(x, pltpu.HBM) for x in (volume, weights)])
    rim = lax.ppermute(edge, "space", [(i, i + 1) for i in range(n_space - 1)])
    for z in reversed(out_planes):
        cols[z], *parts = pl.pallas_call(
            functools.partial(fwd_kernel, n, ob, z),
            out_shape=[shape((taps, cells), bf16)] + part_shapes,
            scratch_shapes=scratch,
            compiler_params=params(),
        )(*(() if z else (rim,)), vol, w)
        if direct:
            parts = parts[:1] + [moved(p, "chan", k) for k, p in zip(RS, parts[1:])]
        else:
            parts = [lax.psum_scatter(parts[0], "chan", scatter_dimension=0, tiled=True)]
        own, acts[z] = pl.pallas_call(
            act_kernel,
            out_shape=[shape((ob, cells), bf16), shape((ob, cells), f32)],
            compiler_params=params(),
        )(spread, *parts)
        if direct:
            grads[z] = [own] + [moved(own, "chan", k) for k in AG]
        else:
            grads[z] = [lax.all_gather(own, "chan", axis=0, tiled=True)]

    half = -(-taps // 32) * 16
    grad_shape = shape((out_ch, cells), bf16)
    term, grads[1] = pl.pallas_call(
        functools.partial(weight_kernel, n),
        out_shape=[shape((taps, out_ch), f32), grad_shape],
        compiler_params=params(),
    )(cols[1], *grads[1])
    keep, send, grads[0] = pl.pallas_call(
        functools.partial(last_weight_kernel, n),
        out_shape=[shape((half, out_ch), f32)] * 2 + [grad_shape],
        scratch_shapes=[pltpu.VMEM((2 * half, out_ch), f32)],
        compiler_params=params(),
    )(term, cols[0], *grads[0])

    def input_call(own, *operands):
        n_done = planes - 1 if own else 1
        hbm = pl.BlockSpec(memory_space=pltpu.HBM)
        vmem = pl.BlockSpec(memory_space=pltpu.VMEM)
        return pl.pallas_call(
            functools.partial(input_kernel, own),
            in_specs=[vmem] * 3 + [hbm] * (not own),
            out_specs=hbm,
            out_shape=shape(volume.shape, bf16),
            scratch_shapes=[
                pltpu.VMEM((cb * hgt, wid), f32),
                pltpu.VMEM((n_done, cb, hgt, wid), bf16),
                pltpu.SemaphoreType.DMA((n_done,)),
            ],
            input_output_aliases={} if own else {3: 0},
            compiler_params=params(),
        )(*operands)

    rows = keep + lax.ppermute(send, "space", [(i, i ^ 1) for i in range(n_space)])
    bits = [1 << b for b in range(1, n_space.bit_length() - 1)]
    groups = [bits[i : i + 2] for i in range(0, len(bits), 2)]
    after = input_grad = pooled = None
    for r, group in enumerate(groups):
        sent = rows.astype(bf16)
        if r == len(groups) - 1:
            sent, grads, acts = lax.optimization_barrier((sent, grads, acts))
        partners = [sum(group[b] * (k >> b & 1) for b in range(len(group))) for k in range(1, 1 << len(group))]
        terms = [sent] + [
            lax.ppermute(sent, "space", [(i, i ^ p) for i in range(n_space)]) for p in partners
        ]
        if r == len(groups) - 1:
            after = lax.ppermute(grads[0], "space", [(i + 1, i) for i in range(n_space - 1)])
            pooled = pl.pallas_call(
                pool_kernel, out_shape=shape(upstream.shape, bf16), compiler_params=params()
            )(acts[0], acts[1])
            input_grad = input_call(True, w, grads[0], grads[1])
        terms = [t.astype(f32) for t in terms]
        while len(terms) > 1:
            terms = [a + b for a, b in zip(terms[::2], terms[1::2])]
        rows = terms[0]
    rows, input_grad, pooled, after = lax.optimization_barrier((rows, input_grad, pooled, after))
    input_grad = input_call(False, w, grads[1], after, input_grad)
    other = lax.ppermute(rows, "space", [(i, i ^ 1) for i in range(n_space)])
    weight_grad = pl.pallas_call(
        join_kernel,
        out_specs=pl.BlockSpec(memory_space=pltpu.HBM),
        out_shape=shape((taps, out_ch), f32),
        scratch_shapes=[pltpu.SemaphoreType.DMA((2,))],
        compiler_params=params(),
    )(rows, other)
    weight_grad = weight_grad.reshape(3, 3, 3, cb, out_ch).transpose(3, 0, 1, 2, 4)
    return pooled, input_grad, weight_grad


def solution(mesh):
    return jax.shard_map(
        on_device,
        mesh=mesh,
        in_specs=(
            P("chan", "space", None, None),
            P("chan", None, None, None, None),
            P("chan", "space", None, None),
        ),
        out_specs=(
            P("chan", "space", None, None),
            P("chan", "space", None, None),
            P("chan", None, None, None, None),
        ),
        check_vma=False,
    )
```

```python
import functools

import jax
import jax.numpy as jnp
from jax import lax
from jax.experimental import pallas as pl
from jax.experimental.pallas import tpu as pltpu
from jax.sharding import PartitionSpec as P

SLOPE = 0.3
VMEM = 24 * 1024 * 1024
XOR = True
RS = (1, 2, 3)
AG = (1, 2, 3)
FEW = 4


def params():
    return pltpu.CompilerParams(vmem_limit_bytes=VMEM)


def pair_matrix(transposed, wid, half):
    shape = (3 * wid, 2 * wid) if transposed else (2 * wid, 3 * wid)
    long, short = (0, 1) if transposed else (1, 0)
    src = lax.broadcasted_iota(jnp.int32, shape, short)
    dst = lax.broadcasted_iota(jnp.int32, shape, long)
    e = (dst >= wid).astype(jnp.int32) + (dst >= 2 * wid).astype(jnp.int32)
    rest = dst - e * wid
    h = (rest >= half).astype(jnp.int32)
    x = 2 * (rest - h * half) + e - 1
    hit = (x >= 0) & (x < wid) & (src == h * wid + x)
    return jnp.where(hit, 1.0, 0.0).astype(jnp.bfloat16)


def load_kernel(vol_hbm, vol_ref, edge_ref, sems):
    planes = vol_ref.shape[1]
    copies = [
        pltpu.make_async_copy(vol_hbm.at[:, p], vol_ref.at[:, p], sems.at[p])
        for p in reversed(range(planes))
    ]
    for copy in copies:
        copy.start()
    copies[0].wait()
    edge_ref[...] = vol_ref[:, planes - 1 :]
    for copy in copies[1:]:
        copy.wait()


def fwd_kernel(n, ob, z, *refs):
    if z:
        vol_ref, w_hbm, w_ref, cols_ref, *rest, sem = refs
        w_copy = pltpu.make_async_copy(w_hbm, w_ref, sem)
        w_copy.start()
    else:
        rim_ref, vol_ref, w_ref, cols_ref, *rest = refs
    part_refs = rest[:-2] if n > 1 else rest[:-1]
    wide_ref = rest[-2] if n > 1 else rest[-1]
    cb, _, hgt, wid = vol_ref.shape
    groups = hgt // 4
    sel = pair_matrix(False, wid, wid // 2)
    zero = jnp.zeros((cb, wid), jnp.float32)
    for a in range(3):
        plane = vol_ref[:, 2 * z + a - 1] if z or a else rim_ref[:, 0]
        wide_ref[...] = plane.astype(jnp.float32).reshape(cb * hgt, wid)
        row = [wide_ref[pl.ds(y, cb, stride=hgt), :] for y in range(hgt)]
        cls = [[row[4 * j + r] for j in range(groups)] for r in range(4)]

        def stack(blocks):
            return jnp.concatenate(blocks, axis=0).astype(jnp.bfloat16)

        back = stack([zero] + cls[3][:-1])
        cls = [stack(c) for c in cls]
        for b, (left, right) in enumerate(((back, cls[1]), (cls[0], cls[2]), (cls[1], cls[3]))):
            taps = jnp.dot(
                jnp.concatenate([left, right], axis=1), sel, preferred_element_type=jnp.float32
            )
            for e in range(3):
                block = taps[:, e * wid : (e + 1) * wid].astype(jnp.bfloat16)
                tap = (a * 3 + b) * 3 + e
                cols_ref[tap * cb : (tap + 1) * cb, :] = jnp.concatenate(
                    [block[j * cb : (j + 1) * cb] for j in range(groups)], axis=1
                )
    if z:
        w_copy.wait()
    if cols_ref.shape[0] > 27 * cb:
        pad = (cols_ref.shape[0] - 27 * cb, cols_ref.shape[1])
        cols_ref[27 * cb :, :] = jnp.zeros(pad, jnp.bfloat16)
    part = lax.dot_general(
        w_ref[...],
        cols_ref[0 : 27 * cb, :],
        (((0,), (0,)), ((), ())),
        preferred_element_type=jnp.float32,
    )
    if n == 1:
        part_refs[0][...] = part
        return
    all_ref = rest[-1]
    all_ref[...] = part
    me = lax.axis_index("chan")
    for k, ref in zip((0,) + RS, part_refs):
        start = pl.multiple_of((me ^ k if XOR else lax.rem(me + k, n)) * ob, ob)
        ref[...] = all_ref[pl.ds(start, ob), :]


def spread_kernel(up_ref, out_ref):
    groups, ob, small = up_ref.shape
    wid = 4 * small
    r = lax.broadcasted_iota(jnp.int32, (small, wid), 0)
    c = lax.broadcasted_iota(jnp.int32, (small, wid), 1)
    c = c - jnp.where(c >= 2 * small, 2 * small, 0)
    grow = jnp.where((c >= 2 * r) & (c <= 2 * r + 1), 1.0, 0.0).astype(jnp.bfloat16)
    for j in range(groups):
        spread = jnp.dot(up_ref[j], grow, preferred_element_type=jnp.float32)
        out_ref[:, j * wid : (j + 1) * wid] = spread * 0.125


def act_kernel(spread_ref, *rest):
    *part_refs, grad_ref, act_ref = rest
    pre = part_refs[0][...]
    for ref in part_refs[1:]:
        pre = pre + ref[...]
    grad = spread_ref[...] * jnp.where(pre > 0, 1.0, SLOPE)
    grad_ref[...] = grad.astype(jnp.bfloat16)
    act_ref[...] = jnp.where(pre > 0, pre, SLOPE * pre)


def pool_planes(one_ref, two_ref, out_ref):
    ob, _, groups, small = out_ref.shape
    wid = 4 * small
    r = lax.broadcasted_iota(jnp.int32, (wid, small), 0)
    c = lax.broadcasted_iota(jnp.int32, (wid, small), 1)
    r = r - jnp.where(r >= 2 * small, 2 * small, 0)
    pool = jnp.where((r >= 2 * c) & (r <= 2 * c + 1), 0.125, 0.0)
    act = one_ref[...] + two_ref[...]
    means = [
        jnp.dot(
            act[:, j * wid : (j + 1) * wid],
            pool,
            precision=lax.Precision.HIGHEST,
            preferred_element_type=jnp.float32,
        )
        for j in range(groups)
    ]
    out_ref[:, 0] = jnp.stack(means, axis=1).astype(jnp.bfloat16)


def in_order(n, block_refs, grad_ref):
    if n == 1:
        grad_ref[...] = block_refs[0][...]
        return
    me = lax.axis_index("chan")
    ob = block_refs[0].shape[0]
    for k, ref in zip((0,) + AG, block_refs):
        start = pl.multiple_of((me ^ k if XOR else lax.rem(me + n - k, n)) * ob, ob)
        grad_ref[pl.ds(start, ob), :] = ref[...]


def weight_term(cols, grad_ref):
    return lax.dot_general(
        cols,
        grad_ref[...],
        (((1,), (1,)), ((), ())),
        preferred_element_type=jnp.float32,
    )


def middle_kernel(n, w_ref, act_one_ref, act_two_ref, cols_ref, *refs):
    *block_refs, wgrad_ref, grad_ref, pooled_ref, out_ref, wide_ref, done_ref, sems = refs
    in_order(n, block_refs, grad_ref)
    copies = input_planes([(2, (grad_ref[...],))], w_ref, out_ref, wide_ref, done_ref, sems)
    wgrad_ref[...] = weight_term(cols_ref[...], grad_ref)
    pool_planes(act_one_ref, act_two_ref, pooled_ref)
    for copy in copies:
        copy.wait()


def send_kernel(n, sum_ref, cols_ref, *refs):
    *block_refs, send_ref, grad_ref = refs
    in_order(n, block_refs, grad_ref)
    half = send_ref.shape[0]
    start = pl.multiple_of((1 - lax.rem(lax.axis_index("space"), 2)) * half, 16)
    send_ref[...] = sum_ref[pl.ds(start, half), :] + weight_term(
        cols_ref[pl.ds(start, half), :], grad_ref
    )


def keep_kernel(sum_ref, cols_ref, grad_ref, keep_ref):
    half = keep_ref.shape[0]
    start = pl.multiple_of(lax.rem(lax.axis_index("space"), 2) * half, 16)
    keep_ref[...] = sum_ref[pl.ds(start, half), :] + weight_term(
        cols_ref[pl.ds(start, half), :], grad_ref
    )


def join_kernel(own_ref, other_ref, out_ref, sems):
    half = own_ref.shape[0]
    for core in range(2):

        @pl.when(lax.rem(lax.axis_index("space"), 2) == core)
        def _():
            copies = []
            for ref, start in ((own_ref, core * half), (other_ref, (1 - core) * half)):
                size = min(half, out_ref.shape[0] - start)
                copies.append(
                    pltpu.make_async_copy(
                        ref.at[pl.ds(0, size)], out_ref.at[pl.ds(start, size)], sems.at[start // half]
                    )
                )
            for copy in copies:
                copy.start()
            for copy in copies:
                copy.wait()


def input_planes(todo, w_ref, out_ref, wide_ref, done_ref, sems):
    cb, _, hgt, wid = out_ref.shape
    half = wid // 2
    groups = hgt // 4
    lanes = groups * wid
    taps = 9 * cb
    spread = pair_matrix(True, wid, half)
    spread = jnp.concatenate([spread, spread], axis=0)
    keep = lax.broadcasted_iota(jnp.int32, (3 * cb, lanes), 1) < lanes - half
    w = [w_ref[a * taps : (a + 1) * taps, :] for a in range(3)]
    behind = jnp.concatenate([w[2], w[0]], axis=1)
    copies = []
    for slot, (i, grads) in enumerate(todo):
        if i % 2 == 0:
            e_all = jnp.dot(w[1], grads[0], preferred_element_type=jnp.float32)
        else:
            e_all = jnp.dot(
                behind, jnp.concatenate(grads, axis=0), preferred_element_type=jnp.float32
            )
        by_b = [e_all[b * 3 * cb : (b + 1) * 3 * cb] for b in range(3)]
        shifted = pltpu.roll(by_b[0], lanes - half, 1)
        rows = (by_b[1], by_b[2] + jnp.where(keep, shifted, 0.0))
        left = []
        for f in rows:
            for j in range(groups):
                t = f[:, j * wid : (j + 1) * wid]
                left.append(
                    jnp.concatenate([t[e * cb : (e + 1) * cb] for e in range(3)], axis=1)
                )
        left = jnp.concatenate(left, axis=0)
        high = left.astype(jnp.bfloat16)
        low = (left - high.astype(jnp.float32)).astype(jnp.bfloat16)
        full = jnp.dot(
            jnp.concatenate([high, low], axis=1), spread, preferred_element_type=jnp.float32
        )
        for par in range(2):
            for j in range(groups):
                for h in range(2):
                    y = 2 * (2 * j + h) + par
                    at = (par * groups + j) * cb
                    wide_ref[pl.ds(y, cb, stride=hgt), :] = full[
                        at : at + cb, h * wid : (h + 1) * wid
                    ]
        done_ref[slot] = wide_ref[...].reshape(cb, hgt, wid).astype(jnp.bfloat16)
        copies.append(pltpu.make_async_copy(done_ref.at[slot], out_ref.at[:, i], sems.at[slot]))
        copies[-1].start()
    return copies


def input_kernel(last, w_ref, one_ref, two_ref, _, out_ref, *scratch):
    one, two = one_ref[...], two_ref[...]
    if last:
        todo = [(out_ref.shape[1] - 1, (one, two))]
    else:
        todo = [(0, (one,)), (1, (one, two))]
    for copy in input_planes(todo, w_ref, out_ref, *scratch):
        copy.wait()


def moved(block, axis, k):
    n = lax.axis_size(axis)
    return lax.ppermute(block, axis, [(i, i ^ k if XOR else (i + k) % n) for i in range(n)])


def on_device(volume, kernel, upstream):
    cb, planes, hgt, wid = volume.shape
    ob = upstream.shape[0]
    out_ch = kernel.shape[4]
    n_chan, n_space = lax.axis_size("chan"), lax.axis_size("space")
    direct = n_chan <= FEW and n_chan & (n_chan - 1) == 0
    n = n_chan if direct else 1
    taps = 27 * cb
    cells = hgt // 4 * wid
    f32, bf16 = jnp.float32, jnp.bfloat16
    shape = jax.ShapeDtypeStruct
    weights = kernel.transpose(1, 2, 3, 0, 4).reshape(taps, out_ch)
    up = upstream[:, 0].transpose(1, 0, 2)
    spread = pl.pallas_call(
        spread_kernel, out_shape=shape((ob, cells), f32), compiler_params=params()
    )(up)

    scratch = [pltpu.VMEM((cb * hgt, wid), f32)]
    if n > 1:
        scratch.append(pltpu.VMEM((out_ch, cells), f32))
    part_shapes = [shape((ob if direct else out_ch, cells), f32)] * n
    out_planes = range(planes // 2)
    cols, grads, acts = {}, {}, {}
    vmem = pl.BlockSpec(memory_space=pltpu.VMEM)
    hbm = pl.BlockSpec(memory_space=pltpu.HBM)

    def from_hbm(x):
        return pltpu.with_memory_space_constraint(x, pltpu.HBM)

    half = -(-taps // 32) * 16
    cols_shape = shape((2 * half, cells), bf16)
    vol, edge = pl.pallas_call(
        load_kernel,
        in_specs=[hbm],
        out_shape=[shape(volume.shape, bf16), shape((cb, 1, hgt, wid), bf16)],
        scratch_shapes=[pltpu.SemaphoreType.DMA((planes,))],
        compiler_params=params(),
    )(from_hbm(volume))
    rim = lax.ppermute(edge, "space", [(i, i + 1) for i in range(n_space - 1)])
    for z in reversed(out_planes):
        call = functools.partial(fwd_kernel, n, ob, z)
        if z:
            w, cols[z], *parts = pl.pallas_call(
                call,
                in_specs=[vmem, hbm],
                out_shape=[shape(weights.shape, bf16), cols_shape] + part_shapes,
                scratch_shapes=scratch + [pltpu.SemaphoreType.DMA],
                compiler_params=params(),
            )(vol, from_hbm(weights))
        else:
            cols[z], *parts = pl.pallas_call(
                call,
                out_shape=[cols_shape] + part_shapes,
                scratch_shapes=scratch,
                compiler_params=params(),
            )(rim, vol, w)
        if direct:
            parts = parts[:1] + [moved(p, "chan", k) for k, p in zip(RS, parts[1:])]
        else:
            parts = [lax.psum_scatter(parts[0], "chan", scatter_dimension=0, tiled=True)]
        own, acts[z] = pl.pallas_call(
            act_kernel,
            out_shape=[shape((ob, cells), bf16), shape((ob, cells), f32)],
            compiler_params=params(),
        )(spread, *parts)
        if direct:
            grads[z] = [own] + [moved(own, "chan", k) for k in AG]
        else:
            grads[z] = [lax.all_gather(own, "chan", axis=0, tiled=True)]

    def input_scratch(count):
        return [
            pltpu.VMEM((cb * hgt, wid), f32),
            pltpu.VMEM((count, cb, hgt, wid), bf16),
            pltpu.SemaphoreType.DMA((count,)),
        ]

    def input_call(last, *operands):
        return pl.pallas_call(
            functools.partial(input_kernel, last),
            in_specs=[vmem] * 3 + [hbm],
            out_specs=hbm,
            out_shape=shape(volume.shape, bf16),
            scratch_shapes=input_scratch(1 if last else 2),
            input_output_aliases={3: 0},
            compiler_params=params(),
        )(*operands)

    grad_shape = shape((out_ch, cells), bf16)
    term, grads[1], pooled, input_grad = pl.pallas_call(
        functools.partial(middle_kernel, n),
        out_specs=[vmem, vmem, vmem, hbm],
        out_shape=[
            shape((2 * half, out_ch), f32),
            grad_shape,
            shape(upstream.shape, bf16),
            shape(volume.shape, bf16),
        ],
        scratch_shapes=input_scratch(1),
        compiler_params=params(),
    )(w, acts[0], acts[1], cols[1], *grads[1])
    send, grads[0] = pl.pallas_call(
        functools.partial(send_kernel, n),
        out_shape=[shape((half, out_ch), f32), grad_shape],
        compiler_params=params(),
    )(term, cols[0], *grads[0])
    keep = pl.pallas_call(
        keep_kernel,
        out_shape=shape((half, out_ch), f32),
        compiler_params=params(),
    )(term, cols[0], grads[0])

    rows = keep + lax.ppermute(send, "space", [(i, i ^ 1) for i in range(n_space)])
    bits = [1 << b for b in range(1, n_space.bit_length() - 1)]
    groups = [bits[i : i + 2] for i in range(0, len(bits), 2)]
    after = None
    for r, group in enumerate(groups):
        sent = rows.astype(bf16)
        if r == len(groups) - 1:
            sent, grads, input_grad = lax.optimization_barrier((sent, grads, input_grad))
        partners = [sum(group[b] * (k >> b & 1) for b in range(len(group))) for k in range(1, 1 << len(group))]
        terms = [sent] + [
            lax.ppermute(sent, "space", [(i, i ^ p) for i in range(n_space)]) for p in partners
        ]
        if r == len(groups) - 1:
            after = lax.ppermute(grads[0], "space", [(i + 1, i) for i in range(n_space - 1)])
            input_grad = input_call(False, w, grads[0], grads[1], input_grad)
        terms = [t.astype(f32) for t in terms]
        while len(terms) > 1:
            terms = [a + b for a, b in zip(terms[::2], terms[1::2])]
        rows = terms[0]
    rows, input_grad, after = lax.optimization_barrier((rows, input_grad, after))
    input_grad = input_call(True, w, grads[1], after, input_grad)
    other = lax.ppermute(rows, "space", [(i, i ^ 1) for i in range(n_space)])
    weight_grad = pl.pallas_call(
        join_kernel,
        out_specs=pl.BlockSpec(memory_space=pltpu.HBM),
        out_shape=shape((taps, out_ch), f32),
        scratch_shapes=[pltpu.SemaphoreType.DMA((2,))],
        compiler_params=params(),
    )(rows, other)
    weight_grad = weight_grad.reshape(3, 3, 3, cb, out_ch).transpose(3, 0, 1, 2, 4)
    return pooled, input_grad, weight_grad


def solution(mesh):
    return jax.shard_map(
        on_device,
        mesh=mesh,
        in_specs=(
            P("chan", "space", None, None),
            P("chan", None, None, None, None),
            P("chan", "space", None, None),
        ),
        out_specs=(
            P("chan", "space", None, None),
            P("chan", "space", None, None),
            P("chan", None, None, None, None),
        ),
        check_vma=False,
    )
```

```python
import functools

import jax
import jax.numpy as jnp
from jax import lax
from jax.experimental import pallas as pl
from jax.experimental.pallas import tpu as pltpu
from jax.sharding import PartitionSpec as P

SLOPE = 0.3
VMEM = 24 * 1024 * 1024
XOR = True
RS = {1: (3, 2, 1), 0: (3, 2, 1)}
AG = {1: (1, 3, 2), 0: (2, 3, 1)}
CHIPS = (0, 1, 2)
FEW = 4


def params():
    return pltpu.CompilerParams(vmem_limit_bytes=VMEM)


def pair_matrix(transposed, wid, half):
    shape = (3 * wid, 2 * wid) if transposed else (2 * wid, 3 * wid)
    long, short = (0, 1) if transposed else (1, 0)
    src = lax.broadcasted_iota(jnp.int32, shape, short)
    dst = lax.broadcasted_iota(jnp.int32, shape, long)
    e = (dst >= wid).astype(jnp.int32) + (dst >= 2 * wid).astype(jnp.int32)
    rest = dst - e * wid
    h = (rest >= half).astype(jnp.int32)
    x = 2 * (rest - h * half) + e - 1
    hit = (x >= 0) & (x < wid) & (src == h * wid + x)
    return jnp.where(hit, 1.0, 0.0).astype(jnp.bfloat16)


def load_kernel(vol_hbm, vol_ref, edge_ref, sems):
    planes = vol_ref.shape[1]
    copies = [
        pltpu.make_async_copy(vol_hbm.at[:, p], vol_ref.at[:, p], sems.at[p])
        for p in reversed(range(planes))
    ]
    for copy in copies:
        copy.start()
    copies[0].wait()
    edge_ref[...] = vol_ref[:, planes - 1 :]
    for copy in copies[1:]:
        copy.wait()


def fwd_kernel(n, ob, z, *refs):
    if z:
        vol_ref, w_ref, cols_ref, *rest = refs
    else:
        rim_ref, vol_ref, w_ref, cols_ref, *rest = refs
    part_refs = rest[:-2] if n > 1 else rest[:-1]
    wide_ref = rest[-2] if n > 1 else rest[-1]
    cb, _, hgt, wid = vol_ref.shape
    groups = hgt // 4
    sel = pair_matrix(False, wid, wid // 2)
    zero = jnp.zeros((cb, wid), jnp.float32)
    for a in range(3):
        plane = vol_ref[:, 2 * z + a - 1] if z or a else rim_ref[:, 0]
        wide_ref[...] = plane.astype(jnp.float32).reshape(cb * hgt, wid)
        row = [wide_ref[pl.ds(y, cb, stride=hgt), :] for y in range(hgt)]
        cls = [[row[4 * j + r] for j in range(groups)] for r in range(4)]

        def stack(blocks):
            return jnp.concatenate(blocks, axis=0).astype(jnp.bfloat16)

        back = stack([zero] + cls[3][:-1])
        cls = [stack(c) for c in cls]
        for b, (left, right) in enumerate(((back, cls[1]), (cls[0], cls[2]), (cls[1], cls[3]))):
            taps = jnp.dot(
                jnp.concatenate([left, right], axis=1), sel, preferred_element_type=jnp.float32
            )
            for e in range(3):
                block = taps[:, e * wid : (e + 1) * wid].astype(jnp.bfloat16)
                tap = (a * 3 + b) * 3 + e
                cols_ref[tap * cb : (tap + 1) * cb, :] = jnp.concatenate(
                    [block[j * cb : (j + 1) * cb] for j in range(groups)], axis=1
                )
    if cols_ref.shape[0] > 27 * cb:
        pad = (cols_ref.shape[0] - 27 * cb, cols_ref.shape[1])
        cols_ref[27 * cb :, :] = jnp.zeros(pad, jnp.bfloat16)
    part = lax.dot_general(
        w_ref[...],
        cols_ref[0 : 27 * cb, :],
        (((0,), (0,)), ((), ())),
        preferred_element_type=jnp.float32,
    )
    if n == 1:
        part_refs[0][...] = part
        return
    all_ref = rest[-1]
    all_ref[...] = part
    me = lax.axis_index("chan")
    for k, ref in zip((0,) + RS[z], part_refs):
        start = pl.multiple_of((me ^ k if XOR else lax.rem(me + k, n)) * ob, ob)
        ref[...] = all_ref[pl.ds(start, ob), :]


def spread_kernel(up_ref, out_ref):
    groups, ob, small = up_ref.shape
    wid = 4 * small
    r = lax.broadcasted_iota(jnp.int32, (small, wid), 0)
    c = lax.broadcasted_iota(jnp.int32, (small, wid), 1)
    c = c - jnp.where(c >= 2 * small, 2 * small, 0)
    grow = jnp.where((c >= 2 * r) & (c <= 2 * r + 1), 1.0, 0.0).astype(jnp.bfloat16)
    for j in range(groups):
        spread = jnp.dot(up_ref[j], grow, preferred_element_type=jnp.float32)
        out_ref[:, j * wid : (j + 1) * wid] = spread * 0.125


def act_kernel(spread_ref, *rest):
    *part_refs, grad_ref, act_ref = rest
    pre = part_refs[0][...]
    for ref in part_refs[1:]:
        pre = pre + ref[...]
    grad = spread_ref[...] * jnp.where(pre > 0, 1.0, SLOPE)
    grad_ref[...] = grad.astype(jnp.bfloat16)
    act_ref[...] = jnp.where(pre > 0, pre, SLOPE * pre)


def pool_planes(one_ref, two_ref, out_ref):
    ob, _, groups, small = out_ref.shape
    wid = 4 * small
    r = lax.broadcasted_iota(jnp.int32, (wid, small), 0)
    c = lax.broadcasted_iota(jnp.int32, (wid, small), 1)
    r = r - jnp.where(r >= 2 * small, 2 * small, 0)
    pool = jnp.where((r >= 2 * c) & (r <= 2 * c + 1), 0.125, 0.0)
    act = one_ref[...] + two_ref[...]
    means = [
        jnp.dot(
            act[:, j * wid : (j + 1) * wid],
            pool,
            precision=lax.Precision.HIGHEST,
            preferred_element_type=jnp.float32,
        )
        for j in range(groups)
    ]
    out_ref[:, 0] = jnp.stack(means, axis=1).astype(jnp.bfloat16)


def in_order(n, z, block_refs, grad_ref):
    if n == 1:
        grad_ref[...] = block_refs[0][...]
        return
    me = lax.axis_index("chan")
    ob = block_refs[0].shape[0]
    for k, ref in zip((0,) + AG[z], block_refs):
        start = pl.multiple_of((me ^ k if XOR else lax.rem(me + n - k, n)) * ob, ob)
        grad_ref[pl.ds(start, ob), :] = ref[...]


def weight_term(cols, grad_ref):
    return lax.dot_general(
        cols,
        grad_ref[...],
        (((1,), (1,)), ((), ())),
        preferred_element_type=jnp.float32,
    )


def middle_kernel(n, w_ref, act_one_ref, act_two_ref, cols_ref, *refs):
    *block_refs, wgrad_ref, grad_ref, pooled_ref, out_ref, wide_ref, done_ref, sems = refs
    in_order(n, 1, block_refs, grad_ref)
    input_planes([(grad_ref[...],)], w_ref, wide_ref, done_ref)
    for copy in plane_copies(done_ref, out_ref, 2, sems):
        copy.start()
    wgrad_ref[...] = weight_term(cols_ref[...], grad_ref)
    pool_planes(act_one_ref, act_two_ref, pooled_ref)
    for copy in plane_copies(done_ref, out_ref, 2, sems):
        copy.wait()


def send_kernel(n, sum_ref, cols_ref, *refs):
    *block_refs, send_ref, grad_ref = refs
    in_order(n, 0, block_refs, grad_ref)
    half = send_ref.shape[0]
    start = pl.multiple_of((1 - lax.rem(lax.axis_index("space"), 2)) * half, 16)
    send_ref[...] = sum_ref[pl.ds(start, half), :] + weight_term(
        cols_ref[pl.ds(start, half), :], grad_ref
    )


def keep_kernel(sum_ref, cols_ref, grad_ref, keep_ref):
    half = keep_ref.shape[0]
    start = pl.multiple_of(lax.rem(lax.axis_index("space"), 2) * half, 16)
    keep_ref[...] = sum_ref[pl.ds(start, half), :] + weight_term(
        cols_ref[pl.ds(start, half), :], grad_ref
    )


def join_kernel(own_ref, other_ref, plane_ref, _, out_ref, input_ref, sems):
    half = own_ref.shape[0]
    for core in range(2):

        @pl.when(lax.rem(lax.axis_index("space"), 2) == core)
        def _():
            copies = plane_copies(plane_ref, input_ref, input_ref.shape[1] - 1, sems)
            for ref, start in ((own_ref, core * half), (other_ref, (1 - core) * half)):
                size = min(half, out_ref.shape[0] - start)
                copies.append(
                    pltpu.make_async_copy(
                        ref.at[pl.ds(0, size)],
                        out_ref.at[pl.ds(start, size)],
                        sems.at[1 + start // half],
                    )
                )
            for copy in copies:
                copy.start()
            for copy in copies:
                copy.wait()


def input_planes(todo, w_ref, wide_ref, done_ref):
    _, cb, hgt, wid = done_ref.shape
    half = wid // 2
    groups = hgt // 4
    lanes = groups * wid
    taps = 9 * cb
    spread = pair_matrix(True, wid, half)
    spread = jnp.concatenate([spread, spread], axis=0)
    keep = lax.broadcasted_iota(jnp.int32, (3 * cb, lanes), 1) < lanes - half
    w = [w_ref[a * taps : (a + 1) * taps, :] for a in range(3)]
    behind = jnp.concatenate([w[2], w[0]], axis=1)
    for slot, grads in enumerate(todo):
        if len(grads) == 1:
            e_all = jnp.dot(w[1], grads[0], preferred_element_type=jnp.float32)
        else:
            e_all = jnp.dot(
                behind, jnp.concatenate(grads, axis=0), preferred_element_type=jnp.float32
            )
        by_b = [e_all[b * 3 * cb : (b + 1) * 3 * cb] for b in range(3)]
        shifted = pltpu.roll(by_b[0], lanes - half, 1)
        rows = (by_b[1], by_b[2] + jnp.where(keep, shifted, 0.0))
        left = []
        for f in rows:
            for j in range(groups):
                t = f[:, j * wid : (j + 1) * wid]
                left.append(
                    jnp.concatenate([t[e * cb : (e + 1) * cb] for e in range(3)], axis=1)
                )
        left = jnp.concatenate(left, axis=0)
        high = left.astype(jnp.bfloat16)
        low = (left - high.astype(jnp.float32)).astype(jnp.bfloat16)
        full = jnp.dot(
            jnp.concatenate([high, low], axis=1), spread, preferred_element_type=jnp.float32
        )
        for par in range(2):
            for j in range(groups):
                for h in range(2):
                    y = 2 * (2 * j + h) + par
                    at = (par * groups + j) * cb
                    wide_ref[pl.ds(y, cb, stride=hgt), :] = full[
                        at : at + cb, h * wid : (h + 1) * wid
                    ]
        done_ref[slot] = wide_ref[...].reshape(cb, hgt, wid).astype(jnp.bfloat16)


def plane_copies(done_ref, out_ref, first, sems):
    return [
        pltpu.make_async_copy(done_ref.at[i], out_ref.at[:, first + i], sems.at[i])
        for i in range(done_ref.shape[0])
    ]


def input_kernel(w_ref, one_ref, two_ref, _, out_ref, wide_ref, done_ref, sems):
    one, two = one_ref[...], two_ref[...]
    input_planes([(one,), (one, two)], w_ref, wide_ref, done_ref)
    for copy in plane_copies(done_ref, out_ref, 0, sems):
        copy.start()
    for copy in plane_copies(done_ref, out_ref, 0, sems):
        copy.wait()


def edge_kernel(w_ref, one_ref, two_ref, done_ref, wide_ref):
    input_planes([(one_ref[...], two_ref[...])], w_ref, wide_ref, done_ref)


def moved(block, axis, k):
    n = lax.axis_size(axis)
    return lax.ppermute(block, axis, [(i, i ^ k if XOR else (i + k) % n) for i in range(n)])


def on_device(volume, kernel, upstream):
    cb, planes, hgt, wid = volume.shape
    ob = upstream.shape[0]
    out_ch = kernel.shape[4]
    n_chan, n_space = lax.axis_size("chan"), lax.axis_size("space")
    direct = n_chan <= FEW and n_chan & (n_chan - 1) == 0
    n = n_chan if direct else 1
    taps = 27 * cb
    cells = hgt // 4 * wid
    f32, bf16 = jnp.float32, jnp.bfloat16
    shape = jax.ShapeDtypeStruct
    weights = kernel.transpose(1, 2, 3, 0, 4).reshape(taps, out_ch)
    up = upstream[:, 0].transpose(1, 0, 2)
    spread = pl.pallas_call(
        spread_kernel, out_shape=shape((ob, cells), f32), compiler_params=params()
    )(up)

    scratch = [pltpu.VMEM((cb * hgt, wid), f32)]
    if n > 1:
        scratch.append(pltpu.VMEM((out_ch, cells), f32))
    part_shapes = [shape((ob if direct else out_ch, cells), f32)] * n
    out_planes = range(planes // 2)
    cols, grads, acts = {}, {}, {}
    vmem = pl.BlockSpec(memory_space=pltpu.VMEM)
    hbm = pl.BlockSpec(memory_space=pltpu.HBM)

    def from_hbm(x):
        return pltpu.with_memory_space_constraint(x, pltpu.HBM)

    half = -(-taps // 32) * 16
    cols_shape = shape((2 * half, cells), bf16)
    vol, edge = pl.pallas_call(
        load_kernel,
        in_specs=[hbm],
        out_shape=[shape(volume.shape, bf16), shape((cb, 1, hgt, wid), bf16)],
        scratch_shapes=[pltpu.SemaphoreType.DMA((planes,))],
        compiler_params=params(),
    )(from_hbm(volume))
    rim = lax.ppermute(edge, "space", [(i, i + 1) for i in range(n_space - 1)])
    for z in reversed(out_planes):
        cols[z], *parts = pl.pallas_call(
            functools.partial(fwd_kernel, n, ob, z),
            out_shape=[cols_shape] + part_shapes,
            scratch_shapes=scratch,
            compiler_params=params(),
        )(*(() if z else (rim,)), vol, weights)
        if direct:
            parts = parts[:1] + [moved(p, "chan", k) for k, p in zip(RS[z], parts[1:])]
        else:
            parts = [lax.psum_scatter(parts[0], "chan", scatter_dimension=0, tiled=True)]
        own, acts[z] = pl.pallas_call(
            act_kernel,
            out_shape=[shape((ob, cells), bf16), shape((ob, cells), f32)],
            compiler_params=params(),
        )(spread, *parts)
        if direct:
            grads[z] = [own] + [moved(own, "chan", k) for k in AG[z]]
        else:
            grads[z] = [lax.all_gather(own, "chan", axis=0, tiled=True)]

    wide, plane = pltpu.VMEM((cb * hgt, wid), f32), (cb, hgt, wid)
    grad_shape = shape((out_ch, cells), bf16)
    term, grads[1], pooled, input_grad = pl.pallas_call(
        functools.partial(middle_kernel, n),
        out_specs=[vmem, vmem, vmem, hbm],
        out_shape=[
            shape((2 * half, out_ch), f32),
            grad_shape,
            shape(upstream.shape, bf16),
            shape(volume.shape, bf16),
        ],
        scratch_shapes=[wide, pltpu.VMEM((1,) + plane, bf16), pltpu.SemaphoreType.DMA((1,))],
        compiler_params=params(),
    )(weights, acts[0], acts[1], cols[1], *grads[1])
    send, grads[0] = pl.pallas_call(
        functools.partial(send_kernel, n),
        out_shape=[shape((half, out_ch), f32), grad_shape],
        compiler_params=params(),
    )(term, cols[0], *grads[0])
    keep = pl.pallas_call(
        keep_kernel,
        out_shape=shape((half, out_ch), f32),
        compiler_params=params(),
    )(term, cols[0], grads[0])

    rows = keep + lax.ppermute(send, "space", [(i, i ^ 1) for i in range(n_space)])
    bits = [1 << b for b in range(1, n_space.bit_length() - 1)]
    groups = [bits[i : i + 2] for i in range(0, len(bits), 2)]
    after = None
    for r, group in enumerate(groups):
        sent = rows.astype(bf16)
        if r == len(groups) - 1:
            sent, grads, input_grad = lax.optimization_barrier((sent, grads, input_grad))
        partners = [sum(group[b] * (k >> b & 1) for b in range(len(group))) for k in range(1, 1 << len(group))]
        terms = [sent] + [None] * len(partners)
        for k in CHIPS:
            if k < len(partners):
                terms[k + 1] = lax.ppermute(
                    sent, "space", [(i, i ^ partners[k]) for i in range(n_space)]
                )
        if r == len(groups) - 1:
            after = lax.ppermute(grads[0], "space", [(i + 1, i) for i in range(n_space - 1)])
            input_grad = pl.pallas_call(
                input_kernel,
                in_specs=[vmem] * 3 + [hbm],
                out_specs=hbm,
                out_shape=shape(volume.shape, bf16),
                scratch_shapes=[wide, pltpu.VMEM((2,) + plane, bf16), pltpu.SemaphoreType.DMA((2,))],
                input_output_aliases={3: 0},
                compiler_params=params(),
            )(weights, grads[0], grads[1], input_grad)
        terms = [t.astype(f32) for t in terms]
        while len(terms) > 1:
            terms = [a + b for a, b in zip(terms[::2], terms[1::2])]
        rows = terms[0]
    rows, input_grad, after = lax.optimization_barrier((rows, input_grad, after))
    edge = pl.pallas_call(
        edge_kernel,
        out_shape=shape((1,) + plane, bf16),
        scratch_shapes=[wide],
        compiler_params=params(),
    )(weights, grads[1], after)
    other = lax.ppermute(rows, "space", [(i, i ^ 1) for i in range(n_space)])
    weight_grad, input_grad = pl.pallas_call(
        join_kernel,
        in_specs=[vmem] * 3 + [hbm],
        out_specs=[hbm] * 2,
        out_shape=[shape((taps, out_ch), f32), shape(volume.shape, bf16)],
        scratch_shapes=[pltpu.SemaphoreType.DMA((3,))],
        input_output_aliases={3: 1},
        compiler_params=params(),
    )(rows, other, edge, input_grad)
    weight_grad = weight_grad.reshape(3, 3, 3, cb, out_ch).transpose(3, 0, 1, 2, 4)
    return pooled, input_grad, weight_grad


def solution(mesh):
    return jax.shard_map(
        on_device,
        mesh=mesh,
        in_specs=(
            P("chan", "space", None, None),
            P("chan", None, None, None, None),
            P("chan", "space", None, None),
        ),
        out_specs=(
            P("chan", "space", None, None),
            P("chan", "space", None, None),
            P("chan", None, None, None, None),
        ),
        check_vma=False,
    )
```

```python
import functools

import jax
import jax.numpy as jnp
from jax import lax
from jax.experimental import pallas as pl
from jax.experimental.pallas import tpu as pltpu
from jax.sharding import PartitionSpec as P

SLOPE = 0.3
VMEM = 24 * 1024 * 1024
XOR = True
RS = {1: (3, 2, 1), 0: (3, 2, 1)}
AG = {1: (1, 3, 2), 0: (2, 3, 1)}
CHIPS = (0, 1, 2)
FEW = 4


def params():
    return pltpu.CompilerParams(vmem_limit_bytes=VMEM)


def pair_matrix(transposed, wid, half):
    shape = (3 * wid, 2 * wid) if transposed else (2 * wid, 3 * wid)
    long, short = (0, 1) if transposed else (1, 0)
    src = lax.broadcasted_iota(jnp.int32, shape, short)
    dst = lax.broadcasted_iota(jnp.int32, shape, long)
    e = (dst >= wid).astype(jnp.int32) + (dst >= 2 * wid).astype(jnp.int32)
    rest = dst - e * wid
    h = (rest >= half).astype(jnp.int32)
    x = 2 * (rest - h * half) + e - 1
    hit = (x >= 0) & (x < wid) & (src == h * wid + x)
    return jnp.where(hit, 1.0, 0.0).astype(jnp.bfloat16)


def load_kernel(vol_hbm, vol_ref, edge_ref, sems):
    planes = vol_ref.shape[1]
    copies = [
        pltpu.make_async_copy(vol_hbm.at[:, p], vol_ref.at[:, p], sems.at[p])
        for p in reversed(range(planes))
    ]
    for copy in copies:
        copy.start()
    copies[0].wait()
    edge_ref[...] = vol_ref[:, planes - 1 :]
    for copy in copies[1:]:
        copy.wait()


def fwd_kernel(n, ob, z, *refs):
    if z:
        vol_ref, w_ref, cols_ref, *rest = refs
    else:
        rim_ref, vol_ref, w_ref, cols_ref, *rest = refs
    part_refs = rest[:-2] if n > 1 else rest[:-1]
    wide_ref = rest[-2] if n > 1 else rest[-1]
    cb, _, hgt, wid = vol_ref.shape
    groups = hgt // 4
    sel = pair_matrix(False, wid, wid // 2)
    zero = jnp.zeros((cb, wid), jnp.float32)
    for a in range(3):
        plane = vol_ref[:, 2 * z + a - 1] if z or a else rim_ref[:, 0]
        plane = plane.astype(jnp.float32).reshape(cb * hgt, wid)
        if not (z or a):
            plane = jnp.where(lax.axis_index("space") == 0, 0.0, plane)
        wide_ref[...] = plane
        row = [wide_ref[pl.ds(y, cb, stride=hgt), :] for y in range(hgt)]
        cls = [[row[4 * j + r] for j in range(groups)] for r in range(4)]

        def stack(blocks):
            return jnp.concatenate(blocks, axis=0).astype(jnp.bfloat16)

        back = stack([zero] + cls[3][:-1])
        cls = [stack(c) for c in cls]
        for b, (left, right) in enumerate(((back, cls[1]), (cls[0], cls[2]), (cls[1], cls[3]))):
            taps = jnp.dot(
                jnp.concatenate([left, right], axis=1), sel, preferred_element_type=jnp.float32
            )
            for e in range(3):
                block = taps[:, e * wid : (e + 1) * wid].astype(jnp.bfloat16)
                tap = (a * 3 + b) * 3 + e
                cols_ref[tap * cb : (tap + 1) * cb, :] = jnp.concatenate(
                    [block[j * cb : (j + 1) * cb] for j in range(groups)], axis=1
                )
    if cols_ref.shape[0] > 27 * cb:
        pad = (cols_ref.shape[0] - 27 * cb, cols_ref.shape[1])
        cols_ref[27 * cb :, :] = jnp.zeros(pad, jnp.bfloat16)
    part = lax.dot_general(
        w_ref[...],
        cols_ref[0 : 27 * cb, :],
        (((0,), (0,)), ((), ())),
        preferred_element_type=jnp.float32,
    )
    if n == 1:
        part_refs[0][...] = part
        return
    all_ref = rest[-1]
    all_ref[...] = part
    me = lax.axis_index("chan")
    for k, ref in zip((0,) + RS[z], part_refs):
        start = pl.multiple_of((me ^ k if XOR else lax.rem(me + k, n)) * ob, ob)
        ref[...] = all_ref[pl.ds(start, ob), :]


def spread_kernel(up_ref, out_ref):
    groups, ob, small = up_ref.shape
    wid = 4 * small
    r = lax.broadcasted_iota(jnp.int32, (small, wid), 0)
    c = lax.broadcasted_iota(jnp.int32, (small, wid), 1)
    c = c - jnp.where(c >= 2 * small, 2 * small, 0)
    grow = jnp.where((c >= 2 * r) & (c <= 2 * r + 1), 1.0, 0.0).astype(jnp.bfloat16)
    for j in range(groups):
        spread = jnp.dot(up_ref[j], grow, preferred_element_type=jnp.float32)
        out_ref[:, j * wid : (j + 1) * wid] = spread * 0.125


def act_kernel(spread_ref, *rest):
    *part_refs, grad_ref, act_ref = rest
    pre = part_refs[0][...]
    for ref in part_refs[1:]:
        pre = pre + ref[...]
    grad = spread_ref[...] * jnp.where(pre > 0, 1.0, SLOPE)
    grad_ref[...] = grad.astype(jnp.bfloat16)
    act_ref[...] = jnp.where(pre > 0, pre, SLOPE * pre)


def pool_planes(one_ref, two_ref, out_ref):
    ob, _, groups, small = out_ref.shape
    wid = 4 * small
    r = lax.broadcasted_iota(jnp.int32, (wid, small), 0)
    c = lax.broadcasted_iota(jnp.int32, (wid, small), 1)
    r = r - jnp.where(r >= 2 * small, 2 * small, 0)
    pool = jnp.where((r >= 2 * c) & (r <= 2 * c + 1), 0.125, 0.0)
    act = one_ref[...] + two_ref[...]
    means = [
        jnp.dot(
            act[:, j * wid : (j + 1) * wid],
            pool,
            precision=lax.Precision.HIGHEST,
            preferred_element_type=jnp.float32,
        )
        for j in range(groups)
    ]
    out_ref[:, 0] = jnp.stack(means, axis=1).astype(jnp.bfloat16)


def in_order(n, z, block_refs, grad_ref):
    if n == 1:
        grad_ref[...] = block_refs[0][...]
        return
    me = lax.axis_index("chan")
    ob = block_refs[0].shape[0]
    for k, ref in zip((0,) + AG[z], block_refs):
        start = pl.multiple_of((me ^ k if XOR else lax.rem(me + n - k, n)) * ob, ob)
        grad_ref[pl.ds(start, ob), :] = ref[...]


def weight_term(cols, grad_ref):
    return lax.dot_general(
        cols,
        grad_ref[...],
        (((1,), (1,)), ((), ())),
        preferred_element_type=jnp.float32,
    )


def middle_kernel(n, w_ref, act_one_ref, act_two_ref, cols_ref, *refs):
    *block_refs, wgrad_ref, grad_ref, pooled_ref, out_ref, wide_ref, done_ref, sems = refs
    in_order(n, 1, block_refs, grad_ref)
    input_planes([(grad_ref[...],)], w_ref, wide_ref, done_ref)
    for copy in plane_copies(done_ref, out_ref, 2, sems):
        copy.start()
    wgrad_ref[...] = weight_term(cols_ref[...], grad_ref)
    pool_planes(act_one_ref, act_two_ref, pooled_ref)
    for copy in plane_copies(done_ref, out_ref, 2, sems):
        copy.wait()


def send_kernel(n, sum_ref, cols_ref, *refs):
    *block_refs, send_ref, grad_ref = refs
    in_order(n, 0, block_refs, grad_ref)
    half = send_ref.shape[0]
    start = pl.multiple_of((1 - lax.rem(lax.axis_index("space"), 2)) * half, 16)
    send_ref[...] = sum_ref[pl.ds(start, half), :] + weight_term(
        cols_ref[pl.ds(start, half), :], grad_ref
    )


def keep_kernel(sum_ref, cols_ref, grad_ref, keep_ref):
    half = keep_ref.shape[0]
    start = pl.multiple_of(lax.rem(lax.axis_index("space"), 2) * half, 16)
    keep_ref[...] = sum_ref[pl.ds(start, half), :] + weight_term(
        cols_ref[pl.ds(start, half), :], grad_ref
    )


def join_kernel(own_ref, other_ref, plane_ref, _, out_ref, input_ref, sems):
    half = own_ref.shape[0]
    for core in range(2):

        @pl.when(lax.rem(lax.axis_index("space"), 2) == core)
        def _():
            copies = plane_copies(plane_ref, input_ref, input_ref.shape[1] - 1, sems)
            for ref, start in ((own_ref, core * half), (other_ref, (1 - core) * half)):
                size = min(half, out_ref.shape[0] - start)
                copies.append(
                    pltpu.make_async_copy(
                        ref.at[pl.ds(0, size)],
                        out_ref.at[pl.ds(start, size)],
                        sems.at[1 + start // half],
                    )
                )
            for copy in copies:
                copy.start()
            for copy in copies:
                copy.wait()


def input_planes(todo, w_ref, wide_ref, done_ref):
    _, cb, hgt, wid = done_ref.shape
    half = wid // 2
    groups = hgt // 4
    lanes = groups * wid
    taps = 9 * cb
    spread = pair_matrix(True, wid, half)
    spread = jnp.concatenate([spread, spread], axis=0)
    keep = lax.broadcasted_iota(jnp.int32, (3 * cb, lanes), 1) < lanes - half
    w = [w_ref[a * taps : (a + 1) * taps, :] for a in range(3)]
    behind = jnp.concatenate([w[2], w[0]], axis=1)
    for slot, grads in enumerate(todo):
        if len(grads) == 1:
            e_all = jnp.dot(w[1], grads[0], preferred_element_type=jnp.float32)
        else:
            e_all = jnp.dot(
                behind, jnp.concatenate(grads, axis=0), preferred_element_type=jnp.float32
            )
        by_b = [e_all[b * 3 * cb : (b + 1) * 3 * cb] for b in range(3)]
        shifted = pltpu.roll(by_b[0], lanes - half, 1)
        rows = (by_b[1], by_b[2] + jnp.where(keep, shifted, 0.0))
        left = []
        for f in rows:
            for j in range(groups):
                t = f[:, j * wid : (j + 1) * wid]
                left.append(
                    jnp.concatenate([t[e * cb : (e + 1) * cb] for e in range(3)], axis=1)
                )
        left = jnp.concatenate(left, axis=0)
        high = left.astype(jnp.bfloat16)
        low = (left - high.astype(jnp.float32)).astype(jnp.bfloat16)
        full = jnp.dot(
            jnp.concatenate([high, low], axis=1), spread, preferred_element_type=jnp.float32
        )
        for par in range(2):
            for j in range(groups):
                for h in range(2):
                    y = 2 * (2 * j + h) + par
                    at = (par * groups + j) * cb
                    wide_ref[pl.ds(y, cb, stride=hgt), :] = full[
                        at : at + cb, h * wid : (h + 1) * wid
                    ]
        done_ref[slot] = wide_ref[...].reshape(cb, hgt, wid).astype(jnp.bfloat16)


def plane_copies(done_ref, out_ref, first, sems):
    return [
        pltpu.make_async_copy(done_ref.at[i], out_ref.at[:, first + i], sems.at[i])
        for i in range(done_ref.shape[0])
    ]


def input_kernel(w_ref, one_ref, two_ref, _, out_ref, wide_ref, done_ref, sems):
    one, two = one_ref[...], two_ref[...]
    input_planes([(one,), (one, two)], w_ref, wide_ref, done_ref)
    for copy in plane_copies(done_ref, out_ref, 0, sems):
        copy.start()
    for copy in plane_copies(done_ref, out_ref, 0, sems):
        copy.wait()


def edge_kernel(w_ref, one_ref, two_ref, done_ref, wide_ref):
    two = two_ref[...]
    inside = lax.axis_index("space") < lax.axis_size("space") - 1
    two = jnp.where(inside, two.astype(jnp.float32), 0.0).astype(jnp.bfloat16)
    input_planes([(one_ref[...], two)], w_ref, wide_ref, done_ref)


def moved(block, axis, k):
    n = lax.axis_size(axis)
    return lax.ppermute(block, axis, [(i, i ^ k if XOR else (i + k) % n) for i in range(n)])


def on_device(volume, kernel, upstream):
    cb, planes, hgt, wid = volume.shape
    ob = upstream.shape[0]
    out_ch = kernel.shape[4]
    n_chan, n_space = lax.axis_size("chan"), lax.axis_size("space")
    direct = n_chan <= FEW and n_chan & (n_chan - 1) == 0
    n = n_chan if direct else 1
    taps = 27 * cb
    cells = hgt // 4 * wid
    f32, bf16 = jnp.float32, jnp.bfloat16
    shape = jax.ShapeDtypeStruct
    weights = kernel.transpose(1, 2, 3, 0, 4).reshape(taps, out_ch)
    up = upstream[:, 0].transpose(1, 0, 2)
    spread = pl.pallas_call(
        spread_kernel, out_shape=shape((ob, cells), f32), compiler_params=params()
    )(up)

    scratch = [pltpu.VMEM((cb * hgt, wid), f32)]
    if n > 1:
        scratch.append(pltpu.VMEM((out_ch, cells), f32))
    part_shapes = [shape((ob if direct else out_ch, cells), f32)] * n
    out_planes = range(planes // 2)
    cols, grads, acts = {}, {}, {}
    vmem = pl.BlockSpec(memory_space=pltpu.VMEM)
    hbm = pl.BlockSpec(memory_space=pltpu.HBM)

    def from_hbm(x):
        return pltpu.with_memory_space_constraint(x, pltpu.HBM)

    half = -(-taps // 32) * 16
    cols_shape = shape((2 * half, cells), bf16)
    vol, edge = pl.pallas_call(
        load_kernel,
        in_specs=[hbm],
        out_shape=[shape(volume.shape, bf16), shape((cb, 1, hgt, wid), bf16)],
        scratch_shapes=[pltpu.SemaphoreType.DMA((planes,))],
        compiler_params=params(),
    )(from_hbm(volume))
    rim = lax.ppermute(edge, "space", [(i, (i + 1) % n_space) for i in range(n_space)])
    for z in reversed(out_planes):
        cols[z], *parts = pl.pallas_call(
            functools.partial(fwd_kernel, n, ob, z),
            out_shape=[cols_shape] + part_shapes,
            scratch_shapes=scratch,
            compiler_params=params(),
        )(*(() if z else (rim,)), vol, weights)
        if direct:
            parts = parts[:1] + [moved(p, "chan", k) for k, p in zip(RS[z], parts[1:])]
        else:
            parts = [lax.psum_scatter(parts[0], "chan", scatter_dimension=0, tiled=True)]
        own, acts[z] = pl.pallas_call(
            act_kernel,
            out_shape=[shape((ob, cells), bf16), shape((ob, cells), f32)],
            compiler_params=params(),
        )(spread, *parts)
        if direct:
            grads[z] = [own] + [moved(own, "chan", k) for k in AG[z]]
        else:
            grads[z] = [lax.all_gather(own, "chan", axis=0, tiled=True)]

    wide, plane = pltpu.VMEM((cb * hgt, wid), f32), (cb, hgt, wid)
    grad_shape = shape((out_ch, cells), bf16)
    term, grads[1], pooled, input_grad = pl.pallas_call(
        functools.partial(middle_kernel, n),
        out_specs=[vmem, vmem, vmem, hbm],
        out_shape=[
            shape((2 * half, out_ch), f32),
            grad_shape,
            shape(upstream.shape, bf16),
            shape(volume.shape, bf16),
        ],
        scratch_shapes=[wide, pltpu.VMEM((1,) + plane, bf16), pltpu.SemaphoreType.DMA((1,))],
        compiler_params=params(),
    )(weights, acts[0], acts[1], cols[1], *grads[1])
    send, grads[0] = pl.pallas_call(
        functools.partial(send_kernel, n),
        out_shape=[shape((half, out_ch), f32), grad_shape],
        compiler_params=params(),
    )(term, cols[0], *grads[0])
    keep = pl.pallas_call(
        keep_kernel,
        out_shape=shape((half, out_ch), f32),
        compiler_params=params(),
    )(term, cols[0], grads[0])

    rows = keep + lax.ppermute(send, "space", [(i, i ^ 1) for i in range(n_space)])
    bits = [1 << b for b in range(1, n_space.bit_length() - 1)]
    groups = [bits[i : i + 2] for i in range(0, len(bits), 2)]
    after = None
    for r, group in enumerate(groups):
        sent = rows.astype(bf16)
        if r == len(groups) - 1:
            sent, grads, input_grad = lax.optimization_barrier((sent, grads, input_grad))
        partners = [sum(group[b] * (k >> b & 1) for b in range(len(group))) for k in range(1, 1 << len(group))]
        terms = [sent] + [None] * len(partners)
        for k in CHIPS:
            if k < len(partners):
                terms[k + 1] = lax.ppermute(
                    sent, "space", [(i, i ^ partners[k]) for i in range(n_space)]
                )
        if r == len(groups) - 1:
            after = lax.ppermute(grads[0], "space", [((i + 1) % n_space, i) for i in range(n_space)])
            input_grad = pl.pallas_call(
                input_kernel,
                in_specs=[vmem] * 3 + [hbm],
                out_specs=hbm,
                out_shape=shape(volume.shape, bf16),
                scratch_shapes=[wide, pltpu.VMEM((2,) + plane, bf16), pltpu.SemaphoreType.DMA((2,))],
                input_output_aliases={3: 0},
                compiler_params=params(),
            )(weights, grads[0], grads[1], input_grad)
        terms = [t.astype(f32) for t in terms]
        while len(terms) > 1:
            terms = [a + b for a, b in zip(terms[::2], terms[1::2])]
        rows = terms[0]
    rows, input_grad, after = lax.optimization_barrier((rows, input_grad, after))
    edge = pl.pallas_call(
        edge_kernel,
        out_shape=shape((1,) + plane, bf16),
        scratch_shapes=[wide],
        compiler_params=params(),
    )(weights, grads[1], after)
    other = lax.ppermute(rows, "space", [(i, i ^ 1) for i in range(n_space)])
    weight_grad, input_grad = pl.pallas_call(
        join_kernel,
        in_specs=[vmem] * 3 + [hbm],
        out_specs=[hbm] * 2,
        out_shape=[shape((taps, out_ch), f32), shape(volume.shape, bf16)],
        scratch_shapes=[pltpu.SemaphoreType.DMA((3,))],
        input_output_aliases={3: 1},
        compiler_params=params(),
    )(rows, other, edge, input_grad)
    weight_grad = weight_grad.reshape(3, 3, 3, cb, out_ch).transpose(3, 0, 1, 2, 4)
    return pooled, input_grad, weight_grad


def solution(mesh):
    return jax.shard_map(
        on_device,
        mesh=mesh,
        in_specs=(
            P("chan", "space", None, None),
            P("chan", None, None, None, None),
            P("chan", "space", None, None),
        ),
        out_specs=(
            P("chan", "space", None, None),
            P("chan", "space", None, None),
            P("chan", None, None, None, None),
        ),
        check_vma=False,
    )
```

```python
import functools

import jax
import jax.numpy as jnp
from jax import lax
from jax.experimental import pallas as pl
from jax.experimental.pallas import tpu as pltpu
from jax.sharding import PartitionSpec as P

SLOPE = 0.3
VMEM = 24 * 1024 * 1024
XOR = True
RS = {1: (3, 2, 1), 0: (3, 2, 1)}
AG = {1: (1, 3, 2), 0: (2, 3, 1)}
CHIPS = (0, 1, 2)
FEW = 4


def params():
    return pltpu.CompilerParams(vmem_limit_bytes=VMEM)


def pair_matrix(transposed, wid, half):
    shape = (3 * wid, 2 * wid) if transposed else (2 * wid, 3 * wid)
    long, short = (0, 1) if transposed else (1, 0)
    src = lax.broadcasted_iota(jnp.int32, shape, short)
    dst = lax.broadcasted_iota(jnp.int32, shape, long)
    e = (dst >= wid).astype(jnp.int32) + (dst >= 2 * wid).astype(jnp.int32)
    rest = dst - e * wid
    h = (rest >= half).astype(jnp.int32)
    x = 2 * (rest - h * half) + e - 1
    hit = (x >= 0) & (x < wid) & (src == h * wid + x)
    return jnp.where(hit, 1.0, 0.0).astype(jnp.bfloat16)


def load_kernel(vol_hbm, vol_ref, edge_ref, sems):
    cb, planes = vol_ref.shape[:2]
    pieces = sems.shape[0]
    size = cb // pieces
    copies = [
        pltpu.make_async_copy(
            vol_hbm.at[pl.ds(i * size, size)], vol_ref.at[pl.ds(i * size, size)], sems.at[i]
        )
        for i in range(pieces)
    ]
    for copy in copies:
        copy.start()
    for copy in copies:
        copy.wait()
    edge_ref[...] = vol_ref[:, planes - 1 :]


def fwd_kernel(n, ob, z, *refs):
    if z:
        vol_ref, w_ref, cols_ref, *rest = refs
    else:
        rim_ref, vol_ref, w_ref, cols_ref, *rest = refs
    part_refs = rest[:-2] if n > 1 else rest[:-1]
    wide_ref = rest[-2] if n > 1 else rest[-1]
    cb, _, hgt, wid = vol_ref.shape
    groups = hgt // 4
    sel = pair_matrix(False, wid, wid // 2)
    zero = jnp.zeros((cb, wid), jnp.float32)
    left, right = [], []
    for a in range(3):
        plane = vol_ref[:, 2 * z + a - 1] if z or a else rim_ref[:, 0]
        plane = plane.astype(jnp.float32).reshape(cb * hgt, wid)
        if not (z or a):
            plane = jnp.where(lax.axis_index("space") == 0, 0.0, plane)
        wide_ref[a * cb * hgt : (a + 1) * cb * hgt, :] = plane
        row = [wide_ref[pl.ds(a * cb * hgt + y, cb, stride=hgt), :] for y in range(hgt)]
        cls = [[row[4 * j + r] for j in range(groups)] for r in range(4)]

        def stack(blocks):
            return jnp.concatenate(blocks, axis=0).astype(jnp.bfloat16)

        back = stack([zero] + cls[3][:-1])
        cls = [stack(c) for c in cls]
        left += [back, cls[0], cls[1]]
        right += [cls[1], cls[2], cls[3]]
    taps = jnp.dot(
        jnp.concatenate([jnp.concatenate(left, axis=0), jnp.concatenate(right, axis=0)], axis=1),
        sel,
        preferred_element_type=jnp.float32,
    ).astype(jnp.bfloat16)
    for ab in range(9):
        for e in range(3):
            tap = ab * 3 + e
            cols_ref[tap * cb : (tap + 1) * cb, :] = jnp.concatenate(
                [
                    taps[(ab * groups + j) * cb : (ab * groups + j + 1) * cb, e * wid : (e + 1) * wid]
                    for j in range(groups)
                ],
                axis=1,
            )
    if cols_ref.shape[0] > 27 * cb:
        pad = (cols_ref.shape[0] - 27 * cb, cols_ref.shape[1])
        cols_ref[27 * cb :, :] = jnp.zeros(pad, jnp.bfloat16)
    part = lax.dot_general(
        w_ref[...],
        cols_ref[0 : 27 * cb, :],
        (((0,), (0,)), ((), ())),
        preferred_element_type=jnp.float32,
    )
    if n == 1:
        part_refs[0][...] = part
        return
    all_ref = rest[-1]
    all_ref[...] = part
    me = lax.axis_index("chan")
    for k, ref in zip((0,) + RS[z], part_refs):
        start = pl.multiple_of((me ^ k if XOR else lax.rem(me + k, n)) * ob, ob)
        ref[...] = all_ref[pl.ds(start, ob), :]


def spread_kernel(up_ref, out_ref):
    groups, ob, small = up_ref.shape
    wid = 4 * small
    r = lax.broadcasted_iota(jnp.int32, (small, wid), 0)
    c = lax.broadcasted_iota(jnp.int32, (small, wid), 1)
    c = c - jnp.where(c >= 2 * small, 2 * small, 0)
    grow = jnp.where((c >= 2 * r) & (c <= 2 * r + 1), 1.0, 0.0).astype(jnp.bfloat16)
    for j in range(groups):
        spread = jnp.dot(up_ref[j], grow, preferred_element_type=jnp.float32)
        out_ref[:, j * wid : (j + 1) * wid] = spread * 0.125


def act_kernel(spread_ref, *rest):
    *part_refs, grad_ref, act_ref = rest
    pre = part_refs[0][...]
    for ref in part_refs[1:]:
        pre = pre + ref[...]
    grad = spread_ref[...] * jnp.where(pre > 0, 1.0, SLOPE)
    grad_ref[...] = grad.astype(jnp.bfloat16)
    act_ref[...] = jnp.where(pre > 0, pre, SLOPE * pre)


def pool_planes(one_ref, two_ref, out_ref):
    ob, _, groups, small = out_ref.shape
    wid = 4 * small
    r = lax.broadcasted_iota(jnp.int32, (wid, small), 0)
    c = lax.broadcasted_iota(jnp.int32, (wid, small), 1)
    r = r - jnp.where(r >= 2 * small, 2 * small, 0)
    pool = jnp.where((r >= 2 * c) & (r <= 2 * c + 1), 0.125, 0.0)
    act = one_ref[...] + two_ref[...]
    means = [
        jnp.dot(
            act[:, j * wid : (j + 1) * wid],
            pool,
            precision=lax.Precision.HIGHEST,
            preferred_element_type=jnp.float32,
        )
        for j in range(groups)
    ]
    out_ref[:, 0] = jnp.stack(means, axis=1).astype(jnp.bfloat16)


def in_order(n, z, block_refs, grad_ref):
    if n == 1:
        grad_ref[...] = block_refs[0][...]
        return
    me = lax.axis_index("chan")
    ob = block_refs[0].shape[0]
    for k, ref in zip((0,) + AG[z], block_refs):
        start = pl.multiple_of((me ^ k if XOR else lax.rem(me + n - k, n)) * ob, ob)
        grad_ref[pl.ds(start, ob), :] = ref[...]


def weight_term(cols, grad_ref):
    return lax.dot_general(
        cols,
        grad_ref[...],
        (((1,), (1,)), ((), ())),
        preferred_element_type=jnp.float32,
    )


def middle_kernel(n, w_ref, act_one_ref, act_two_ref, cols_ref, *refs):
    *block_refs, wgrad_ref, grad_ref, pooled_ref, out_ref, wide_ref, done_ref, sems = refs
    in_order(n, 1, block_refs, grad_ref)
    input_planes([(grad_ref[...],)], w_ref, wide_ref, done_ref)
    for copy in plane_copies(done_ref, out_ref, 2, sems):
        copy.start()
    wgrad_ref[...] = weight_term(cols_ref[...], grad_ref)
    pool_planes(act_one_ref, act_two_ref, pooled_ref)
    for copy in plane_copies(done_ref, out_ref, 2, sems):
        copy.wait()


def send_kernel(n, sum_ref, cols_ref, *refs):
    *block_refs, send_ref, grad_ref = refs
    in_order(n, 0, block_refs, grad_ref)
    half = send_ref.shape[0]
    start = pl.multiple_of((1 - lax.rem(lax.axis_index("space"), 2)) * half, 16)
    send_ref[...] = sum_ref[pl.ds(start, half), :] + weight_term(
        cols_ref[pl.ds(start, half), :], grad_ref
    )


def keep_kernel(sum_ref, cols_ref, grad_ref, keep_ref):
    half = keep_ref.shape[0]
    start = pl.multiple_of(lax.rem(lax.axis_index("space"), 2) * half, 16)
    keep_ref[...] = sum_ref[pl.ds(start, half), :] + weight_term(
        cols_ref[pl.ds(start, half), :], grad_ref
    )


def join_kernel(own_ref, other_ref, plane_ref, _, out_ref, input_ref, sems):
    half = own_ref.shape[0]
    for core in range(2):

        @pl.when(lax.rem(lax.axis_index("space"), 2) == core)
        def _():
            copies = plane_copies(plane_ref, input_ref, input_ref.shape[1] - 1, sems)
            for ref, start in ((own_ref, core * half), (other_ref, (1 - core) * half)):
                size = min(half, out_ref.shape[0] - start)
                copies.append(
                    pltpu.make_async_copy(
                        ref.at[pl.ds(0, size)],
                        out_ref.at[pl.ds(start, size)],
                        sems.at[1 + start // half],
                    )
                )
            for copy in copies:
                copy.start()
            for copy in copies:
                copy.wait()


def input_planes(todo, w_ref, wide_ref, done_ref):
    _, cb, hgt, wid = done_ref.shape
    half = wid // 2
    groups = hgt // 4
    lanes = groups * wid
    taps = 9 * cb
    spread = pair_matrix(True, wid, half)
    spread = jnp.concatenate([spread, spread], axis=0)
    keep = lax.broadcasted_iota(jnp.int32, (3 * cb, lanes), 1) < lanes - half
    w = [w_ref[a * taps : (a + 1) * taps, :] for a in range(3)]
    behind = jnp.concatenate([w[2], w[0]], axis=1)
    for slot, grads in enumerate(todo):
        if len(grads) == 1:
            e_all = jnp.dot(w[1], grads[0], preferred_element_type=jnp.float32)
        else:
            e_all = jnp.dot(
                behind, jnp.concatenate(grads, axis=0), preferred_element_type=jnp.float32
            )
        by_b = [e_all[b * 3 * cb : (b + 1) * 3 * cb] for b in range(3)]
        shifted = pltpu.roll(by_b[0], lanes - half, 1)
        rows = (by_b[1], by_b[2] + jnp.where(keep, shifted, 0.0))
        left = []
        for f in rows:
            for j in range(groups):
                t = f[:, j * wid : (j + 1) * wid]
                left.append(
                    jnp.concatenate([t[e * cb : (e + 1) * cb] for e in range(3)], axis=1)
                )
        left = jnp.concatenate(left, axis=0)
        high = left.astype(jnp.bfloat16)
        low = (left - high.astype(jnp.float32)).astype(jnp.bfloat16)
        full = jnp.dot(
            jnp.concatenate([high, low], axis=1), spread, preferred_element_type=jnp.float32
        )
        for par in range(2):
            for j in range(groups):
                for h in range(2):
                    y = 2 * (2 * j + h) + par
                    at = (par * groups + j) * cb
                    wide_ref[pl.ds(y, cb, stride=hgt), :] = full[
                        at : at + cb, h * wid : (h + 1) * wid
                    ]
        done_ref[slot] = wide_ref[...].reshape(cb, hgt, wid).astype(jnp.bfloat16)


def plane_copies(done_ref, out_ref, first, sems):
    return [
        pltpu.make_async_copy(done_ref.at[i], out_ref.at[:, first + i], sems.at[i])
        for i in range(done_ref.shape[0])
    ]


def input_kernel(w_ref, one_ref, two_ref, _, out_ref, wide_ref, done_ref, sems):
    one, two = one_ref[...], two_ref[...]
    input_planes([(one,), (one, two)], w_ref, wide_ref, done_ref)
    for copy in plane_copies(done_ref, out_ref, 0, sems):
        copy.start()
    for copy in plane_copies(done_ref, out_ref, 0, sems):
        copy.wait()


def edge_kernel(w_ref, one_ref, two_ref, done_ref, wide_ref):
    two = two_ref[...]
    inside = lax.axis_index("space") < lax.axis_size("space") - 1
    two = jnp.where(inside, two.astype(jnp.float32), 0.0).astype(jnp.bfloat16)
    input_planes([(one_ref[...], two)], w_ref, wide_ref, done_ref)


def moved(block, axis, k):
    n = lax.axis_size(axis)
    return lax.ppermute(block, axis, [(i, i ^ k if XOR else (i + k) % n) for i in range(n)])


def on_device(volume, kernel, upstream):
    cb, planes, hgt, wid = volume.shape
    ob = upstream.shape[0]
    out_ch = kernel.shape[4]
    n_chan, n_space = lax.axis_size("chan"), lax.axis_size("space")
    direct = n_chan <= FEW and n_chan & (n_chan - 1) == 0
    n = n_chan if direct else 1
    taps = 27 * cb
    cells = hgt // 4 * wid
    f32, bf16 = jnp.float32, jnp.bfloat16
    shape = jax.ShapeDtypeStruct
    weights = kernel.transpose(1, 2, 3, 0, 4).reshape(taps, out_ch)
    up = upstream[:, 0].transpose(1, 0, 2)
    spread = pl.pallas_call(
        spread_kernel, out_shape=shape((ob, cells), f32), compiler_params=params()
    )(up)

    scratch = [pltpu.VMEM((3 * cb * hgt, wid), f32)]
    if n > 1:
        scratch.append(pltpu.VMEM((out_ch, cells), f32))
    part_shapes = [shape((ob if direct else out_ch, cells), f32)] * n
    out_planes = range(planes // 2)
    cols, grads, acts = {}, {}, {}
    vmem = pl.BlockSpec(memory_space=pltpu.VMEM)
    hbm = pl.BlockSpec(memory_space=pltpu.HBM)

    def from_hbm(x):
        return pltpu.with_memory_space_constraint(x, pltpu.HBM)

    half = -(-taps // 32) * 16
    cols_shape = shape((2 * half, cells), bf16)
    vol, edge = pl.pallas_call(
        load_kernel,
        in_specs=[hbm],
        out_shape=[shape(volume.shape, bf16), shape((cb, 1, hgt, wid), bf16)],
        scratch_shapes=[pltpu.SemaphoreType.DMA((1,))],
        compiler_params=params(),
    )(from_hbm(volume))
    rim = lax.ppermute(edge, "space", [(i, (i + 1) % n_space) for i in range(n_space)])
    for z in reversed(out_planes):
        cols[z], *parts = pl.pallas_call(
            functools.partial(fwd_kernel, n, ob, z),
            out_shape=[cols_shape] + part_shapes,
            scratch_shapes=scratch,
            compiler_params=params(),
        )(*(() if z else (rim,)), vol, weights)
        if direct:
            parts = parts[:1] + [moved(p, "chan", k) for k, p in zip(RS[z], parts[1:])]
        else:
            parts = [lax.psum_scatter(parts[0], "chan", scatter_dimension=0, tiled=True)]
        own, acts[z] = pl.pallas_call(
            act_kernel,
            out_shape=[shape((ob, cells), bf16), shape((ob, cells), f32)],
            compiler_params=params(),
        )(spread, *parts)
        if direct:
            grads[z] = [own] + [moved(own, "chan", k) for k in AG[z]]
        else:
            grads[z] = [lax.all_gather(own, "chan", axis=0, tiled=True)]

    wide, plane = pltpu.VMEM((cb * hgt, wid), f32), (cb, hgt, wid)
    grad_shape = shape((out_ch, cells), bf16)
    term, grads[1], pooled, input_grad = pl.pallas_call(
        functools.partial(middle_kernel, n),
        out_specs=[vmem, vmem, vmem, hbm],
        out_shape=[
            shape((2 * half, out_ch), f32),
            grad_shape,
            shape(upstream.shape, bf16),
            shape(volume.shape, bf16),
        ],
        scratch_shapes=[wide, pltpu.VMEM((1,) + plane, bf16), pltpu.SemaphoreType.DMA((1,))],
        compiler_params=params(),
    )(weights, acts[0], acts[1], cols[1], *grads[1])
    send, grads[0] = pl.pallas_call(
        functools.partial(send_kernel, n),
        out_shape=[shape((half, out_ch), f32), grad_shape],
        compiler_params=params(),
    )(term, cols[0], *grads[0])
    keep = pl.pallas_call(
        keep_kernel,
        out_shape=shape((half, out_ch), f32),
        compiler_params=params(),
    )(term, cols[0], grads[0])

    rows = keep + lax.ppermute(send, "space", [(i, i ^ 1) for i in range(n_space)])
    bits = [1 << b for b in range(1, n_space.bit_length() - 1)]
    groups = [bits[i : i + 2] for i in range(0, len(bits), 2)]
    after = None
    for r, group in enumerate(groups):
        sent = rows.astype(bf16)
        if r == len(groups) - 1:
            sent, grads, input_grad = lax.optimization_barrier((sent, grads, input_grad))
        partners = [sum(group[b] * (k >> b & 1) for b in range(len(group))) for k in range(1, 1 << len(group))]
        terms = [sent] + [None] * len(partners)
        for k in CHIPS:
            if k < len(partners):
                terms[k + 1] = lax.ppermute(
                    sent, "space", [(i, i ^ partners[k]) for i in range(n_space)]
                )
        if r == len(groups) - 1:
            after = lax.ppermute(grads[0], "space", [((i + 1) % n_space, i) for i in range(n_space)])
            input_grad = pl.pallas_call(
                input_kernel,
                in_specs=[vmem] * 3 + [hbm],
                out_specs=hbm,
                out_shape=shape(volume.shape, bf16),
                scratch_shapes=[wide, pltpu.VMEM((2,) + plane, bf16), pltpu.SemaphoreType.DMA((2,))],
                input_output_aliases={3: 0},
                compiler_params=params(),
            )(weights, grads[0], grads[1], input_grad)
        terms = [t.astype(f32) for t in terms]
        while len(terms) > 1:
            terms = [a + b for a, b in zip(terms[::2], terms[1::2])]
        rows = terms[0]
    rows, input_grad, after = lax.optimization_barrier((rows, input_grad, after))
    edge = pl.pallas_call(
        edge_kernel,
        out_shape=shape((1,) + plane, bf16),
        scratch_shapes=[wide],
        compiler_params=params(),
    )(weights, grads[1], after)
    other = lax.ppermute(rows, "space", [(i, i ^ 1) for i in range(n_space)])
    weight_grad, input_grad = pl.pallas_call(
        join_kernel,
        in_specs=[vmem] * 3 + [hbm],
        out_specs=[hbm] * 2,
        out_shape=[shape((taps, out_ch), f32), shape(volume.shape, bf16)],
        scratch_shapes=[pltpu.SemaphoreType.DMA((3,))],
        input_output_aliases={3: 1},
        compiler_params=params(),
    )(rows, other, edge, input_grad)
    weight_grad = weight_grad.reshape(3, 3, 3, cb, out_ch).transpose(3, 0, 1, 2, 4)
    return pooled, input_grad, weight_grad


def solution(mesh):
    return jax.shard_map(
        on_device,
        mesh=mesh,
        in_specs=(
            P("chan", "space", None, None),
            P("chan", None, None, None, None),
            P("chan", "space", None, None),
        ),
        out_specs=(
            P("chan", "space", None, None),
            P("chan", "space", None, None),
            P("chan", None, None, None, None),
        ),
        check_vma=False,
    )
```

```python
import functools

import jax
import jax.numpy as jnp
from jax import lax
from jax.experimental import pallas as pl
from jax.experimental.pallas import tpu as pltpu
from jax.sharding import PartitionSpec as P

SLOPE = 0.3
VMEM = 24 * 1024 * 1024
RS = {1: ((3, 2, 1, 0), (2, 3, 0, 1), (1, 0, 3, 2)), 0: ((3, 2, 1, 0), (2, 0, 3, 1), (1, 3, 0, 2))}
AG = {1: ((1, 0, 3, 2), (3, 2, 1, 0), (2, 3, 0, 1)), 0: ((1, 3, 0, 2), (3, 2, 1, 0), (2, 0, 3, 1))}
CHIPS = (0, 1, 2)
FEW = 4


def params():
    return pltpu.CompilerParams(vmem_limit_bytes=VMEM)


def pair_matrix(transposed, wid, half):
    shape = (3 * wid, 2 * wid) if transposed else (2 * wid, 3 * wid)
    long, short = (0, 1) if transposed else (1, 0)
    src = lax.broadcasted_iota(jnp.int32, shape, short)
    dst = lax.broadcasted_iota(jnp.int32, shape, long)
    e = (dst >= wid).astype(jnp.int32) + (dst >= 2 * wid).astype(jnp.int32)
    rest = dst - e * wid
    h = (rest >= half).astype(jnp.int32)
    x = 2 * (rest - h * half) + e - 1
    hit = (x >= 0) & (x < wid) & (src == h * wid + x)
    return jnp.where(hit, 1.0, 0.0).astype(jnp.bfloat16)


def load_kernel(vol_hbm, vol_ref, edge_ref, sems):
    cb, planes = vol_ref.shape[:2]
    pieces = sems.shape[0]
    size = cb // pieces
    copies = [
        pltpu.make_async_copy(
            vol_hbm.at[pl.ds(i * size, size)], vol_ref.at[pl.ds(i * size, size)], sems.at[i]
        )
        for i in range(pieces)
    ]
    for copy in copies:
        copy.start()
    for copy in copies:
        copy.wait()
    edge_ref[...] = vol_ref[:, planes - 1 :]


def pick(table, i):
    value = jnp.int32(table[0])
    for k, entry in enumerate(table[1:], 1):
        value = jnp.where(i == k, entry, value)
    return value


def fwd_kernel(n, ob, z, *refs):
    if z:
        vol_ref, w_ref, cols_ref, *rest = refs
    else:
        rim_ref, vol_ref, w_ref, cols_ref, *rest = refs
    part_refs = rest[:-2] if n > 1 else rest[:-1]
    wide_ref = rest[-2] if n > 1 else rest[-1]
    cb, _, hgt, wid = vol_ref.shape
    groups = hgt // 4
    sel = pair_matrix(False, wid, wid // 2)
    zero = jnp.zeros((cb, wid), jnp.float32)
    left, right = [], []
    for a in range(3):
        plane = vol_ref[:, 2 * z + a - 1] if z or a else rim_ref[:, 0]
        plane = plane.astype(jnp.float32).reshape(cb * hgt, wid)
        if not (z or a):
            plane = jnp.where(lax.axis_index("space") == 0, 0.0, plane)
        wide_ref[a * cb * hgt : (a + 1) * cb * hgt, :] = plane
        row = [wide_ref[pl.ds(a * cb * hgt + y, cb, stride=hgt), :] for y in range(hgt)]
        cls = [[row[4 * j + r] for j in range(groups)] for r in range(4)]

        def stack(blocks):
            return jnp.concatenate(blocks, axis=0).astype(jnp.bfloat16)

        back = stack([zero] + cls[3][:-1])
        cls = [stack(c) for c in cls]
        left += [back, cls[0], cls[1]]
        right += [cls[1], cls[2], cls[3]]
    taps = jnp.dot(
        jnp.concatenate([jnp.concatenate(left, axis=0), jnp.concatenate(right, axis=0)], axis=1),
        sel,
        preferred_element_type=jnp.float32,
    ).astype(jnp.bfloat16)
    for ab in range(9):
        for e in range(3):
            tap = ab * 3 + e
            cols_ref[tap * cb : (tap + 1) * cb, :] = jnp.concatenate(
                [
                    taps[(ab * groups + j) * cb : (ab * groups + j + 1) * cb, e * wid : (e + 1) * wid]
                    for j in range(groups)
                ],
                axis=1,
            )
    if cols_ref.shape[0] > 27 * cb:
        pad = (cols_ref.shape[0] - 27 * cb, cols_ref.shape[1])
        cols_ref[27 * cb :, :] = jnp.zeros(pad, jnp.bfloat16)
    part = lax.dot_general(
        w_ref[...],
        cols_ref[0 : 27 * cb, :],
        (((0,), (0,)), ((), ())),
        preferred_element_type=jnp.float32,
    )
    if n == 1:
        part_refs[0][...] = part
        return
    all_ref = rest[-1]
    all_ref[...] = part
    me = lax.axis_index("chan")
    for to, ref in zip((tuple(range(n)),) + RS[z], part_refs):
        start = pl.multiple_of(pick(to, me) * ob, ob)
        ref[...] = all_ref[pl.ds(start, ob), :]


def spread_kernel(up_ref, out_ref):
    groups, ob, small = up_ref.shape
    wid = 4 * small
    r = lax.broadcasted_iota(jnp.int32, (small, wid), 0)
    c = lax.broadcasted_iota(jnp.int32, (small, wid), 1)
    c = c - jnp.where(c >= 2 * small, 2 * small, 0)
    grow = jnp.where((c >= 2 * r) & (c <= 2 * r + 1), 1.0, 0.0).astype(jnp.bfloat16)
    for j in range(groups):
        spread = jnp.dot(up_ref[j], grow, preferred_element_type=jnp.float32)
        out_ref[:, j * wid : (j + 1) * wid] = spread * 0.125


def act_kernel(spread_ref, *rest):
    *part_refs, grad_ref, act_ref = rest
    pre = part_refs[0][...]
    for ref in part_refs[1:]:
        pre = pre + ref[...]
    grad = spread_ref[...] * jnp.where(pre > 0, 1.0, SLOPE)
    grad_ref[...] = grad.astype(jnp.bfloat16)
    act_ref[...] = jnp.where(pre > 0, pre, SLOPE * pre)


def pool_planes(one_ref, two_ref, out_ref):
    ob, _, groups, small = out_ref.shape
    wid = 4 * small
    r = lax.broadcasted_iota(jnp.int32, (wid, small), 0)
    c = lax.broadcasted_iota(jnp.int32, (wid, small), 1)
    r = r - jnp.where(r >= 2 * small, 2 * small, 0)
    pool = jnp.where((r >= 2 * c) & (r <= 2 * c + 1), 0.125, 0.0)
    act = one_ref[...] + two_ref[...]
    means = [
        jnp.dot(
            act[:, j * wid : (j + 1) * wid],
            pool,
            precision=lax.Precision.HIGHEST,
            preferred_element_type=jnp.float32,
        )
        for j in range(groups)
    ]
    out_ref[:, 0] = jnp.stack(means, axis=1).astype(jnp.bfloat16)


def in_order(n, z, block_refs, grad_ref):
    if n == 1:
        grad_ref[...] = block_refs[0][...]
        return
    me = lax.axis_index("chan")
    ob = block_refs[0].shape[0]
    for to, ref in zip((tuple(range(n)),) + AG[z], block_refs):
        start = pl.multiple_of(pick([to.index(i) for i in range(n)], me) * ob, ob)
        grad_ref[pl.ds(start, ob), :] = ref[...]


def weight_term(cols, grad_ref):
    return lax.dot_general(
        cols,
        grad_ref[...],
        (((1,), (1,)), ((), ())),
        preferred_element_type=jnp.float32,
    )


def middle_kernel(n, w_ref, act_one_ref, act_two_ref, cols_ref, *refs):
    *block_refs, wgrad_ref, grad_ref, pooled_ref, out_ref, wide_ref, done_ref, sems = refs
    in_order(n, 1, block_refs, grad_ref)
    input_planes([(grad_ref[...],)], w_ref, wide_ref, done_ref)
    for copy in plane_copies(done_ref, out_ref, 2, sems):
        copy.start()
    wgrad_ref[...] = weight_term(cols_ref[...], grad_ref)
    pool_planes(act_one_ref, act_two_ref, pooled_ref)
    for copy in plane_copies(done_ref, out_ref, 2, sems):
        copy.wait()


def send_kernel(n, sum_ref, cols_ref, *refs):
    *block_refs, send_ref, grad_ref = refs
    in_order(n, 0, block_refs, grad_ref)
    half = send_ref.shape[0]
    start = pl.multiple_of((1 - lax.rem(lax.axis_index("space"), 2)) * half, 16)
    send_ref[...] = sum_ref[pl.ds(start, half), :] + weight_term(
        cols_ref[pl.ds(start, half), :], grad_ref
    )


def keep_kernel(sum_ref, cols_ref, grad_ref, keep_ref):
    half = keep_ref.shape[0]
    start = pl.multiple_of(lax.rem(lax.axis_index("space"), 2) * half, 16)
    keep_ref[...] = sum_ref[pl.ds(start, half), :] + weight_term(
        cols_ref[pl.ds(start, half), :], grad_ref
    )


def half_copy(ref, out_ref, of, sem):
    half = ref.shape[0]
    size = min(half, out_ref.shape[0] - of * half)
    return pltpu.make_async_copy(ref.at[pl.ds(0, size)], out_ref.at[pl.ds(of * half, size)], sem)


def on_core(act):
    for core in range(2):

        @pl.when(lax.rem(lax.axis_index("space"), 2) == core)
        def _():
            act(core)


def join_kernel(other_ref, _, out_ref, sem):
    def place(core):
        copy = half_copy(other_ref, out_ref, 1 - core, sem)
        copy.start()
        copy.wait()

    on_core(place)


def input_planes(todo, w_ref, wide_ref, done_ref):
    _, cb, hgt, wid = done_ref.shape
    half = wid // 2
    groups = hgt // 4
    lanes = groups * wid
    taps = 9 * cb
    spread = pair_matrix(True, wid, half)
    spread = jnp.concatenate([spread, spread], axis=0)
    keep = lax.broadcasted_iota(jnp.int32, (3 * cb, lanes), 1) < lanes - half
    w = [w_ref[a * taps : (a + 1) * taps, :] for a in range(3)]
    behind = jnp.concatenate([w[2], w[0]], axis=1)
    for slot, grads in enumerate(todo):
        if len(grads) == 1:
            e_all = jnp.dot(w[1], grads[0], preferred_element_type=jnp.float32)
        else:
            e_all = jnp.dot(
                behind, jnp.concatenate(grads, axis=0), preferred_element_type=jnp.float32
            )
        by_b = [e_all[b * 3 * cb : (b + 1) * 3 * cb] for b in range(3)]
        shifted = pltpu.roll(by_b[0], lanes - half, 1)
        rows = (by_b[1], by_b[2] + jnp.where(keep, shifted, 0.0))
        left = []
        for f in rows:
            for j in range(groups):
                t = f[:, j * wid : (j + 1) * wid]
                left.append(
                    jnp.concatenate([t[e * cb : (e + 1) * cb] for e in range(3)], axis=1)
                )
        left = jnp.concatenate(left, axis=0)
        high = left.astype(jnp.bfloat16)
        low = (left - high.astype(jnp.float32)).astype(jnp.bfloat16)
        full = jnp.dot(
            jnp.concatenate([high, low], axis=1), spread, preferred_element_type=jnp.float32
        )
        for par in range(2):
            for j in range(groups):
                for h in range(2):
                    y = 2 * (2 * j + h) + par
                    at = (par * groups + j) * cb
                    wide_ref[pl.ds(y, cb, stride=hgt), :] = full[
                        at : at + cb, h * wid : (h + 1) * wid
                    ]
        done_ref[slot] = wide_ref[...].reshape(cb, hgt, wid).astype(jnp.bfloat16)


def plane_copies(done_ref, out_ref, first, sems):
    return [
        pltpu.make_async_copy(done_ref.at[i], out_ref.at[:, first + i], sems.at[i])
        for i in range(done_ref.shape[0])
    ]


def input_kernel(w_ref, one_ref, two_ref, _, out_ref, wide_ref, done_ref, sems):
    one, two = one_ref[...], two_ref[...]
    input_planes([(one,), (one, two)], w_ref, wide_ref, done_ref)
    for copy in plane_copies(done_ref, out_ref, 0, sems):
        copy.start()
    for copy in plane_copies(done_ref, out_ref, 0, sems):
        copy.wait()


def edge_kernel(w_ref, one_ref, two_ref, own_ref, _, out_ref, wgrad_ref, wide_ref, done_ref, sems):
    on_core(lambda core: half_copy(own_ref, wgrad_ref, core, sems.at[1]).start())
    two = two_ref[...]
    inside = lax.axis_index("space") < lax.axis_size("space") - 1
    two = jnp.where(inside, two.astype(jnp.float32), 0.0).astype(jnp.bfloat16)
    input_planes([(one_ref[...], two)], w_ref, wide_ref, done_ref)
    copies = plane_copies(done_ref, out_ref, out_ref.shape[1] - 1, sems)
    for copy in copies:
        copy.start()
    on_core(lambda core: half_copy(own_ref, wgrad_ref, core, sems.at[1]).wait())
    for copy in copies:
        copy.wait()


def moved(block, axis, to):
    return lax.ppermute(block, axis, list(enumerate(to)))


def on_device(volume, kernel, upstream):
    cb, planes, hgt, wid = volume.shape
    ob = upstream.shape[0]
    out_ch = kernel.shape[4]
    n_chan, n_space = lax.axis_size("chan"), lax.axis_size("space")
    direct = n_chan == FEW
    n = n_chan if direct else 1
    taps = 27 * cb
    cells = hgt // 4 * wid
    f32, bf16 = jnp.float32, jnp.bfloat16
    shape = jax.ShapeDtypeStruct
    weights = kernel.transpose(1, 2, 3, 0, 4).reshape(taps, out_ch)
    up = upstream[:, 0].transpose(1, 0, 2)
    spread = pl.pallas_call(
        spread_kernel, out_shape=shape((ob, cells), f32), compiler_params=params()
    )(up)

    scratch = [pltpu.VMEM((3 * cb * hgt, wid), f32)]
    if n > 1:
        scratch.append(pltpu.VMEM((out_ch, cells), f32))
    part_shapes = [shape((ob if direct else out_ch, cells), f32)] * n
    out_planes = range(planes // 2)
    cols, grads, acts = {}, {}, {}
    vmem = pl.BlockSpec(memory_space=pltpu.VMEM)
    hbm = pl.BlockSpec(memory_space=pltpu.HBM)

    def from_hbm(x):
        return pltpu.with_memory_space_constraint(x, pltpu.HBM)

    half = -(-taps // 32) * 16
    cols_shape = shape((2 * half, cells), bf16)
    vol, edge = pl.pallas_call(
        load_kernel,
        in_specs=[hbm],
        out_shape=[shape(volume.shape, bf16), shape((cb, 1, hgt, wid), bf16)],
        scratch_shapes=[pltpu.SemaphoreType.DMA((1,))],
        compiler_params=params(),
    )(from_hbm(volume))
    rim = lax.ppermute(edge, "space", [(i, (i + 1) % n_space) for i in range(n_space)])
    for z in reversed(out_planes):
        cols[z], *parts = pl.pallas_call(
            functools.partial(fwd_kernel, n, ob, z),
            out_shape=[cols_shape] + part_shapes,
            scratch_shapes=scratch,
            compiler_params=params(),
        )(*(() if z else (rim,)), vol, weights)
        if direct:
            parts = parts[:1] + [moved(p, "chan", to) for to, p in zip(RS[z], parts[1:])]
        else:
            parts = [lax.psum_scatter(parts[0], "chan", scatter_dimension=0, tiled=True)]
        own, acts[z] = pl.pallas_call(
            act_kernel,
            out_shape=[shape((ob, cells), bf16), shape((ob, cells), f32)],
            compiler_params=params(),
        )(spread, *parts)
        if direct:
            grads[z] = [own] + [moved(own, "chan", to) for to in AG[z]]
        else:
            grads[z] = [lax.all_gather(own, "chan", axis=0, tiled=True)]

    wide, plane = pltpu.VMEM((cb * hgt, wid), f32), (cb, hgt, wid)
    grad_shape = shape((out_ch, cells), bf16)
    term, grads[1], pooled, input_grad = pl.pallas_call(
        functools.partial(middle_kernel, n),
        out_specs=[vmem, vmem, vmem, hbm],
        out_shape=[
            shape((2 * half, out_ch), f32),
            grad_shape,
            shape(upstream.shape, bf16),
            shape(volume.shape, bf16),
        ],
        scratch_shapes=[wide, pltpu.VMEM((1,) + plane, bf16), pltpu.SemaphoreType.DMA((1,))],
        compiler_params=params(),
    )(weights, acts[0], acts[1], cols[1], *grads[1])
    send, grads[0] = pl.pallas_call(
        functools.partial(send_kernel, n),
        out_shape=[shape((half, out_ch), f32), grad_shape],
        compiler_params=params(),
    )(term, cols[0], *grads[0])
    keep = pl.pallas_call(
        keep_kernel,
        out_shape=shape((half, out_ch), f32),
        compiler_params=params(),
    )(term, cols[0], grads[0])

    rows = keep + lax.ppermute(send, "space", [(i, i ^ 1) for i in range(n_space)])
    bits = [1 << b for b in range(1, n_space.bit_length() - 1)]
    groups = [bits[i : i + 2] for i in range(0, len(bits), 2)]
    after = None
    for r, group in enumerate(groups):
        sent = rows.astype(bf16)
        if r == len(groups) - 1:
            sent, grads, input_grad = lax.optimization_barrier((sent, grads, input_grad))
        partners = [sum(group[b] * (k >> b & 1) for b in range(len(group))) for k in range(1, 1 << len(group))]
        terms = [sent] + [None] * len(partners)
        for k in CHIPS:
            if k < len(partners):
                terms[k + 1] = lax.ppermute(
                    sent, "space", [(i, i ^ partners[k]) for i in range(n_space)]
                )
        if r == len(groups) - 1:
            after = lax.ppermute(grads[0], "space", [((i + 1) % n_space, i) for i in range(n_space)])
            input_grad = pl.pallas_call(
                input_kernel,
                in_specs=[vmem] * 3 + [hbm],
                out_specs=hbm,
                out_shape=shape(volume.shape, bf16),
                scratch_shapes=[wide, pltpu.VMEM((2,) + plane, bf16), pltpu.SemaphoreType.DMA((2,))],
                input_output_aliases={3: 0},
                compiler_params=params(),
            )(weights, grads[0], grads[1], input_grad)
        terms = [t.astype(f32) for t in terms]
        while len(terms) > 1:
            terms = [a + b for a, b in zip(terms[::2], terms[1::2])]
        rows = terms[0]
    rows, input_grad, after = lax.optimization_barrier((rows, input_grad, after))
    input_grad, weight_grad = pl.pallas_call(
        edge_kernel,
        in_specs=[vmem] * 4 + [hbm],
        out_specs=[hbm] * 2,
        out_shape=[shape(volume.shape, bf16), shape((taps, out_ch), f32)],
        scratch_shapes=[wide, pltpu.VMEM((1,) + plane, bf16), pltpu.SemaphoreType.DMA((2,))],
        input_output_aliases={4: 0},
        compiler_params=params(),
    )(weights, grads[1], after, rows, input_grad)
    other = lax.ppermute(rows, "space", [(i, i ^ 1) for i in range(n_space)])
    weight_grad = pl.pallas_call(
        join_kernel,
        in_specs=[vmem, hbm],
        out_specs=hbm,
        out_shape=shape((taps, out_ch), f32),
        scratch_shapes=[pltpu.SemaphoreType.DMA],
        input_output_aliases={1: 0},
        compiler_params=params(),
    )(other, weight_grad)
    weight_grad = weight_grad.reshape(3, 3, 3, cb, out_ch).transpose(3, 0, 1, 2, 4)
    return pooled, input_grad, weight_grad


def solution(mesh):
    return jax.shard_map(
        on_device,
        mesh=mesh,
        in_specs=(
            P("chan", "space", None, None),
            P("chan", None, None, None, None),
            P("chan", "space", None, None),
        ),
        out_specs=(
            P("chan", "space", None, None),
            P("chan", "space", None, None),
            P("chan", None, None, None, None),
        ),
        check_vma=False,
    )
```

```python
import functools

import jax
import jax.numpy as jnp
from jax import lax
from jax.experimental import pallas as pl
from jax.experimental.pallas import tpu as pltpu
from jax.sharding import PartitionSpec as P

SLOPE = 0.3
VMEM = 24 * 1024 * 1024
RS = {1: ((3, 2, 1, 0), (2, 3, 0, 1), (1, 0, 3, 2)), 0: ((3, 2, 1, 0), (2, 0, 3, 1), (1, 3, 0, 2))}
AG = {1: ((1, 0, 3, 2), (3, 2, 1, 0), (2, 3, 0, 1)), 0: ((1, 3, 0, 2), (3, 2, 1, 0), (2, 0, 3, 1))}
CHIPS = (0, 1, 2)
FEW = 4


def params():
    return pltpu.CompilerParams(vmem_limit_bytes=VMEM)


def pair_matrix(transposed, wid, half):
    shape = (3 * wid, 2 * wid) if transposed else (2 * wid, 3 * wid)
    long, short = (0, 1) if transposed else (1, 0)
    src = lax.broadcasted_iota(jnp.int32, shape, short)
    dst = lax.broadcasted_iota(jnp.int32, shape, long)
    e = (dst >= wid).astype(jnp.int32) + (dst >= 2 * wid).astype(jnp.int32)
    rest = dst - e * wid
    h = (rest >= half).astype(jnp.int32)
    x = 2 * (rest - h * half) + e - 1
    hit = (x >= 0) & (x < wid) & (src == h * wid + x)
    return jnp.where(hit, 1.0, 0.0).astype(jnp.bfloat16)


def load_kernel(vol_hbm, vol_ref, edge_ref, sems):
    cb, planes = vol_ref.shape[:2]
    pieces = sems.shape[0]
    size = cb // pieces
    copies = [
        pltpu.make_async_copy(
            vol_hbm.at[pl.ds(i * size, size)], vol_ref.at[pl.ds(i * size, size)], sems.at[i]
        )
        for i in range(pieces)
    ]
    for copy in copies:
        copy.start()
    for copy in copies:
        copy.wait()
    edge_ref[...] = vol_ref[:, planes - 1 :]


def pick(table, i):
    value = jnp.int32(table[0])
    for k, entry in enumerate(table[1:], 1):
        value = jnp.where(i == k, entry, value)
    return value


def fwd_kernel(n, ob, z, *refs):
    if z:
        vol_ref, w_ref, cols_ref, *rest = refs
    else:
        rim_ref, vol_ref, w_ref, cols_ref, *rest = refs
    part_refs = rest[:-2] if n > 1 else rest[:-1]
    wide_ref = rest[-2] if n > 1 else rest[-1]
    cb, _, hgt, wid = vol_ref.shape
    groups = hgt // 4
    sel = pair_matrix(False, wid, wid // 2)
    zero = jnp.zeros((cb, wid), jnp.float32)
    left, right = [], []
    for a in range(3):
        plane = vol_ref[:, 2 * z + a - 1] if z or a else rim_ref[:, 0]
        plane = plane.astype(jnp.float32).reshape(cb * hgt, wid)
        if not (z or a):
            plane = jnp.where(lax.axis_index("space") == 0, 0.0, plane)
        wide_ref[a * cb * hgt : (a + 1) * cb * hgt, :] = plane
        row = [wide_ref[pl.ds(a * cb * hgt + y, cb, stride=hgt), :] for y in range(hgt)]
        cls = [[row[4 * j + r] for j in range(groups)] for r in range(4)]

        def stack(blocks):
            return jnp.concatenate(blocks, axis=0).astype(jnp.bfloat16)

        back = stack([zero] + cls[3][:-1])
        cls = [stack(c) for c in cls]
        left += [back, cls[0], cls[1]]
        right += [cls[1], cls[2], cls[3]]
    taps = jnp.dot(
        jnp.concatenate([jnp.concatenate(left, axis=0), jnp.concatenate(right, axis=0)], axis=1),
        sel,
        preferred_element_type=jnp.float32,
    ).astype(jnp.bfloat16)
    for ab in range(9):
        for e in range(3):
            tap = ab * 3 + e
            cols_ref[tap * cb : (tap + 1) * cb, :] = jnp.concatenate(
                [
                    taps[(ab * groups + j) * cb : (ab * groups + j + 1) * cb, e * wid : (e + 1) * wid]
                    for j in range(groups)
                ],
                axis=1,
            )
    if cols_ref.shape[0] > 27 * cb:
        pad = (cols_ref.shape[0] - 27 * cb, cols_ref.shape[1])
        cols_ref[27 * cb :, :] = jnp.zeros(pad, jnp.bfloat16)
    part = lax.dot_general(
        w_ref[...],
        cols_ref[0 : 27 * cb, :],
        (((0,), (0,)), ((), ())),
        preferred_element_type=jnp.float32,
    )
    if n == 1:
        part_refs[0][...] = part
        return
    all_ref = rest[-1]
    all_ref[...] = part
    me = lax.axis_index("chan")
    for to, ref in zip((tuple(range(n)),) + RS[z], part_refs):
        start = pl.multiple_of(pick(to, me) * ob, ob)
        ref[...] = all_ref[pl.ds(start, ob), :]


def spread_kernel(up_ref, out_ref):
    groups, ob, small = up_ref.shape
    wid = 4 * small
    r = lax.broadcasted_iota(jnp.int32, (small, wid), 0)
    c = lax.broadcasted_iota(jnp.int32, (small, wid), 1)
    c = c - jnp.where(c >= 2 * small, 2 * small, 0)
    grow = jnp.where((c >= 2 * r) & (c <= 2 * r + 1), 1.0, 0.0).astype(jnp.bfloat16)
    for j in range(groups):
        spread = jnp.dot(up_ref[j], grow, preferred_element_type=jnp.float32)
        out_ref[:, j * wid : (j + 1) * wid] = spread * 0.125


def act_kernel(spread_ref, *rest):
    *part_refs, grad_ref, act_ref = rest
    pre = part_refs[0][...]
    for ref in part_refs[1:]:
        pre = pre + ref[...]
    grad = spread_ref[...] * jnp.where(pre > 0, 1.0, SLOPE)
    grad_ref[...] = grad.astype(jnp.bfloat16)
    act_ref[...] = jnp.where(pre > 0, pre, SLOPE * pre)


def pool_planes(one_ref, two_ref, out_ref):
    ob, _, groups, small = out_ref.shape
    wid = 4 * small
    r = lax.broadcasted_iota(jnp.int32, (wid, small), 0)
    c = lax.broadcasted_iota(jnp.int32, (wid, small), 1)
    r = r - jnp.where(r >= 2 * small, 2 * small, 0)
    pool = jnp.where((r >= 2 * c) & (r <= 2 * c + 1), 0.125, 0.0)
    act = one_ref[...] + two_ref[...]
    means = [
        jnp.dot(
            act[:, j * wid : (j + 1) * wid],
            pool,
            precision=lax.Precision.HIGHEST,
            preferred_element_type=jnp.float32,
        )
        for j in range(groups)
    ]
    out_ref[:, 0] = jnp.stack(means, axis=1).astype(jnp.bfloat16)


def in_order(n, z, block_refs, grad_ref):
    if n == 1:
        grad_ref[...] = block_refs[0][...]
        return
    me = lax.axis_index("chan")
    ob = block_refs[0].shape[0]
    for to, ref in zip((tuple(range(n)),) + AG[z], block_refs):
        start = pl.multiple_of(pick([to.index(i) for i in range(n)], me) * ob, ob)
        grad_ref[pl.ds(start, ob), :] = ref[...]


def weight_term(cols, grad_ref):
    return lax.dot_general(
        cols,
        grad_ref[...],
        (((1,), (1,)), ((), ())),
        preferred_element_type=jnp.float32,
    )


def middle_kernel(n, w_ref, act_one_ref, act_two_ref, cols_ref, *refs):
    *block_refs, wgrad_ref, grad_ref, pooled_ref, out_ref, wide_ref, done_ref, sems = refs
    in_order(n, 1, block_refs, grad_ref)
    input_planes([(grad_ref[...],)], w_ref, wide_ref, done_ref)
    for copy in plane_copies(done_ref, out_ref, 2, sems):
        copy.start()
    wgrad_ref[...] = weight_term(cols_ref[...], grad_ref)
    pool_planes(act_one_ref, act_two_ref, pooled_ref)
    for copy in plane_copies(done_ref, out_ref, 2, sems):
        copy.wait()


def send_kernel(n, sum_ref, cols_ref, *refs):
    *block_refs, send_ref, grad_ref = refs
    in_order(n, 0, block_refs, grad_ref)
    half = send_ref.shape[0]
    start = pl.multiple_of((1 - lax.rem(lax.axis_index("space"), 2)) * half, 16)
    send = sum_ref[pl.ds(start, half), :] + weight_term(cols_ref[pl.ds(start, half), :], grad_ref)
    send_ref[...] = send.astype(send_ref.dtype)


def keep_kernel(sum_ref, cols_ref, grad_ref, keep_ref):
    half = keep_ref.shape[0]
    start = pl.multiple_of(lax.rem(lax.axis_index("space"), 2) * half, 16)
    keep_ref[...] = sum_ref[pl.ds(start, half), :] + weight_term(
        cols_ref[pl.ds(start, half), :], grad_ref
    )


def half_copy(ref, out_ref, of, sem):
    half = ref.shape[0]
    size = min(half, out_ref.shape[0] - of * half)
    return pltpu.make_async_copy(ref.at[pl.ds(0, size)], out_ref.at[pl.ds(of * half, size)], sem)


def on_core(act):
    for core in range(2):

        @pl.when(lax.rem(lax.axis_index("space"), 2) == core)
        def _():
            act(core)


def join_kernel(other_ref, _, out_ref, sem):
    def place(core):
        copy = half_copy(other_ref, out_ref, 1 - core, sem)
        copy.start()
        copy.wait()

    on_core(place)


def input_planes(todo, w_ref, wide_ref, done_ref):
    _, cb, hgt, wid = done_ref.shape
    half = wid // 2
    groups = hgt // 4
    lanes = groups * wid
    taps = 9 * cb
    spread = pair_matrix(True, wid, half)
    spread = jnp.concatenate([spread, spread], axis=0)
    keep = lax.broadcasted_iota(jnp.int32, (3 * cb, lanes), 1) < lanes - half
    w = [w_ref[a * taps : (a + 1) * taps, :] for a in range(3)]
    behind = jnp.concatenate([w[2], w[0]], axis=1)
    for slot, grads in enumerate(todo):
        if len(grads) == 1:
            e_all = jnp.dot(w[1], grads[0], preferred_element_type=jnp.float32)
        else:
            e_all = jnp.dot(
                behind, jnp.concatenate(grads, axis=0), preferred_element_type=jnp.float32
            )
        by_b = [e_all[b * 3 * cb : (b + 1) * 3 * cb] for b in range(3)]
        shifted = pltpu.roll(by_b[0], lanes - half, 1)
        rows = (by_b[1], by_b[2] + jnp.where(keep, shifted, 0.0))
        left = []
        for f in rows:
            for j in range(groups):
                t = f[:, j * wid : (j + 1) * wid]
                left.append(
                    jnp.concatenate([t[e * cb : (e + 1) * cb] for e in range(3)], axis=1)
                )
        left = jnp.concatenate(left, axis=0)
        high = left.astype(jnp.bfloat16)
        low = (left - high.astype(jnp.float32)).astype(jnp.bfloat16)
        full = jnp.dot(
            jnp.concatenate([high, low], axis=1), spread, preferred_element_type=jnp.float32
        )
        for par in range(2):
            for j in range(groups):
                for h in range(2):
                    y = 2 * (2 * j + h) + par
                    at = (par * groups + j) * cb
                    wide_ref[pl.ds(y, cb, stride=hgt), :] = full[
                        at : at + cb, h * wid : (h + 1) * wid
                    ]
        done_ref[slot] = wide_ref[...].reshape(cb, hgt, wid).astype(jnp.bfloat16)


def plane_copies(done_ref, out_ref, first, sems):
    return [
        pltpu.make_async_copy(done_ref.at[i], out_ref.at[:, first + i], sems.at[i])
        for i in range(done_ref.shape[0])
    ]


def input_kernel(w_ref, one_ref, two_ref, _, out_ref, wide_ref, done_ref, sems):
    one, two = one_ref[...], two_ref[...]
    input_planes([(one,), (one, two)], w_ref, wide_ref, done_ref)
    for copy in plane_copies(done_ref, out_ref, 0, sems):
        copy.start()
    for copy in plane_copies(done_ref, out_ref, 0, sems):
        copy.wait()


def edge_kernel(w_ref, one_ref, two_ref, own_ref, _, out_ref, wgrad_ref, wide_ref, done_ref, sems):
    on_core(lambda core: half_copy(own_ref, wgrad_ref, core, sems.at[1]).start())
    two = two_ref[...]
    inside = lax.axis_index("space") < lax.axis_size("space") - 1
    two = jnp.where(inside, two.astype(jnp.float32), 0.0).astype(jnp.bfloat16)
    input_planes([(one_ref[...], two)], w_ref, wide_ref, done_ref)
    copies = plane_copies(done_ref, out_ref, out_ref.shape[1] - 1, sems)
    for copy in copies:
        copy.start()
    on_core(lambda core: half_copy(own_ref, wgrad_ref, core, sems.at[1]).wait())
    for copy in copies:
        copy.wait()


def moved(block, axis, to):
    return lax.ppermute(block, axis, list(enumerate(to)))


def on_device(volume, kernel, upstream):
    cb, planes, hgt, wid = volume.shape
    ob = upstream.shape[0]
    out_ch = kernel.shape[4]
    n_chan, n_space = lax.axis_size("chan"), lax.axis_size("space")
    direct = n_chan == FEW
    n = n_chan if direct else 1
    taps = 27 * cb
    cells = hgt // 4 * wid
    f32, bf16 = jnp.float32, jnp.bfloat16
    shape = jax.ShapeDtypeStruct
    weights = kernel.transpose(1, 2, 3, 0, 4).reshape(taps, out_ch)
    up = upstream[:, 0].transpose(1, 0, 2)
    spread = pl.pallas_call(
        spread_kernel, out_shape=shape((ob, cells), f32), compiler_params=params()
    )(up)

    scratch = [pltpu.VMEM((3 * cb * hgt, wid), f32)]
    if n > 1:
        scratch.append(pltpu.VMEM((out_ch, cells), f32))
    part_shapes = [shape((ob if direct else out_ch, cells), f32)] * n
    out_planes = range(planes // 2)
    cols, grads, acts = {}, {}, {}
    vmem = pl.BlockSpec(memory_space=pltpu.VMEM)
    hbm = pl.BlockSpec(memory_space=pltpu.HBM)

    def from_hbm(x):
        return pltpu.with_memory_space_constraint(x, pltpu.HBM)

    half = -(-taps // 32) * 16
    cols_shape = shape((2 * half, cells), bf16)
    vol, edge = pl.pallas_call(
        load_kernel,
        in_specs=[hbm],
        out_shape=[shape(volume.shape, bf16), shape((cb, 1, hgt, wid), bf16)],
        scratch_shapes=[pltpu.SemaphoreType.DMA((1,))],
        compiler_params=params(),
    )(from_hbm(volume))
    rim = lax.ppermute(edge, "space", [(i, (i + 1) % n_space) for i in range(n_space)])
    for z in reversed(out_planes):
        cols[z], *parts = pl.pallas_call(
            functools.partial(fwd_kernel, n, ob, z),
            out_shape=[cols_shape] + part_shapes,
            scratch_shapes=scratch,
            compiler_params=params(),
        )(*(() if z else (rim,)), vol, weights)
        if direct:
            parts = parts[:1] + [moved(p, "chan", to) for to, p in zip(RS[z], parts[1:])]
        else:
            parts = [lax.psum_scatter(parts[0], "chan", scatter_dimension=0, tiled=True)]
        own, acts[z] = pl.pallas_call(
            act_kernel,
            out_shape=[shape((ob, cells), bf16), shape((ob, cells), f32)],
            compiler_params=params(),
        )(spread, *parts)
        if direct:
            grads[z] = [own] + [moved(own, "chan", to) for to in AG[z]]
        else:
            grads[z] = [lax.all_gather(own, "chan", axis=0, tiled=True)]

    wide, plane = pltpu.VMEM((cb * hgt, wid), f32), (cb, hgt, wid)
    grad_shape = shape((out_ch, cells), bf16)
    term, grads[1], pooled, input_grad = pl.pallas_call(
        functools.partial(middle_kernel, n),
        out_specs=[vmem, vmem, vmem, hbm],
        out_shape=[
            shape((2 * half, out_ch), f32),
            grad_shape,
            shape(upstream.shape, bf16),
            shape(volume.shape, bf16),
        ],
        scratch_shapes=[wide, pltpu.VMEM((1,) + plane, bf16), pltpu.SemaphoreType.DMA((1,))],
        compiler_params=params(),
    )(weights, acts[0], acts[1], cols[1], *grads[1])
    send, grads[0] = pl.pallas_call(
        functools.partial(send_kernel, n),
        out_shape=[shape((half, out_ch), bf16), grad_shape],
        compiler_params=params(),
    )(term, cols[0], *grads[0])
    keep = pl.pallas_call(
        keep_kernel,
        out_shape=shape((half, out_ch), f32),
        compiler_params=params(),
    )(term, cols[0], grads[0])

    rows = keep + lax.ppermute(send, "space", [(i, i ^ 1) for i in range(n_space)]).astype(f32)
    bits = [1 << b for b in range(1, n_space.bit_length() - 1)]
    groups = [bits[i : i + 2] for i in range(0, len(bits), 2)]
    after = None
    for r, group in enumerate(groups):
        sent = rows.astype(bf16)
        if r == len(groups) - 1:
            sent, grads, input_grad = lax.optimization_barrier((sent, grads, input_grad))
        partners = [sum(group[b] * (k >> b & 1) for b in range(len(group))) for k in range(1, 1 << len(group))]
        terms = [sent] + [None] * len(partners)
        for k in CHIPS:
            if k < len(partners):
                terms[k + 1] = lax.ppermute(
                    sent, "space", [(i, i ^ partners[k]) for i in range(n_space)]
                )
        if r == len(groups) - 1:
            after = lax.ppermute(grads[0], "space", [((i + 1) % n_space, i) for i in range(n_space)])
            input_grad = pl.pallas_call(
                input_kernel,
                in_specs=[vmem] * 3 + [hbm],
                out_specs=hbm,
                out_shape=shape(volume.shape, bf16),
                scratch_shapes=[wide, pltpu.VMEM((2,) + plane, bf16), pltpu.SemaphoreType.DMA((2,))],
                input_output_aliases={3: 0},
                compiler_params=params(),
            )(weights, grads[0], grads[1], input_grad)
        terms = [t.astype(f32) for t in terms]
        while len(terms) > 1:
            terms = [a + b for a, b in zip(terms[::2], terms[1::2])]
        rows = terms[0]
    rows, input_grad, after = lax.optimization_barrier((rows, input_grad, after))
    input_grad, weight_grad = pl.pallas_call(
        edge_kernel,
        in_specs=[vmem] * 4 + [hbm],
        out_specs=[hbm] * 2,
        out_shape=[shape(volume.shape, bf16), shape((taps, out_ch), f32)],
        scratch_shapes=[wide, pltpu.VMEM((1,) + plane, bf16), pltpu.SemaphoreType.DMA((2,))],
        input_output_aliases={4: 0},
        compiler_params=params(),
    )(weights, grads[1], after, rows, input_grad)
    other = lax.ppermute(rows, "space", [(i, i ^ 1) for i in range(n_space)])
    weight_grad = pl.pallas_call(
        join_kernel,
        in_specs=[vmem, hbm],
        out_specs=hbm,
        out_shape=shape((taps, out_ch), f32),
        scratch_shapes=[pltpu.SemaphoreType.DMA],
        input_output_aliases={1: 0},
        compiler_params=params(),
    )(other, weight_grad)
    weight_grad = weight_grad.reshape(3, 3, 3, cb, out_ch).transpose(3, 0, 1, 2, 4)
    return pooled, input_grad, weight_grad


def solution(mesh):
    return jax.shard_map(
        on_device,
        mesh=mesh,
        in_specs=(
            P("chan", "space", None, None),
            P("chan", None, None, None, None),
            P("chan", "space", None, None),
        ),
        out_specs=(
            P("chan", "space", None, None),
            P("chan", "space", None, None),
            P("chan", None, None, None, None),
        ),
        check_vma=False,
    )
```

```python
import functools

import jax
import jax.numpy as jnp
from jax import lax
from jax.experimental import pallas as pl
from jax.experimental.pallas import tpu as pltpu
from jax.sharding import PartitionSpec as P

SLOPE = 0.3
VMEM = 24 * 1024 * 1024
RS = {1: ((3, 2, 1, 0), (2, 3, 0, 1), (1, 0, 3, 2)), 0: ((3, 2, 1, 0), (2, 0, 3, 1), (1, 3, 0, 2))}
AG = {1: ((1, 0, 3, 2), (3, 2, 1, 0), (2, 3, 0, 1)), 0: ((1, 3, 0, 2), (3, 2, 1, 0), (2, 0, 3, 1))}
CHIPS = (0, 1, 2)
FEW = 4


def params():
    return pltpu.CompilerParams(vmem_limit_bytes=VMEM)


def pair_matrix(transposed, wid, half):
    shape = (3 * wid, 2 * wid) if transposed else (2 * wid, 3 * wid)
    long, short = (0, 1) if transposed else (1, 0)
    src = lax.broadcasted_iota(jnp.int32, shape, short)
    dst = lax.broadcasted_iota(jnp.int32, shape, long)
    e = (dst >= wid).astype(jnp.int32) + (dst >= 2 * wid).astype(jnp.int32)
    rest = dst - e * wid
    h = (rest >= half).astype(jnp.int32)
    x = 2 * (rest - h * half) + e - 1
    hit = (x >= 0) & (x < wid) & (src == h * wid + x)
    return jnp.where(hit, 1.0, 0.0).astype(jnp.bfloat16)


def load_kernel(vol_hbm, vol_ref, edge_ref, sems):
    cb, planes = vol_ref.shape[:2]
    pieces = sems.shape[0]
    size = cb // pieces
    copies = [
        pltpu.make_async_copy(
            vol_hbm.at[pl.ds(i * size, size)], vol_ref.at[pl.ds(i * size, size)], sems.at[i]
        )
        for i in range(pieces)
    ]
    for copy in copies:
        copy.start()
    for copy in copies:
        copy.wait()
    edge_ref[...] = vol_ref[:, planes - 1 :]


def pick(table, i):
    value = jnp.int32(table[0])
    for k, entry in enumerate(table[1:], 1):
        value = jnp.where(i == k, entry, value)
    return value


def fwd_kernel(n, ob, z, *refs):
    if z:
        vol_ref, w_ref, cols_ref, *rest = refs
    else:
        rim_ref, vol_ref, w_ref, cols_ref, *rest = refs
    part_refs = rest[:-2] if n > 1 else rest[:-1]
    wide_ref = rest[-2] if n > 1 else rest[-1]
    cb, _, hgt, wid = vol_ref.shape
    groups = hgt // 4
    sel = pair_matrix(False, wid, wid // 2)
    zero = jnp.zeros((cb, wid), jnp.float32)
    left, right = [], []
    for a in range(3):
        plane = vol_ref[:, 2 * z + a - 1] if z or a else rim_ref[:, 0]
        plane = plane.astype(jnp.float32).reshape(cb * hgt, wid)
        if not (z or a):
            plane = jnp.where(lax.axis_index("space") == 0, 0.0, plane)
        wide_ref[a * cb * hgt : (a + 1) * cb * hgt, :] = plane
        row = [wide_ref[pl.ds(a * cb * hgt + y, cb, stride=hgt), :] for y in range(hgt)]
        cls = [[row[4 * j + r] for j in range(groups)] for r in range(4)]

        def stack(blocks):
            return jnp.concatenate(blocks, axis=0).astype(jnp.bfloat16)

        back = stack([zero] + cls[3][:-1])
        cls = [stack(c) for c in cls]
        left += [back, cls[0], cls[1]]
        right += [cls[1], cls[2], cls[3]]
    taps = jnp.dot(
        jnp.concatenate([jnp.concatenate(left, axis=0), jnp.concatenate(right, axis=0)], axis=1),
        sel,
        preferred_element_type=jnp.float32,
    ).astype(jnp.bfloat16)
    for ab in range(9):
        for e in range(3):
            tap = ab * 3 + e
            cols_ref[tap * cb : (tap + 1) * cb, :] = jnp.concatenate(
                [
                    taps[(ab * groups + j) * cb : (ab * groups + j + 1) * cb, e * wid : (e + 1) * wid]
                    for j in range(groups)
                ],
                axis=1,
            )
    if cols_ref.shape[0] > 27 * cb:
        pad = (cols_ref.shape[0] - 27 * cb, cols_ref.shape[1])
        cols_ref[27 * cb :, :] = jnp.zeros(pad, jnp.bfloat16)
    part = lax.dot_general(
        w_ref[...],
        cols_ref[0 : 27 * cb, :],
        (((0,), (0,)), ((), ())),
        preferred_element_type=jnp.float32,
    )
    if n == 1:
        part_refs[0][...] = part
        return
    all_ref = rest[-1]
    all_ref[...] = part
    me = lax.axis_index("chan")
    for to, ref in zip((tuple(range(n)),) + RS[z], part_refs):
        start = pl.multiple_of(pick(to, me) * ob, ob)
        ref[...] = all_ref[pl.ds(start, ob), :]


def spread_kernel(up_ref, out_ref):
    groups, ob, small = up_ref.shape
    wid = 4 * small
    r = lax.broadcasted_iota(jnp.int32, (small, wid), 0)
    c = lax.broadcasted_iota(jnp.int32, (small, wid), 1)
    c = c - jnp.where(c >= 2 * small, 2 * small, 0)
    grow = jnp.where((c >= 2 * r) & (c <= 2 * r + 1), 1.0, 0.0).astype(jnp.bfloat16)
    for j in range(groups):
        spread = jnp.dot(up_ref[j], grow, preferred_element_type=jnp.float32)
        out_ref[:, j * wid : (j + 1) * wid] = spread * 0.125


def act_kernel(spread_ref, *rest):
    *part_refs, grad_ref, act_ref = rest
    pre = part_refs[0][...]
    for ref in part_refs[1:]:
        pre = pre + ref[...]
    grad = spread_ref[...] * jnp.where(pre > 0, 1.0, SLOPE)
    grad_ref[...] = grad.astype(jnp.bfloat16)
    act_ref[...] = jnp.where(pre > 0, pre, SLOPE * pre)


def pool_planes(one_ref, two_ref, out_ref):
    ob, _, groups, small = out_ref.shape
    wid = 4 * small
    r = lax.broadcasted_iota(jnp.int32, (wid, small), 0)
    c = lax.broadcasted_iota(jnp.int32, (wid, small), 1)
    r = r - jnp.where(r >= 2 * small, 2 * small, 0)
    pool = jnp.where((r >= 2 * c) & (r <= 2 * c + 1), 0.125, 0.0)
    act = one_ref[...] + two_ref[...]
    means = [
        jnp.dot(
            act[:, j * wid : (j + 1) * wid],
            pool,
            precision=lax.Precision.HIGHEST,
            preferred_element_type=jnp.float32,
        )
        for j in range(groups)
    ]
    out_ref[:, 0] = jnp.stack(means, axis=1).astype(jnp.bfloat16)


def in_order(n, z, block_refs, grad_ref):
    if n == 1:
        grad_ref[...] = block_refs[0][...]
        return
    me = lax.axis_index("chan")
    ob = block_refs[0].shape[0]
    for to, ref in zip((tuple(range(n)),) + AG[z], block_refs):
        start = pl.multiple_of(pick([to.index(i) for i in range(n)], me) * ob, ob)
        grad_ref[pl.ds(start, ob), :] = ref[...]


def weight_term(cols, grad_ref):
    return lax.dot_general(
        cols,
        grad_ref[...],
        (((1,), (1,)), ((), ())),
        preferred_element_type=jnp.float32,
    )


def middle_kernel(n, w_ref, act_one_ref, act_two_ref, cols_ref, *refs):
    *block_refs, wgrad_ref, grad_ref, pooled_ref, out_ref, wide_ref, done_ref, sems = refs
    in_order(n, 1, block_refs, grad_ref)
    input_planes([(grad_ref[...],)], w_ref, wide_ref, done_ref)
    for copy in plane_copies(done_ref, out_ref, 2, sems):
        copy.start()
    wgrad_ref[...] = weight_term(cols_ref[...], grad_ref)
    pool_planes(act_one_ref, act_two_ref, pooled_ref)
    for copy in plane_copies(done_ref, out_ref, 2, sems):
        copy.wait()


def send_kernel(n, sum_ref, cols_ref, *refs):
    *block_refs, send_ref, grad_ref = refs
    in_order(n, 0, block_refs, grad_ref)
    half = send_ref.shape[0]
    start = pl.multiple_of((1 - lax.rem(lax.axis_index("space"), 2)) * half, 16)
    send = sum_ref[pl.ds(start, half), :] + weight_term(cols_ref[pl.ds(start, half), :], grad_ref)
    send_ref[...] = send.astype(send_ref.dtype)


def keep_kernel(sum_ref, cols_ref, grad_ref, keep_ref):
    half = keep_ref.shape[0]
    start = pl.multiple_of(lax.rem(lax.axis_index("space"), 2) * half, 16)
    keep_ref[...] = sum_ref[pl.ds(start, half), :] + weight_term(
        cols_ref[pl.ds(start, half), :], grad_ref
    )


def half_copy(ref, out_ref, of, sem):
    half = ref.shape[0]
    size = min(half, out_ref.shape[0] - of * half)
    return pltpu.make_async_copy(ref.at[pl.ds(0, size)], out_ref.at[pl.ds(of * half, size)], sem)


def on_core(act):
    for core in range(2):

        @pl.when(lax.rem(lax.axis_index("space"), 2) == core)
        def _():
            act(core)


def join_kernel(other_ref, _, out_ref, sem):
    def place(core):
        copy = half_copy(other_ref, out_ref, 1 - core, sem)
        copy.start()
        copy.wait()

    on_core(place)


def input_planes(todo, w_ref, wide_ref, done_ref):
    _, cb, hgt, wid = done_ref.shape
    half = wid // 2
    groups = hgt // 4
    lanes = groups * wid
    taps = 9 * cb
    spread = pair_matrix(True, wid, half)
    spread = jnp.concatenate([spread, spread], axis=0)
    keep = lax.broadcasted_iota(jnp.int32, (3 * cb, lanes), 1) < lanes - half
    w = [w_ref[a * taps : (a + 1) * taps, :] for a in range(3)]
    behind = jnp.concatenate([w[2], w[0]], axis=1)
    for slot, grads in enumerate(todo):
        if len(grads) == 1:
            e_all = jnp.dot(w[1], grads[0], preferred_element_type=jnp.float32)
        else:
            e_all = jnp.dot(
                behind, jnp.concatenate(grads, axis=0), preferred_element_type=jnp.float32
            )
        by_b = [e_all[b * 3 * cb : (b + 1) * 3 * cb] for b in range(3)]
        shifted = pltpu.roll(by_b[0], lanes - half, 1)
        rows = (by_b[1], by_b[2] + jnp.where(keep, shifted, 0.0))
        left = []
        for f in rows:
            for j in range(groups):
                t = f[:, j * wid : (j + 1) * wid]
                left.append(
                    jnp.concatenate([t[e * cb : (e + 1) * cb] for e in range(3)], axis=1)
                )
        left = jnp.concatenate(left, axis=0)
        high = left.astype(jnp.bfloat16)
        low = (left - high.astype(jnp.float32)).astype(jnp.bfloat16)
        full = jnp.dot(
            jnp.concatenate([high, low], axis=1), spread, preferred_element_type=jnp.float32
        )
        for par in range(2):
            for j in range(groups):
                for h in range(2):
                    y = 2 * (2 * j + h) + par
                    at = (par * groups + j) * cb
                    wide_ref[pl.ds(y, cb, stride=hgt), :] = full[
                        at : at + cb, h * wid : (h + 1) * wid
                    ]
        done_ref[slot] = wide_ref[...].reshape(cb, hgt, wid).astype(jnp.bfloat16)


def plane_copies(done_ref, out_ref, first, sems):
    return [
        pltpu.make_async_copy(done_ref.at[i], out_ref.at[:, first + i], sems.at[i])
        for i in range(done_ref.shape[0])
    ]


def input_kernel(w_ref, one_ref, two_ref, _, out_ref, wide_ref, done_ref, sems):
    one, two = one_ref[...], two_ref[...]
    input_planes([(one,), (one, two)], w_ref, wide_ref, done_ref)
    for copy in plane_copies(done_ref, out_ref, 0, sems):
        copy.start()
    for copy in plane_copies(done_ref, out_ref, 0, sems):
        copy.wait()


def edge_kernel(w_ref, one_ref, two_ref, own_ref, _, out_ref, wgrad_ref, wide_ref, done_ref, sems):
    on_core(lambda core: half_copy(own_ref, wgrad_ref, core, sems.at[1]).start())
    two = two_ref[...]
    inside = lax.axis_index("space") < lax.axis_size("space") - 1
    two = jnp.where(inside, two.astype(jnp.float32), 0.0).astype(jnp.bfloat16)
    input_planes([(one_ref[...], two)], w_ref, wide_ref, done_ref)
    copies = plane_copies(done_ref, out_ref, out_ref.shape[1] - 1, sems)
    for copy in copies:
        copy.start()
    on_core(lambda core: half_copy(own_ref, wgrad_ref, core, sems.at[1]).wait())
    for copy in copies:
        copy.wait()


def moved(block, axis, to):
    return lax.ppermute(block, axis, list(enumerate(to)))


def on_device(volume, kernel, upstream):
    cb, planes, hgt, wid = volume.shape
    ob = upstream.shape[0]
    out_ch = kernel.shape[4]
    n_chan, n_space = lax.axis_size("chan"), lax.axis_size("space")
    direct = n_chan == FEW
    n = n_chan if direct else 1
    taps = 27 * cb
    cells = hgt // 4 * wid
    f32, bf16 = jnp.float32, jnp.bfloat16
    shape = jax.ShapeDtypeStruct
    weights = kernel.transpose(1, 2, 3, 0, 4).reshape(taps, out_ch)
    up = upstream[:, 0].transpose(1, 0, 2)
    spread = pl.pallas_call(
        spread_kernel, out_shape=shape((ob, cells), f32), compiler_params=params()
    )(up)

    scratch = [pltpu.VMEM((3 * cb * hgt, wid), f32)]
    if n > 1:
        scratch.append(pltpu.VMEM((out_ch, cells), f32))
    part_shapes = [shape((ob if direct else out_ch, cells), f32)] * n
    out_planes = range(planes // 2)
    cols, grads, acts = {}, {}, {}
    vmem = pl.BlockSpec(memory_space=pltpu.VMEM)
    hbm = pl.BlockSpec(memory_space=pltpu.HBM)

    def from_hbm(x):
        return pltpu.with_memory_space_constraint(x, pltpu.HBM)

    half = -(-taps // 32) * 16
    cols_shape = shape((2 * half, cells), bf16)
    vol, edge = pl.pallas_call(
        load_kernel,
        in_specs=[hbm],
        out_shape=[shape(volume.shape, bf16), shape((cb, 1, hgt, wid), bf16)],
        scratch_shapes=[pltpu.SemaphoreType.DMA((1,))],
        compiler_params=params(),
    )(from_hbm(volume))
    rim = lax.ppermute(edge, "space", [(i, (i + 1) % n_space) for i in range(n_space)])
    for z in reversed(out_planes):
        cols[z], *parts = pl.pallas_call(
            functools.partial(fwd_kernel, n, ob, z),
            out_shape=[cols_shape] + part_shapes,
            scratch_shapes=scratch,
            compiler_params=params(),
        )(*(() if z else (rim,)), vol, weights)
        if direct:
            parts = parts[:1] + [moved(p, "chan", to) for to, p in zip(RS[z], parts[1:])]
        else:
            parts = [lax.psum_scatter(parts[0], "chan", scatter_dimension=0, tiled=True)]
        own, acts[z] = pl.pallas_call(
            act_kernel,
            out_shape=[shape((ob, cells), bf16), shape((ob, cells), f32)],
            compiler_params=params(),
        )(spread, *parts)
        if direct:
            grads[z] = [own] + [moved(own, "chan", to) for to in AG[z]]
        else:
            grads[z] = [lax.all_gather(own, "chan", axis=0, tiled=True)]

    wide, plane = pltpu.VMEM((cb * hgt, wid), f32), (cb, hgt, wid)
    grad_shape = shape((out_ch, cells), bf16)
    term, grads[1], pooled, input_grad = pl.pallas_call(
        functools.partial(middle_kernel, n),
        out_specs=[vmem, vmem, vmem, hbm],
        out_shape=[
            shape((2 * half, out_ch), f32),
            grad_shape,
            shape(upstream.shape, bf16),
            shape(volume.shape, bf16),
        ],
        scratch_shapes=[wide, pltpu.VMEM((1,) + plane, bf16), pltpu.SemaphoreType.DMA((1,))],
        compiler_params=params(),
    )(weights, acts[0], acts[1], cols[1], *grads[1])
    send, grads[0] = pl.pallas_call(
        functools.partial(send_kernel, n),
        out_shape=[shape((half, out_ch), bf16), grad_shape],
        compiler_params=params(),
    )(term, cols[0], *grads[0])
    keep = pl.pallas_call(
        keep_kernel,
        out_shape=shape((half, out_ch), f32),
        compiler_params=params(),
    )(term, cols[0], grads[0])

    rows = keep + lax.ppermute(send, "space", [(i, i ^ 1) for i in range(n_space)]).astype(f32)
    bits = [1 << b for b in range(1, n_space.bit_length() - 1)]
    groups = [bits[i : i + 2] for i in range(0, len(bits), 2)]
    after = None
    for r, group in enumerate(groups):
        sent = rows.astype(bf16)
        if r == len(groups) - 1:
            sent, grads, input_grad = lax.optimization_barrier((sent, grads, input_grad))
        partners = [sum(group[b] * (k >> b & 1) for b in range(len(group))) for k in range(1, 1 << len(group))]
        terms = [sent] + [None] * len(partners)
        for k in CHIPS:
            if k < len(partners):
                terms[k + 1] = lax.ppermute(
                    sent, "space", [(i, i ^ partners[k]) for i in range(n_space)]
                )
        if r == len(groups) - 1:
            after = lax.ppermute(grads[0], "space", [((i + 1) % n_space, i) for i in range(n_space)])
            input_grad = pl.pallas_call(
                input_kernel,
                in_specs=[vmem] * 3 + [hbm],
                out_specs=hbm,
                out_shape=shape(volume.shape, bf16),
                scratch_shapes=[wide, pltpu.VMEM((2,) + plane, bf16), pltpu.SemaphoreType.DMA((2,))],
                input_output_aliases={3: 0},
                compiler_params=params(),
            )(weights, grads[0], grads[1], input_grad)
        terms = [t.astype(f32) for t in terms]
        while len(terms) > 1:
            terms = [a + b for a, b in zip(terms[::2], terms[1::2])]
        rows = terms[0]
    rows = rows.astype(bf16)
    rows, input_grad, after = lax.optimization_barrier((rows, input_grad, after))
    input_grad, weight_grad = pl.pallas_call(
        edge_kernel,
        in_specs=[vmem] * 4 + [hbm],
        out_specs=[hbm] * 2,
        out_shape=[shape(volume.shape, bf16), shape((taps, out_ch), f32)],
        scratch_shapes=[wide, pltpu.VMEM((1,) + plane, bf16), pltpu.SemaphoreType.DMA((2,))],
        input_output_aliases={4: 0},
        compiler_params=params(),
    )(weights, grads[1], after, rows.astype(f32), input_grad)
    other = lax.ppermute(rows, "space", [(i, i ^ 1) for i in range(n_space)])
    weight_grad = pl.pallas_call(
        join_kernel,
        in_specs=[vmem, hbm],
        out_specs=hbm,
        out_shape=shape((taps, out_ch), f32),
        scratch_shapes=[pltpu.SemaphoreType.DMA],
        input_output_aliases={1: 0},
        compiler_params=params(),
    )(other.astype(f32), weight_grad)
    weight_grad = weight_grad.reshape(3, 3, 3, cb, out_ch).transpose(3, 0, 1, 2, 4)
    return pooled, input_grad, weight_grad


def solution(mesh):
    return jax.shard_map(
        on_device,
        mesh=mesh,
        in_specs=(
            P("chan", "space", None, None),
            P("chan", None, None, None, None),
            P("chan", "space", None, None),
        ),
        out_specs=(
            P("chan", "space", None, None),
            P("chan", "space", None, None),
            P("chan", None, None, None, None),
        ),
        check_vma=False,
    )
```
